32 devices in a mesh: dp: 8 (over z, y), seq: 4 (over x, core).
Axes of the slice: x: 2, y: 2, z: 4, core: 2. Of those that a mesh axis runs over, the one named last changes fastest.
Arguments:
- tokens: bfloat16 [32, 512, 768], P('dp', 'seq'), may hold values from -6 to 6
- seg_ids: int32 [32, 512], P('dp'), may hold values from 0 to 4, as said below
- text_len: int32 [32, 4], P('dp'), may hold values from 16 to 288, as said below
- out_grad: bfloat16 [32, 512, 768], P('dp', 'seq'), may hold values from -6 to 6
- pooled_grad: bfloat16 [32, 4, 768], P('dp'), may hold values from -48 to 48
- w_query: bfloat16 [768, 768], replicated, may hold values from -0.4375 to 0.4375
- b_query: bfloat16 [768], replicated, may hold values from -1.5 to 1.5
- w_key: bfloat16 [768, 768], replicated, may hold values from -0.21875 to 0.21875
- w_value: bfloat16 [768, 768], replicated, may hold values from -0.21875 to 0.21875
- b_value: bfloat16 [768], replicated, may hold values from -1.5 to 1.5
- w_out: bfloat16 [768, 768], replicated, may hold values from -1 to 1
- b_out: bfloat16 [768], replicated, may hold values from -1.5 to 1.5
- attn_gain: bfloat16 [768], replicated, may hold values from 0.5 to 1.5
- attn_shift: bfloat16 [768], replicated, may hold values from -1.5 to 1.5
- w_up: bfloat16 [768, 3072], replicated, may hold values from -0.21875 to 0.21875
- b_up: bfloat16 [3072], replicated, may hold values from -1.5 to 1.5
- w_down: bfloat16 [3072, 768], replicated, may hold values from -0.109375 to 0.109375
- b_down: bfloat16 [768], replicated, may hold values from -1.5 to 1.5
- ffn_gain: bfloat16 [768], replicated, may hold values from 0.5 to 1.5
- ffn_shift: bfloat16 [768], replicated, may hold values from -1.5 to 1.5
Outputs:
- layer_out: float32 [32, 512, 768], P('dp', 'seq')
- pooled: float32 [32, 4, 768], P('dp')
- grad_tokens: float32 [32, 512, 768], P('dp', 'seq')
- grad_w_query: float32 [768, 768], P('dp')
- grad_b_query: float32 [768], P('dp')
- grad_w_key: float32 [768, 768], P('dp')
- grad_w_value: float32 [768, 768], P('dp')
- grad_b_value: float32 [768], P('dp')
- grad_w_out: float32 [768, 768], P('dp')
- grad_b_out: float32 [768], P('dp')
- grad_attn_gain: float32 [768], P('dp')
- grad_attn_shift: float32 [768], P('dp')
- grad_w_up: float32 [768, 3072], P('dp')
- grad_b_up: float32 [3072], P('dp')
- grad_w_down: float32 [3072, 768], P('dp')
- grad_b_down: float32 [768], P('dp')
- grad_ffn_gain: float32 [768], P('dp')
- grad_ffn_shift: float32 [768], P('dp')
The draws below stay inside these ranges and needn't reach their ends.
Inputs may be any that keep to these rules, and one draw needn't show every extreme that they name: `seg_ids`: in every row the ids are 1, 2, ..., 4 on consecutive tokens, text i taking text_len[row, i - 1] tokens from the row's start, then 0 on the remaining pad slots; every row holds exactly 4 texts. `text_len`: in every row exactly one text has 288 tokens; the others have 16 to 64.
All inputs are finite; a program needn't handle non-finite values.
Results may differ from the reference program's by a relative error of at most 0.018.
Values may be sent and summed in bfloat16 or wider, within the bound.
No kernel may reach another device: no remote copies, remote signals or barrier semaphores. Data moves between devices by JAX's collectives and lax.ppermute only.
A program may use at most 192 MiB of HBM per device.

```python
import math
import jax
import jax.numpy as jnp
from jax import lax

D = 768
HEADS = 12
HEAD = 64
FF = 3072
L = 512
SEGS = 4
TEXT_MAX = 288
SHORT_MIN = 16
SHORT_MAX = 64
ROWS = 32


def text_sizes(key):
    first, second = jax.random.split(jax.random.fold_in(key, 17))
    short_sizes = jax.random.randint(first, (ROWS, SEGS), SHORT_MIN, SHORT_MAX + 1, dtype=jnp.int32)
    long_slot = jax.random.randint(second, (ROWS, 1), 0, SEGS, dtype=jnp.int32)
    columns = jnp.arange(SEGS, dtype=jnp.int32)[None, :]
    return jnp.where(columns == long_slot, TEXT_MAX, short_sizes).astype(jnp.int32)


def draw_text_len(key, part):
    return text_sizes(key)


def draw_seg_ids(key, part):
    sizes = text_sizes(key)
    ends = jnp.cumsum(sizes, axis=1)
    places = jnp.arange(L, dtype=jnp.int32)[None, :, None]
    before = jnp.sum((places >= ends[:, None, :]).astype(jnp.int32), axis=2)
    return jnp.where(before < SEGS, before + 1, 0).astype(jnp.int32)


def steps_of(stream_key, dims, cuts, low, top_value):
    def one(axis_at, blocks):
        heights = jax.random.uniform(jax.random.fold_in(jax.random.fold_in(stream_key, 6), axis_at), (blocks,), jnp.float32, low / len(cuts), top_value / len(cuts))
        return jnp.repeat(jnp.exp(heights), dims[axis_at] // blocks).reshape((-1,) + (1,) * (len(dims) - axis_at - 1))

    factor_of = one(*cuts[0])
    for cut in cuts[1:]:
        factor_of = factor_of * one(*cut)
    return factor_of


def centred(own_key, shape, spread, limit, shards=(), kind=jnp.bfloat16):
    result = spread * jax.random.normal(own_key, shape, jnp.float32)
    if shards:
        result = result * steps_of(own_key, shape, shards, -0.22, 0.18)
    return jnp.clip(result, -limit, limit).astype(kind)


def setup_inputs(seed: int = 0) -> dict:
    streams_of = jax.random.split(jax.random.key(seed), 21)
    return {
        "tokens": centred(streams_of[0], (ROWS, L, D), 1.0, 6.0, ((0, 8), (1, 4))),
        "seg_ids": draw_seg_ids(jax.random.fold_in(streams_of[20], 71), 0),
        "text_len": draw_text_len(jax.random.fold_in(streams_of[20], 71), 0),
        "out_grad": centred(streams_of[3], (ROWS, L, D), 1.0, 6.0, ((0, 8), (1, 4))),
        "pooled_grad": centred(streams_of[4], (ROWS, SEGS, D), 8.0, 48.0, ((0, 8),)),
        "w_query": centred(streams_of[5], (D, D), (D // 4) ** -0.5, 0.4375),
        "b_query": centred(streams_of[6], (D,), 0.3, 1.5),
        "w_key": centred(streams_of[7], (D, D), D ** -0.5, 0.21875),
        "w_value": centred(streams_of[8], (D, D), D ** -0.5, 0.21875),
        "b_value": centred(streams_of[9], (D,), 0.3, 1.5),
        "w_out": centred(streams_of[10], (D, D), (D // 24) ** -0.5, 1.0),
        "b_out": centred(streams_of[11], (D,), 0.3, 1.5),
        "attn_gain": jnp.clip(1.0 + 0.1 * jax.random.normal(streams_of[12], (D,), jnp.float32), 0.5, 1.5).astype(jnp.bfloat16),
        "attn_shift": centred(streams_of[13], (D,), 0.3, 1.5),
        "w_up": centred(streams_of[14], (D, FF), D ** -0.5, 0.21875),
        "b_up": centred(streams_of[15], (FF,), 0.3, 1.5),
        "w_down": centred(streams_of[16], (FF, D), FF ** -0.5, 0.109375),
        "b_down": centred(streams_of[17], (D,), 0.3, 1.5),
        "ffn_gain": jnp.clip(1.0 + 0.1 * jax.random.normal(streams_of[18], (D,), jnp.float32), 0.5, 1.5).astype(jnp.bfloat16),
        "ffn_shift": centred(streams_of[19], (D,), 0.3, 1.5),
    }


EPS = 1e-12

@jax.custom_vjp
def low(v):
    return lax.optimization_barrier(v.astype(jnp.bfloat16)).astype(jnp.float32)

@jax.custom_vjp
def low_back(v):
    return v

def low_keep(v):
    return (low(v), None)

def low_pass(kept, grad):
    return (grad,)

def back_keep(v):
    return (v, None)

def back_low(kept, grad):
    return (low(grad),)
low.defvjp(low_keep, low_pass)
low_back.defvjp(back_keep, back_low)

def mult(left, right, form):
    return jnp.einsum(form, left, right, precision=lax.Precision.HIGHEST)

def layer_norm(hidden, gain, shift):
    centre = hidden - lax.optimization_barrier(jnp.mean(hidden, axis=-1, keepdims=True))
    scale = lax.rsqrt(lax.optimization_barrier(jnp.mean(centre * centre, axis=-1, keepdims=True)) + EPS)
    return centre * scale * gain + shift

def attend_rows(block):
    queries, keys, values, row_ids = block
    raw_scores = mult(queries, keys, 'rqhd,rkhd->rhqk')
    allowed = row_ids[:, None, :, None] == row_ids[:, None, None, :]
    scores = jnp.where(allowed, low_back(raw_scores) * 0.125, -1e+30)
    row_max = lax.optimization_barrier(jnp.max(scores, axis=-1, keepdims=True))
    expo = jnp.exp(scores - row_max)
    probs = expo / lax.optimization_barrier(jnp.sum(expo, axis=-1, keepdims=True))
    return mult(low(probs), values, 'rhqk,rkhd->rqhd')

def reference(tokens, seg_ids, text_len, out_grad, pooled_grad, w_query, b_query, w_key, w_value, b_value, w_out, b_out, attn_gain, attn_shift, w_up, b_up, w_down, b_down, ffn_gain, ffn_shift):
    rows = tokens.shape[0]
    group = math.gcd(rows, 8)
    count = rows // group
    select = (seg_ids[:, :, None] == jnp.arange(1, SEGS + 1, dtype=jnp.int32)[None, None, :]).astype(jnp.float32)
    lengths = text_len.astype(jnp.float32)[:, :, None]
    ids_grouped = seg_ids.reshape(count, group, L)

    def split_heads(array):
        return array.reshape(count, group, L, HEADS, HEAD)

    def forward(inputs, wq, bq, wk, wv, bv, wo, bo, gain_a, shift_a, wu, bu, wd, bd, gain_f, shift_f):
        queries = low(low_back(mult(inputs, wq, 'rtd,de->rte') + bq))
        keys = low(low_back(mult(inputs, wk, 'rtd,de->rte')))
        values = low(low_back(mult(inputs, wv, 'rtd,de->rte') + bv))
        mixed = lax.map(jax.checkpoint(attend_rows), (split_heads(queries), split_heads(keys), split_heads(values), ids_grouped))
        mixed = low(low_back(mixed.reshape(rows, L, D)))
        branch = low_back(mult(mixed, wo, 'rte,ed->rtd') + bo)
        after_attn = layer_norm(inputs + branch, gain_a, shift_a)
        upper = low_back(mult(low(after_attn), wu, 'rtd,df->rtf') + bu)
        hidden = low(jax.nn.gelu(upper, approximate=False))
        ffn = low_back(mult(hidden, wd, 'rtf,fd->rtd') + bd)
        layer_out = layer_norm(after_attn + ffn, gain_f, shift_f)
        pooled = mult(select, layer_out, 'rts,rtd->rsd') / lengths
        return (layer_out, pooled)
    weights = (w_query, b_query, w_key, w_value, b_value, w_out, b_out, attn_gain, attn_shift, w_up, b_up, w_down, b_down, ffn_gain, ffn_shift)
    weights = tuple((item.astype(jnp.float32) for item in weights))
    (layer_out, pooled), pull = jax.vjp(forward, tokens.astype(jnp.float32), *weights)
    grads = pull((out_grad.astype(jnp.float32), pooled_grad.astype(jnp.float32)))
    return (layer_out, pooled, grads[0], grads[1], grads[2], grads[3], grads[4], grads[5], grads[6], grads[7], grads[8], grads[9], grads[10], grads[11], grads[12], grads[13], grads[14], grads[15])
```

```python
from functools import partial
import math

import jax
import jax.numpy as jnp
from jax import lax
from jax.sharding import PartitionSpec as P

HEADS = 12
HEAD = 64
SEGS = 4

EPS = 1e-12
BF = jnp.bfloat16
F32 = jnp.float32
AXES = ("dp", "seq")


def product(left, right, form):
    return jnp.einsum(form, left, right, preferred_element_type=F32)


def layer_norm(hidden):
    centre = hidden - jnp.mean(hidden, axis=-1, keepdims=True)
    scale = lax.rsqrt(jnp.mean(centre * centre, axis=-1, keepdims=True) + EPS)
    return (centre * scale, scale)


def norm_back(grad, normed, scale):
    return scale * (
        grad
        - jnp.mean(grad, axis=-1, keepdims=True)
        - normed * jnp.mean(grad * normed, axis=-1, keepdims=True)
    )


def masked_scores(queries, keys, ids):
    raw_scores = product(queries, keys, "rqhd,rkhd->rhqk")
    allowed = ids[:, None, :, None] == ids[:, None, None, :]
    return jnp.where(allowed, raw_scores * 0.125, -1e30)


def pick(array, index):
    return lax.dynamic_index_in_dim(array, index, 0, keepdims=False)


class Links:
    def __init__(self, dp):
        self.dp = dp
        self.bits = dp.bit_length() - 1
        seq = lax.axis_index("seq")
        self.core = lax.rem(seq, 2)
        self.x = lax.div(seq, 2)
        self.place = lax.axis_index("dp")

    def swap(self, array, first, second):
        perm = []
        for d in range(self.dp):
            for s in range(4):
                ds, dd = second if s % 2 else first
                perm.append((d * 4 + s, (d ^ dd) * 4 + (s ^ ds)))
        return lax.ppermute(array, AXES, perm)

    def flip_core(self, array):
        return self.swap(array, (1, 0), (1, 0))

    def flip_x(self, array):
        return self.swap(array, (2, 0), (2, 0))

    def to_rows(self, array):
        a = array.reshape((2, 2) + array.shape[1:])
        a = jnp.swapaxes(a, 0, 1)
        keep, send = pick(a, self.core), pick(a, 1 - self.core)
        both = jnp.stack([keep, self.flip_core(send)], 1)
        keep, send = pick(both, self.x), pick(both, 1 - self.x)
        return jnp.concatenate([keep, self.flip_x(send)], 0)

    def to_blocks(self, array):
        other = self.flip_x(array[2:])
        mine = array[:2]
        pair = jnp.stack([mine, other])
        pair = jnp.where(self.x == 0, pair, pair[::-1])
        back = self.flip_core(pair[:, 1])
        own = pair[:, 0]
        rows = jnp.stack([own, back])
        rows = jnp.where(self.core == 0, rows, rows[::-1])
        return jnp.swapaxes(rows, 0, 1).reshape((4,) + array.shape[1:])

    def scatter(self, payload):
        core, x = self.core, self.x
        got = self.flip_core(pick(payload, 1 - core))
        total = (pick(payload, core).astype(F32) + got.astype(F32)).astype(BF)
        tail = total.shape[2:]
        nb = self.bits
        total = total.reshape((2,) * (nb + 1) + tail)
        low_first = tuple(range(nb, 0, -1))
        rest = (nb + 1, nb + 2)
        one = total.transpose((0,) + low_first + rest)
        two = total.transpose(low_first + (0,) + rest)
        total = jnp.where(core == 0, one, two)
        dp_steps = [(0, 1 << i) for i in range(nb)]
        steps_a = [(2, 0)] + dp_steps
        steps_b = dp_steps + [(2, 0)]
        dp_bits = [lax.rem(lax.div(self.place, 1 << i), 2) for i in range(nb)]
        bits_a = [x] + dp_bits
        bits_b = dp_bits + [x]
        for sa, sb, ba, bb in zip(steps_a, steps_b, bits_a, bits_b):
            bit = jnp.where(core == 0, ba, bb)
            got = self.swap(pick(total, 1 - bit), sa, sb)
            total = (pick(total, bit).astype(F32) + got.astype(F32)).astype(BF)
        return total

    def gather(self, chunk):
        got = self.flip_x(chunk)
        pair = jnp.where(self.x == 0, jnp.stack([chunk, got]), jnp.stack([got, chunk]))
        got = self.flip_core(pair)
        four = jnp.where(self.core == 0, jnp.stack([pair, got]), jnp.stack([got, pair]))
        return four.reshape((4,) + chunk.shape)


def local(
    dp,
    tokens,
    seg_ids,
    text_len,
    out_grad,
    pooled_grad,
    w_query,
    b_query,
    w_key,
    w_value,
    b_value,
    w_out,
    b_out,
    attn_gain,
    attn_shift,
    w_up,
    b_up,
    w_down,
    b_down,
    ffn_gain,
    ffn_shift,
):
    rows_dev, local_len, width = tokens.shape
    row_len = seg_ids.shape[1]
    links = Links(dp)
    seq = lax.axis_index("seq")
    wide = w_up.shape[1]
    part = width // dp

    blocks = pick(seg_ids, seq).reshape(4, local_len)
    ids = jnp.stack([pick(blocks, seq ^ k) for k in range(4)]).reshape(1, row_len)
    lengths = pick(text_len, seq).astype(F32)[None, :, None]
    pool_grad = pick(pooled_grad, seq).astype(F32)[None]

    x = links.to_rows(tokens).reshape(1, row_len, width)
    og = links.to_rows(out_grad).reshape(1, row_len, width)

    def heads(array):
        return array.reshape(array.shape[0], array.shape[1], HEADS, HEAD)

    query_b = (product(x, w_query, "rtd,de->rte") + b_query.astype(F32)).astype(BF)
    key_b = product(x, w_key, "rtd,de->rte").astype(BF)
    value_b = (product(x, w_value, "rtd,de->rte") + b_value.astype(F32)).astype(BF)
    qh, kh, vh = heads(query_b), heads(key_b), heads(value_b)
    scores = masked_scores(qh, kh, ids)
    row_max = jnp.max(scores, axis=-1, keepdims=True)
    expo = jnp.exp(scores - row_max)
    total = jnp.sum(expo, axis=-1, keepdims=True)
    probs_b = (expo / total).astype(BF)
    mixed_b = product(probs_b, vh, "rhqk,rkhd->rqhd").astype(BF).reshape(1, row_len, width)

    branch = product(mixed_b, w_out, "rte,ed->rtd") + b_out.astype(F32)
    normed_a, scale_a = layer_norm(x.astype(F32) + branch)
    after_attn = normed_a * attn_gain.astype(F32) + attn_shift.astype(F32)
    after_b = after_attn.astype(BF)
    upper = product(after_b, w_up, "rtd,df->rtf") + b_up.astype(F32)
    hidden_b = jax.nn.gelu(upper, approximate=False).astype(BF)
    ffn = product(hidden_b, w_down, "rtf,fd->rtd") + b_down.astype(F32)
    normed_f, scale_f = layer_norm(after_attn + ffn)
    layer_out = normed_f * ffn_gain.astype(F32) + ffn_shift.astype(F32)
    select = (ids[:, :, None] == jnp.arange(1, SEGS + 1, dtype=jnp.int32)[None, None, :]).astype(F32)
    pooled = jnp.einsum("rts,rtd->rsd", select, layer_out, precision=lax.Precision.HIGHEST) / lengths
    grad_out = og.astype(F32) + jnp.einsum(
        "rts,rsd->rtd", select, pool_grad / lengths, precision=lax.Precision.HIGHEST
    )

    def token_sum(array):
        return jnp.sum(array.astype(F32), axis=(0, 1))

    g_ffn_gain = token_sum(grad_out * normed_f)
    g_ffn_shift = token_sum(grad_out)
    grad_hf = norm_back(grad_out * ffn_gain.astype(F32), normed_f, scale_f)
    grad_ffn_b = grad_hf.astype(BF)
    g_down = product(hidden_b, grad_ffn_b, "rtf,rtd->fd").astype(BF)
    down = links.scatter(
        g_down.reshape(dp, 2, 2, part, width).transpose(1, 2, 0, 3, 4)
    )
    g_b_down = token_sum(grad_ffn_b)
    grad_hidden = product(grad_ffn_b, w_down, "rtd,fd->rtf")
    unused, gelu_pull = jax.vjp(partial(jax.nn.gelu, approximate=False), upper)
    grad_up_b = gelu_pull(grad_hidden)[0].astype(BF)
    g_up = product(after_b, grad_up_b, "rtd,rtf->df").astype(BF)
    up = links.scatter(
        g_up.reshape(dp, part, 2, 2, width).transpose(2, 3, 0, 1, 4)
    )
    g_b_up = token_sum(grad_up_b)
    grad_after = grad_hf + product(grad_up_b, w_up, "rtf,df->rtd")
    g_attn_gain = token_sum(grad_after * normed_a)
    g_attn_shift = token_sum(grad_after)
    grad_ha = norm_back(grad_after * attn_gain.astype(F32), normed_a, scale_a)
    grad_branch_b = grad_ha.astype(BF)
    g_out = product(mixed_b, grad_branch_b, "rte,rtd->ed").astype(BF)
    g_b_out = token_sum(grad_branch_b)
    grad_mixed_b = product(grad_branch_b, w_out, "rtd,ed->rte").astype(BF)

    gm = heads(grad_mixed_b)
    probs = expo / total
    grad_probs = product(gm, vh, "rqhd,rkhd->rhqk")
    inner = jnp.sum(probs * grad_probs, axis=-1, keepdims=True)
    grad_scores = (probs * (grad_probs - inner) * 0.125).astype(BF)
    gq = product(grad_scores, kh, "rhqk,rkhd->rqhd").astype(BF).reshape(1, row_len, width)
    gk = product(grad_scores, qh, "rhqk,rqhd->rkhd").astype(BF).reshape(1, row_len, width)
    gv = product(probs_b, gm, "rhqk,rqhd->rkhd").astype(BF).reshape(1, row_len, width)
    g_query = product(x, gq, "rtd,rte->de").astype(BF)
    g_key = product(x, gk, "rtd,rte->de").astype(BF)
    g_value = product(x, gv, "rtd,rte->de").astype(BF)
    g_b_query = token_sum(gq)
    g_b_value = token_sum(gv)
    grad_x = (
        grad_ha
        + product(gq, w_query, "rte,de->rtd")
        + product(gk, w_key, "rte,de->rtd")
        + product(gv, w_value, "rte,de->rtd")
    )

    small = jnp.stack(
        [g_b_query, g_b_value, g_b_out, g_attn_gain, g_attn_shift, g_b_down, g_ffn_gain, g_ffn_shift]
    ).reshape(8, dp, part)
    small = jnp.concatenate(
        [small, g_b_up.reshape(dp, 4, part).transpose(1, 0, 2)], 0
    )
    small = small.reshape(4, 3, dp, part).transpose(0, 2, 1, 3).reshape(4, dp, 1, 3 * part)
    small = jnp.pad(small, ((0, 0), (0, 0), (0, 7), (0, width - 3 * part))).astype(BF)
    four = jnp.stack([g_query, g_key, g_value, g_out]).reshape(4, dp, part, width)
    four = jnp.concatenate([four, small], 2).reshape(2, 2, dp, part + 8, width)
    attn = links.scatter(four)

    ffn_all = links.gather(jnp.stack([down, up])).astype(F32)
    attn_all = links.gather(attn).astype(F32)
    out_down = ffn_all[:, 0].reshape(4 * part, width)
    out_up = ffn_all[:, 1].transpose(1, 0, 2).reshape(part, wide)
    vec = attn_all[:, part, : 3 * part].reshape(12, part)

    lo = layer_out.reshape(4, local_len, width).astype(BF)
    layer_back = links.to_blocks(lo).astype(F32)
    grad_tokens = links.to_blocks(grad_x.reshape(4, local_len, width).astype(BF)).astype(F32)
    pooled_all = lax.all_gather(pooled[0].astype(BF), "seq", axis=0).astype(F32)
    return (
        layer_back,
        pooled_all,
        grad_tokens,
        attn_all[0, :part],
        vec[0],
        attn_all[1, :part],
        attn_all[2, :part],
        vec[1],
        attn_all[3, :part],
        vec[2],
        vec[3],
        vec[4],
        out_up,
        vec[8:].reshape(4 * part),
        out_down,
        vec[5],
        vec[6],
        vec[7],
    )


def solution(mesh):
    rows, cols = P("dp", None), P("dp")
    blocks = P("dp", "seq", None)
    return jax.shard_map(
        partial(local, mesh.shape["dp"]),
        mesh=mesh,
        in_specs=(blocks, rows, rows, blocks, P("dp", None, None)) + (P(),) * 15,
        out_specs=(
            blocks,
            P("dp", None, None),
            blocks,
            rows,
            cols,
            rows,
            rows,
            cols,
            rows,
            cols,
            cols,
            cols,
            rows,
            cols,
            rows,
            cols,
            cols,
            cols,
        ),
        check_vma=False,
    )
```

```python
from functools import partial

import jax
import jax.numpy as jnp
from jax import lax
from jax.experimental import pallas as pl
from jax.experimental.pallas import tpu as pltpu
from jax.sharding import PartitionSpec as P

HEAD = 64
SEGS = 4
EPS = 1e-12
PAD = 16
TILE = 384
BF = jnp.bfloat16
F32 = jnp.float32
AXES = ("dp", "seq")
VM = pl.BlockSpec(memory_space=pltpu.VMEM)
SM = pl.BlockSpec(memory_space=pltpu.SMEM)
ANY = pl.BlockSpec(memory_space=pl.ANY)


def dot(a, b, da, db):
    return lax.dot_general(a, b, (((da,), (db,)), ((), ())), preferred_element_type=F32)


def nn(a, b):
    return dot(a, b, 1, 0)


def tn(a, b):
    return dot(a, b, 0, 0)


def nt(a, b):
    return dot(a, b, 1, 1)


def shape(dims, kind=BF):
    return jax.ShapeDtypeStruct(dims, kind)


def whole(dims):
    return pl.BlockSpec(dims, lambda *_: (0,) * len(dims))


def call(name, kernel, args, out_shape, flops, deps=(), scalars=None, vmem=56, in_specs=None, **kw):
    in_specs = list(in_specs or [VM] * len(args))
    n = len(args)
    head = 0
    if scalars is not None:
        args, in_specs, head = [scalars] + list(args), [SM] + in_specs, 1
    nbytes = sum(a.size * a.dtype.itemsize for a in args)
    outs = out_shape if isinstance(out_shape, (tuple, list)) else (out_shape,)
    nbytes += sum(o.size * o.dtype.itemsize for o in outs)

    def body(*refs):
        kernel(*refs[: n + head], *refs[n + head + len(deps) :])

    return pl.pallas_call(
        body,
        out_shape=out_shape,
        in_specs=in_specs + [ANY] * len(deps),
        name=name,
        cost_estimate=pl.CostEstimate(flops=int(flops), bytes_accessed=int(nbytes), transcendentals=0),
        compiler_params=pltpu.CompilerParams(vmem_limit_bytes=vmem * 2**20),
        **kw,
    )(*args, *deps)


def reverse(number, bits):
    return sum(((number >> i) & 1) << (bits - 1 - i) for i in range(bits))


def attn_fwd_kernel(x, ids_row, ids_col, par, wq, wk, wv, a_o, qkv_o, p_o, mask):
    width = wq.shape[0]
    step = pl.program_id(0)
    rows = x.shape[0]

    @pl.when(step == 0)
    def _():
        xt = x[...].T
        a_o[0, :width] = xt
        ones = jnp.ones((PAD, rows), BF)
        a_o[0, width:] = ones
        a_o[1, width:] = ones
        cols = par[...].T
        qkv_o[0] = (tn(wq[...], xt) + cols[:, 0:1]).astype(BF)
        qkv_o[1] = tn(wk[...], xt).astype(BF)
        qkv_o[2] = (tn(wv[...], xt) + cols[:, 1:2]).astype(BF)
        mask[...] = jnp.where(ids_col[...] == ids_row[...], 0.0, -1e30)

    for i in range(2):
        at = pl.ds(pl.multiple_of(step * 2 * HEAD + i * HEAD, HEAD), HEAD)
        q = qkv_o[0, at] * BF(0.125)
        s = tn(qkv_o[1, at], q) + mask[...]
        top = jnp.max(s, axis=0, keepdims=True)
        e = jnp.exp(s - top)
        total = jnp.sum(e, axis=0, keepdims=True)
        p = (e * (1.0 / total)).astype(BF)
        p_o[i] = p
        a_o[1, at] = nn(qkv_o[2, at], p).astype(BF)


def attn_fwd(x, ids_row, ids_col, par, wq, wk, wv):
    rows, width = x.shape
    heads = width // HEAD
    args = (x, ids_row, ids_col, par, wq, wk, wv)
    return call(
        "attn_fwd",
        attn_fwd_kernel,
        args,
        (shape((2, width + PAD, rows)), shape((3, width, rows)), shape((heads, rows, rows))),
        6 * rows * width * width + 4 * rows * rows * width * 4,
        grid=(heads // 2,),
        in_specs=[whole(a.shape) for a in args],
        out_specs=(
            whole((2, width + PAD, rows)),
            whole((3, width, rows)),
            pl.BlockSpec((2, rows, rows), lambda i: (i, 0, 0)),
        ),
        scratch_shapes=[pltpu.VMEM((rows, rows), F32)],
    )


def norm_cols(h):
    centre = h - jnp.mean(h, axis=0, keepdims=True)
    scale = lax.rsqrt(jnp.mean(centre * centre, axis=0, keepdims=True) + EPS)
    return centre * scale, scale


def norm_cols_back(grad, normed, scale):
    return scale * (
        grad
        - jnp.mean(grad, axis=0, keepdims=True)
        - normed * jnp.mean(grad * normed, axis=0, keepdims=True)
    )


def gelu_both(u):
    t = 1.0 / (1.0 + 0.23164189 * jnp.abs(u))
    e = jnp.exp(u * u * -0.5)
    poly = t * (
        0.127414796
        + t * (-0.142248368 + t * (0.7107068705 + t * (-0.7265760135 + t * 0.5307027145)))
    )
    tail = poly * e
    phi = jnp.where(u >= 0, 1.0 - tail, tail)
    return u * phi, phi + u * e * 0.3989422804014327


def split_two(value):
    high = value.astype(BF)
    return high, (value - high.astype(F32)).astype(BF)


def ffn_kernel(
    part, sc, a, par, w_out, w_up, w_down, og, ids_row, pg, lens,
    keep_o, send_o, dg_o, after_o, na_o, sa_o, ghf_o, lay_o, pool_o, cols_o, acc,
):
    width, wide = w_up.shape
    rows = a.shape[2]
    first = sc[0] == 0
    cols = par[...].T
    normed_a, scale_a = norm_cols(
        a[0, :width].astype(F32) + (tn(w_out[...], a[1, :width]) + cols[:, 2:3])
    )
    na_o[...] = normed_a
    sa_o[...] = scale_a
    after = normed_a * cols[:, 3:4] + cols[:, 4:5]
    after_o[:width] = after.astype(BF)
    after_o[width:] = jnp.ones((PAD, rows), BF)
    acc[...] = after + cols[:, 5:6]
    pair = 2 * part
    for i in range(wide // TILE):
        at = slice(i * TILE, (i + 1) * TILE)
        lane, row = divmod(i * TILE, width)
        up = tn(w_up[:, at], after_o[:width]) + cols[row : row + TILE, 8 + lane : 9 + lane]
        hid, slope = gelu_both(up)
        dg_o[at] = slope.astype(BF)
        acc[...] += tn(w_down[at], hid.astype(BF))
        hid = hid.reshape(TILE // (2 * pair), 2, pair, rows)
        zero, one = hid[:, 0].reshape(TILE // 2, rows), hid[:, 1].reshape(TILE // 2, rows)
        half = slice(i * TILE // 2, (i + 1) * TILE // 2)
        keep_o[half] = jnp.where(first, zero, one).astype(BF)
        send_o[half] = jnp.where(first, one, zero).astype(BF)
    normed_f, scale_f = norm_cols(acc[...])
    layer = normed_f * cols[:, 6:7] + cols[:, 7:8]
    high, low = split_two(layer)
    lay_o[...] = high.T
    text = lax.broadcasted_iota(jnp.int32, (8, rows), 0) + 1
    select = jnp.where(ids_row[...] == text, 1.0, 0.0).astype(BF)
    pool_o[...] = (nt(select, high) + nt(select, low)) / lens[...]
    high, low = split_two(pg[...] / lens[...])
    grad_out = og[...].T.astype(F32) + (tn(high, select) + tn(low, select))
    cols_o[:, 0:1] = jnp.sum(grad_out * normed_f, axis=1, keepdims=True)
    cols_o[:, 1:2] = jnp.sum(grad_out, axis=1, keepdims=True)
    ghf = norm_cols_back(grad_out * cols[:, 6:7], normed_f, scale_f)
    ghf_o[...] = ghf
    ghf_b = ghf.astype(BF)
    keep_o[wide // 2 :] = ghf_b
    send_o[wide // 2 :] = ghf_b


def ffn(part, sc, a, par, w_out, w_up, w_down, og, ids_row, pg, lens):
    width, wide = w_up.shape
    rows = a.shape[2]
    tall = wide // 2 + width
    return call(
        "ffn",
        partial(ffn_kernel, part),
        (a, par, w_out, w_up, w_down, og, ids_row, pg, lens),
        (
            shape((tall, rows)),
            shape((tall, rows)),
            shape((wide, rows)),
            shape((width + PAD, rows)),
            shape((width, rows), F32),
            shape((1, rows), F32),
            shape((width, rows), F32),
            shape((rows, width)),
            shape((8, width), F32),
            shape((width, 8), F32),
        ),
        rows * width * (2 * width + 4 * wide) * 2,
        scalars=sc,
        scratch_shapes=[pltpu.VMEM((width, rows), F32)],
    )


def grad_up_kernel(sc, keep, w_down, dg, after, gu_o, send_o):
    wide, width = w_down.shape
    half = wide // 2
    core = sc[0]
    grad = keep[half:]
    for c, out in ((core, gu_o), (1 - core, send_o)):
        for k in range(half // TILE):
            at = pl.ds(pl.multiple_of(c * half + k * TILE, TILE), TILE)
            out[k * TILE : (k + 1) * TILE] = (nn(w_down[at], grad) * dg[at].astype(F32)).astype(BF)
    send_o[half:] = after[:width]


def grad_up(sc, keep, w_down, dg, after, deps):
    wide, width = w_down.shape
    rows = keep.shape[1]
    return call(
        "grad_up",
        grad_up_kernel,
        (keep, w_down, dg, after),
        (shape((wide // 2, rows)), shape((wide // 2 + width, rows))),
        2 * rows * width * wide,
        scalars=sc,
        deps=deps,
    )


def deal(sc, res, keep_o, send_o):
    dp = keep_o.shape[0]
    bits = dp.bit_length() - 1
    for out, hi in ((keep_o, sc[1]), (send_o, 1 - sc[1])):
        for lo in range(dp):
            out[lo] = res[
                jnp.where(
                    sc[0] == 0,
                    hi * dp + reverse(lo, bits),
                    (lo % 2) * dp + hi + reverse(lo // 2, bits),
                )
            ]


def down_kernel(part, sc, mine, other, keep_o, send_o, row_o, res):
    dp = keep_o.shape[0]
    half = 2 * dp * part
    rows = mine.shape[1]
    grad, grad2 = mine[half:], other[half:]
    for k in range(half // TILE):
        at = slice(k * TILE, (k + 1) * TILE)
        value = nt(mine[at], grad) + nt(other[at], grad2)
        for i in range(TILE // part):
            j, x = divmod(k * TILE // part + i, 2)
            res[x * dp + j] = value[i * part : (i + 1) * part].astype(BF)
    row_o[...] = nt(jnp.ones((8, rows), BF), grad)
    deal(sc, res, keep_o, send_o)


def grad_down(dp, sc, mine, other, width, deps):
    part = width // dp
    rows = mine.shape[1]
    piece = shape((dp, part, width))
    return call(
        "grad_down",
        partial(down_kernel, part),
        (mine, other),
        (piece, piece, shape((8, width), F32)),
        8 * rows * width * dp * part * 2,
        scalars=sc,
        deps=deps,
        scratch_shapes=[pltpu.VMEM((2 * dp, part, width), BF)],
    )


def up_kernel(part, sc, after, gu, other, keep_o, send_o, row_o, res):
    dp = keep_o.shape[0]
    width = dp * part
    half, rows = gu.shape
    ones = jnp.ones((8, rows), BF)
    for x in range(2):
        cut = slice(x * width, (x + 1) * width)
        mine, theirs = gu[cut], other[cut]
        for k in range(width // TILE):
            at = slice(k * TILE, (k + 1) * TILE)
            there = slice(half + k * TILE, half + (k + 1) * TILE)
            value = nt(after[at], mine) + nt(other[there], theirs)
            for i in range(TILE // part):
                res[x * dp + k * TILE // part + i] = value[i * part : (i + 1) * part].astype(BF)
        row_o[x] = nt(ones, mine) + nt(ones, theirs)
    deal(sc, res, keep_o, send_o)


def grad_w_up(dp, sc, after, gu, other, width, deps):
    part = width // dp
    rows = gu.shape[1]
    piece = shape((dp, part, width))
    return call(
        "grad_w_up",
        partial(up_kernel, part),
        (after, gu, other),
        (piece, piece, shape((2, 8, width), F32)),
        8 * rows * width * width * 2,
        scalars=sc,
        deps=deps,
        scratch_shapes=[pltpu.VMEM((2 * dp, part, width), BF)],
    )


def middle_kernel(sc, gu, send, w_up, w_out, na, sa, ghf, par, cols_f, gha_o, gb_o, gm_o, rows_o):
    half = gu.shape[0]
    width = w_out.shape[0]
    core = sc[0]
    cols = par[...].T
    at = pl.ds(pl.multiple_of(core * half, half), half)
    to = pl.ds(pl.multiple_of((1 - core) * half, half), half)
    grad = ghf[...] + nn(w_up[:, at], gu[...]) + nn(w_up[:, to], send[:half])
    normed = na[...]
    four = jnp.concatenate(
        [
            jnp.sum(grad * normed, axis=1, keepdims=True),
            jnp.sum(grad, axis=1, keepdims=True),
            cols_f[:, 0:2],
            jnp.zeros((width, 124), F32),
        ],
        axis=1,
    )
    rows_o[...] = four.T[:8]
    gha = norm_cols_back(grad * cols[:, 3:4], normed, sa[...])
    gha_o[...] = gha
    gb = gha.astype(BF)
    gb_o[...] = gb
    gm_o[...] = nn(w_out[...], gb).astype(BF)


def middle(sc, gu, send, w_up, w_out, na, sa, ghf, par, cols_f, deps):
    width, rows = na.shape
    return call(
        "middle",
        middle_kernel,
        (gu, send, w_up, w_out, na, sa, ghf, par, cols_f),
        (shape((width, rows), F32), shape((width, rows)), shape((width, rows)), shape((8, width), F32)),
        2 * rows * width * (w_up.shape[1] + width),
        scalars=sc,
        deps=deps,
    )


def attn_bwd_kernel(sc, qkv, p, a, gm, gb, d_o, keep_o, send_o):
    first = sc[0] == 0
    for i in range(2):
        at = slice(i * HEAD, (i + 1) * HEAD)
        grad = gm[at]
        inner = jnp.sum(a[0, at].astype(F32) * grad.astype(F32), axis=0, keepdims=True)
        probs = p[i]
        gp = tn(qkv[2, at], grad)
        gs = (probs.astype(F32) * (gp - inner)).astype(BF)
        gq = (nn(qkv[1, at], gs) * 0.125).astype(BF)
        gk = (nt(qkv[0, at], gs) * 0.125).astype(BF)
        gv = nt(grad, probs).astype(BF)
        d_o[0, at] = gq
        d_o[1, at] = gk
        d_o[2, at] = gv
        last = gb[at]
        keep_o[0, at] = jnp.where(first, gq, gv)
        keep_o[1, at] = jnp.where(first, gk, last)
        send_o[0, at] = jnp.where(first, gv, gq)
        send_o[1, at] = jnp.where(first, last, gk)


def attn_bwd(part_no, sc, qkv, p, a, gm, gb, deps):
    rows = p.shape[1]
    width = gm.shape[0]
    half = width // 2
    pairs = half // (2 * HEAD)
    base = part_no * pairs
    block = 2 * HEAD
    row = pl.BlockSpec((block, rows), lambda i: (base + i, 0))
    two = pl.BlockSpec((2, block, rows), lambda i: (0, i, 0))
    return call(
        "attn_bwd",
        attn_bwd_kernel,
        (qkv, p, a, gm, gb),
        (shape((3, half, rows)), shape((2, half, rows)), shape((2, half, rows))),
        2 * rows * rows * half * 4 * 4,
        scalars=sc,
        deps=deps,
        grid=(pairs,),
        in_specs=[
            pl.BlockSpec((3, block, rows), lambda i: (0, base + i, 0)),
            pl.BlockSpec((2, rows, rows), lambda i: (base + i, 0, 0)),
            pl.BlockSpec((1, block, rows), lambda i: (1, base + i, 0)),
            row,
            row,
        ],
        out_specs=(pl.BlockSpec((3, block, rows), lambda i: (0, i, 0)), two, two),
    )


def attn_w_products(part, sc, a, a2, mine, other, res):
    core = sc[0]
    dp = res.shape[0] // 2
    width = dp * part
    ones = jnp.ones((8, a.shape[2]), BF)
    sums = []
    for m in range(2):
        pick_a = 0 if m == 0 else core
        for k in range(width // TILE):
            at = slice(k * TILE, (k + 1) * TILE)
            value = nt(a[pick_a, at], mine[m]) + nt(a2[pick_a, at], other[m])
            for i in range(TILE // part):
                res[m * dp + k * TILE // part + i, :part] = value[i * part : (i + 1) * part].astype(BF)
        sums.append(nt(ones, mine[m]) + nt(ones, other[m]))
    return sums


def attn_w1_kernel(part, sc, a, a2, mine, other, keep_o, send_o, row_o, res):
    sums = attn_w_products(part, sc, a, a2, mine, other, res)
    row_o[0], row_o[1] = sums
    deal(sc, res, keep_o, send_o)


def attn_w2_kernel(
    part, sc, a, a2, mine, other, row1, rows, row_d, row_u, keep_o, send_o, res
):
    core = sc[0]
    dp = keep_o.shape[0]
    width = dp * part
    half = width // 2
    sums = attn_w_products(part, sc, a, a2, mine, other, res)
    m0 = jnp.concatenate([row1[0], sums[0]], axis=1)[0:1]
    m1 = jnp.concatenate([row1[1], sums[1]], axis=1)[0:1]
    zero = jnp.zeros_like(m0)
    first = core == 0
    vectors = jnp.concatenate(
        [
            jnp.where(first, m0, zero),
            jnp.where(first, zero, m0),
            jnp.where(first, zero, m1),
            rows[0:2],
            row_d[0:1],
            rows[2:4],
        ],
        axis=0,
    )
    for j in range(dp):
        ups = []
        for v in range(4):
            x, lane = divmod((j % (dp // 2)) * 4 * part + v * part, width)
            ups.append(row_u[x, 0:1, lane : lane + part])
        ups = jnp.concatenate(ups + [jnp.zeros((4, part), F32)], axis=0)
        ups = jnp.where(core == j // (dp // 2), ups, jnp.zeros_like(ups))
        block = jnp.concatenate([vectors[:, j * part : (j + 1) * part], ups], axis=0)
        block = jnp.concatenate([block, jnp.zeros((PAD, half - part), F32)], axis=1)
        res[j, part:] = block.astype(BF)
        res[dp + j, part:] = jnp.zeros((PAD, half), BF)
    deal(sc, res, keep_o, send_o)


def attn_w(part, sc, a, a2, mine, other, vectors=(), deps=()):
    half = mine.shape[1]
    width = 2 * half
    dp = width // part
    rows = a.shape[2]
    tall = part + (PAD if vectors else 0)
    piece = shape((dp, tall, half))
    outs = (piece, piece) if vectors else (piece, piece, shape((2, 8, half), F32))
    return call(
        "attn_w",
        partial(attn_w2_kernel if vectors else attn_w1_kernel, part),
        (a, a2, mine, other) + tuple(vectors),
        outs,
        8 * rows * width * half * 2,
        scalars=sc,
        deps=deps,
        scratch_shapes=[pltpu.VMEM((2 * dp, tall, half), BF)],
    )


def tokens_kernel(gha, d1, d2, wq, wk, wv, out):
    half = d1.shape[1]
    total = gha[...]
    for i, w in enumerate((wq, wk, wv)):
        total += nn(w[:, :half], d1[i]) + nn(w[:, half:], d2[i])
    out[...] = total.astype(BF).T


def grad_tokens_rows(gha, d1, d2, wq, wk, wv, deps=()):
    width, rows = gha.shape
    return call(
        "grad_tokens",
        tokens_kernel,
        (gha, d1, d2, wq, wk, wv),
        shape((rows, width)),
        6 * rows * width * width,
        deps=deps,
    )


def add_kernel(at, sc, mine, got, keep_o, send_o):
    bit = sc[at]
    keep_o[...] = (mine[bit].astype(F32) + got[bit].astype(F32)).astype(BF)
    send_o[...] = (mine[1 - bit].astype(F32) + got[1 - bit].astype(F32)).astype(BF)


def add_split(at, sc, mine, got, deps=()):
    half = mine.shape[0] // 2
    tail = mine.shape[1:]
    mine, got = mine.reshape((2, half) + tail), got.reshape((2, half) + tail)
    piece = shape((half,) + tail)
    return call("add_split", partial(add_kernel, at), (mine, got), (piece, piece), mine.size, scalars=sc, deps=deps)


def pick(array, index):
    return lax.dynamic_index_in_dim(array, index, 0, keepdims=False)


class Links:
    def __init__(self, dp):
        self.dp = dp
        self.bits = dp.bit_length() - 1
        seq = lax.axis_index("seq")
        place = lax.axis_index("dp")
        self.core = lax.rem(seq, 2)
        self.x = lax.div(seq, 2)
        dp_bits = [lax.rem(lax.div(place, 1 << i), 2) for i in range(self.bits)]
        dp_steps = [(0, 1 << i) for i in range(self.bits)]
        self.steps = list(zip([(2, 0)] + dp_steps, dp_steps + [(2, 0)]))
        pairs = zip([self.x] + dp_bits, dp_bits + [self.x])
        my_bits = [jnp.where(self.core == 0, p, q) for p, q in pairs]
        self.scalars = jnp.stack([self.core] + my_bits).astype(jnp.int32)

    def swap(self, array, first, second):
        perm = []
        for d in range(self.dp):
            for s in range(4):
                ds, dd = second if s % 2 else first
                perm.append((d * 4 + s, (d ^ dd) * 4 + (s ^ ds)))
        return lax.ppermute(array, AXES, perm)

    def flip_core(self, array):
        return self.swap(array, (1, 0), (1, 0))

    def flip_x(self, array):
        return self.swap(array, (2, 0), (2, 0))

    def to_rows(self, array):
        a = array.reshape((2, 2) + array.shape[1:])
        a = jnp.swapaxes(a, 0, 1)
        keep, send = pick(a, self.core), pick(a, 1 - self.core)
        both = jnp.stack([keep, self.flip_core(send)], 1)
        keep, send = pick(both, self.x), pick(both, 1 - self.x)
        return jnp.concatenate([keep, self.flip_x(send)], 0)

    def to_blocks(self, array):
        other = self.flip_x(array[2:])
        pair = jnp.stack([array[:2], other])
        pair = jnp.where(self.x == 0, pair, pair[::-1])
        back = self.flip_core(pair[:, 1])
        rows = jnp.stack([pair[:, 0], back])
        rows = jnp.where(self.core == 0, rows, rows[::-1])
        return jnp.swapaxes(rows, 0, 1).reshape((4,) + array.shape[1:])

    def step(self, at, keep, send, deps=()):
        got = self.swap(send, *self.steps[at])
        if at < self.bits:
            return add_split(at + 2, self.scalars, keep, got, deps)
        return (keep.astype(F32) + got.astype(F32)).astype(BF)[0]

    def gather(self, chunk):
        got = self.flip_x(chunk)
        pair = jnp.where(self.x == 0, jnp.stack([chunk, got]), jnp.stack([got, chunk]))
        got = self.flip_core(pair)
        four = jnp.where(self.core == 0, jnp.stack([pair, got]), jnp.stack([got, pair]))
        return four.reshape((4,) + chunk.shape)


def local(
    dp,
    tokens,
    seg_ids,
    text_len,
    out_grad,
    pooled_grad,
    w_query,
    b_query,
    w_key,
    w_value,
    b_value,
    w_out,
    b_out,
    attn_gain,
    attn_shift,
    w_up,
    b_up,
    w_down,
    b_down,
    ffn_gain,
    ffn_shift,
):
    rows_dev, local_len, width = tokens.shape
    row_len = seg_ids.shape[1]
    links = Links(dp)
    sc = links.scalars
    seq = lax.axis_index("seq")
    wide = w_up.shape[1]
    part = width // dp

    blocks = pick(seg_ids, seq).reshape(4, local_len)
    ids = jnp.stack([pick(blocks, seq ^ k) for k in range(4)]).reshape(row_len)
    lens = jnp.concatenate([pick(text_len, seq), jnp.ones((4,), jnp.int32)]).astype(F32)[:, None]
    pg = jnp.pad(pick(pooled_grad, seq), ((0, 4), (0, 0))).astype(F32)
    par = jnp.concatenate(
        [
            jnp.stack([b_query, b_value, b_out, attn_gain, attn_shift, b_down, ffn_gain, ffn_shift]),
            b_up.reshape(4, width),
            jnp.zeros((4, width), BF),
        ]
    ).astype(F32)

    x = links.to_rows(tokens).reshape(row_len, width)
    og = links.to_rows(out_grad).reshape(row_len, width)

    a, qkv, probs = attn_fwd(x, ids[None, :], ids[:, None], par, w_query, w_key, w_value)
    a2 = links.flip_core(a)
    keep1, send1, dg, after, na, sa, ghf, lay, pool, cols_f = ffn(
        part, sc, a, par, w_out, w_up, w_down, og, ids[None, :], pg, lens
    )
    got1 = links.flip_core(send1)
    gu, send2 = grad_up(sc, keep1, w_down, dg, after, ())
    got2 = links.flip_core(send2)
    dk, ds, row_d = grad_down(dp, sc, keep1, got1, width, (gu,))
    uk, us, row_u = grad_w_up(dp, sc, after, gu, got2, width, (dk,))
    gha, gb, gm, rows4 = middle(sc, gu, send2, w_up, w_out, na, sa, ghf, par, cols_f, (uk,))
    d1, ak1, as1 = attn_bwd(0, sc, qkv, probs, a, gm, gb, ())
    ag1 = links.flip_core(as1)
    d2, ak2, as2 = attn_bwd(1, sc, qkv, probs, a, gm, gb, (d1,))
    ag2 = links.flip_core(as2)
    tk1, ts1, row1 = attn_w(part, sc, a, a2, ak1, ag1, (), (d2,))
    tk2, ts2 = attn_w(part, sc, a, a2, ak2, ag2, (row1, rows4, row_d, row_u), (tk1,))
    gx = grad_tokens_rows(gha, d1, d2, w_query, w_key, w_value, (tk2,))

    for at in range(links.bits):
        dk, ds = links.step(at, dk, ds)
        uk, us = links.step(at, uk, us)
        tk1, ts1 = links.step(at, tk1, ts1)
        tk2, ts2 = links.step(at, tk2, ts2)
    at = links.bits
    down, up = links.step(at, dk, ds), links.step(at, uk, us)
    t1, t2 = links.step(at, tk1, ts1), links.step(at, tk2, ts2)

    ffn_all = links.gather(jnp.stack([down, up]))
    attn_all = links.gather(jnp.concatenate([t1, t2], 0))
    out_down = ffn_all[:, 0].reshape(4 * part, width).astype(F32)
    out_up = ffn_all[:, 1].transpose(1, 0, 2).reshape(part, wide).astype(F32)
    square = jnp.concatenate([attn_all[:, :part], attn_all[:, part : 2 * part]], 2).astype(F32)
    small = attn_all[0::2, 2 * part :, :part].astype(F32)
    vec = small[0] + small[1]

    layer_back = links.to_blocks(lay.reshape(4, local_len, width)).astype(F32)
    grad_tokens = links.to_blocks(gx.reshape(4, local_len, width)).astype(F32)
    pooled_all = lax.all_gather(pool[:SEGS].astype(BF), "seq", axis=0).astype(F32)
    return (
        layer_back,
        pooled_all,
        grad_tokens,
        square[0],
        vec[0],
        square[1],
        square[2],
        vec[1],
        square[3],
        vec[2],
        vec[3],
        vec[4],
        out_up,
        vec[8:12].reshape(4 * part),
        out_down,
        vec[5],
        vec[6],
        vec[7],
    )


def solution(mesh):
    rows, cols = P("dp", None), P("dp")
    blocks = P("dp", "seq", None)
    return jax.shard_map(
        partial(local, mesh.shape["dp"]),
        mesh=mesh,
        in_specs=(blocks, rows, rows, blocks, P("dp", None, None)) + (P(),) * 15,
        out_specs=(
            blocks,
            P("dp", None, None),
            blocks,
            rows,
            cols,
            rows,
            rows,
            cols,
            rows,
            cols,
            cols,
            cols,
            rows,
            cols,
            rows,
            cols,
            cols,
            cols,
        ),
        check_vma=False,
    )
```

```python
from functools import partial

import jax
import jax.numpy as jnp
from jax import lax
from jax.experimental import pallas as pl
from jax.experimental.pallas import tpu as pltpu
from jax.sharding import PartitionSpec as P

HEAD = 64
SEGS = 4
EPS = 1e-12
PAD = 16
TILE = 384
BF = jnp.bfloat16
F32 = jnp.float32
AXES = ("dp", "seq")
VM = pl.BlockSpec(memory_space=pltpu.VMEM)
SM = pl.BlockSpec(memory_space=pltpu.SMEM)
ANY = pl.BlockSpec(memory_space=pl.ANY)


def dot(a, b, da, db):
    return lax.dot_general(a, b, (((da,), (db,)), ((), ())), preferred_element_type=F32)


def nn(a, b):
    return dot(a, b, 1, 0)


def tn(a, b):
    return dot(a, b, 0, 0)


def nt(a, b):
    return dot(a, b, 1, 1)


def shape(dims, kind=BF):
    return jax.ShapeDtypeStruct(dims, kind)


def whole(dims):
    return pl.BlockSpec(dims, lambda *_: (0,) * len(dims))


def call(name, kernel, args, out_shape, flops, deps=(), scalars=None, vmem=56, in_specs=None, **kw):
    in_specs = list(in_specs or [VM] * len(args))
    n = len(args)
    head = 0
    if scalars is not None:
        args, in_specs, head = [scalars] + list(args), [SM] + in_specs, 1
    nbytes = sum(a.size * a.dtype.itemsize for a in args)
    outs = out_shape if isinstance(out_shape, (tuple, list)) else (out_shape,)
    nbytes += sum(o.size * o.dtype.itemsize for o in outs)

    def body(*refs):
        kernel(*refs[: n + head], *refs[n + head + len(deps) :])

    return pl.pallas_call(
        body,
        out_shape=out_shape,
        in_specs=in_specs + [ANY] * len(deps),
        name=name,
        cost_estimate=pl.CostEstimate(flops=int(flops), bytes_accessed=int(nbytes), transcendentals=0),
        compiler_params=pltpu.CompilerParams(vmem_limit_bytes=vmem * 2**20),
        **kw,
    )(*args, *deps)


def reverse(number, bits):
    return sum(((number >> i) & 1) << (bits - 1 - i) for i in range(bits))


def attn_fwd_kernel(x, ids_row, ids_col, par, wq, wk, wv, a_o, qkv_o, p_o, mask):
    width = wq.shape[0]
    step = pl.program_id(0)
    rows = x.shape[0]

    @pl.when(step == 0)
    def _():
        xt = x[...].T
        a_o[0, :width] = xt
        ones = jnp.ones((PAD, rows), BF)
        a_o[0, width:] = ones
        a_o[1, width:] = ones
        cols = par[...].T
        qkv_o[0] = (tn(wq[...], xt) + cols[:, 0:1]).astype(BF)
        qkv_o[1] = tn(wk[...], xt).astype(BF)
        qkv_o[2] = (tn(wv[...], xt) + cols[:, 1:2]).astype(BF)
        mask[...] = jnp.where(ids_col[...] == ids_row[...], 0.0, -1e30)

    for i in range(2):
        at = pl.ds(pl.multiple_of(step * 2 * HEAD + i * HEAD, HEAD), HEAD)
        q = qkv_o[0, at] * BF(0.125)
        s = tn(qkv_o[1, at], q) + mask[...]
        top = jnp.max(s, axis=0, keepdims=True)
        e = jnp.exp(s - top)
        total = jnp.sum(e, axis=0, keepdims=True)
        p = (e * (1.0 / total)).astype(BF)
        p_o[i] = p
        a_o[1, at] = nn(qkv_o[2, at], p).astype(BF)


def attn_fwd(x, ids_row, ids_col, par, wq, wk, wv):
    rows, width = x.shape
    heads = width // HEAD
    args = (x, ids_row, ids_col, par, wq, wk, wv)
    return call(
        "attn_fwd",
        attn_fwd_kernel,
        args,
        (shape((2, width + PAD, rows)), shape((3, width, rows)), shape((heads, rows, rows))),
        6 * rows * width * width + 4 * rows * rows * width * 4,
        grid=(heads // 2,),
        in_specs=[whole(a.shape) for a in args],
        out_specs=(
            whole((2, width + PAD, rows)),
            whole((3, width, rows)),
            pl.BlockSpec((2, rows, rows), lambda i: (i, 0, 0)),
        ),
        scratch_shapes=[pltpu.VMEM((rows, rows), F32)],
    )


def norm_cols(h):
    centre = h - jnp.mean(h, axis=0, keepdims=True)
    scale = lax.rsqrt(jnp.mean(centre * centre, axis=0, keepdims=True) + EPS)
    return centre * scale, scale


def norm_cols_back(grad, normed, scale):
    return scale * (
        grad
        - jnp.mean(grad, axis=0, keepdims=True)
        - normed * jnp.mean(grad * normed, axis=0, keepdims=True)
    )


def gelu_both(u):
    t = 1.0 / (1.0 + 0.23164189 * jnp.abs(u))
    e = jnp.exp(u * u * -0.5)
    poly = t * (
        0.127414796
        + t * (-0.142248368 + t * (0.7107068705 + t * (-0.7265760135 + t * 0.5307027145)))
    )
    tail = poly * e
    phi = jnp.where(u >= 0, 1.0 - tail, tail)
    return u * phi, phi + u * e * 0.3989422804014327


def split_two(value):
    high = value.astype(BF)
    return high, (value - high.astype(F32)).astype(BF)


def ffn_kernel(
    part, sc, a, par, w_out, w_up, w_down, og, ids_row, pg, lens,
    keep_o, send_o, dg_o, after_o, na_o, sa_o, ghf_o, lay_o, pool_o, cols_o, acc,
):
    width, wide = w_up.shape
    rows = a.shape[2]
    first = sc[0] == 0
    cols = par[...].T
    normed_a, scale_a = norm_cols(
        a[0, :width].astype(F32) + (tn(w_out[...], a[1, :width]) + cols[:, 2:3])
    )
    na_o[...] = normed_a
    sa_o[...] = scale_a
    after = normed_a * cols[:, 3:4] + cols[:, 4:5]
    after_o[:width] = after.astype(BF)
    after_o[width:] = jnp.ones((PAD, rows), BF)
    acc[...] = after + cols[:, 5:6]
    pair = 2 * part
    for i in range(wide // TILE):
        at = slice(i * TILE, (i + 1) * TILE)
        lane, row = divmod(i * TILE, width)
        up = tn(w_up[:, at], after_o[:width]) + cols[row : row + TILE, 8 + lane : 9 + lane]
        hid, slope = gelu_both(up)
        dg_o[at] = slope.astype(BF)
        acc[...] += tn(w_down[at], hid.astype(BF))
        hid = hid.reshape(TILE // (2 * pair), 2, pair, rows)
        zero, one = hid[:, 0].reshape(TILE // 2, rows), hid[:, 1].reshape(TILE // 2, rows)
        half = slice(i * TILE // 2, (i + 1) * TILE // 2)
        keep_o[half] = jnp.where(first, zero, one).astype(BF)
        send_o[half] = jnp.where(first, one, zero).astype(BF)
    normed_f, scale_f = norm_cols(acc[...])
    layer = normed_f * cols[:, 6:7] + cols[:, 7:8]
    high, low = split_two(layer)
    lay_o[...] = high.T
    text = lax.broadcasted_iota(jnp.int32, (8, rows), 0) + 1
    select = jnp.where(ids_row[...] == text, 1.0, 0.0).astype(BF)
    pool_o[...] = (nt(select, high) + nt(select, low)) / lens[...]
    high, low = split_two(pg[...] / lens[...])
    grad_out = og[...].T.astype(F32) + (tn(high, select) + tn(low, select))
    cols_o[:, 0:1] = jnp.sum(grad_out * normed_f, axis=1, keepdims=True)
    cols_o[:, 1:2] = jnp.sum(grad_out, axis=1, keepdims=True)
    ghf = norm_cols_back(grad_out * cols[:, 6:7], normed_f, scale_f)
    ghf_o[...] = ghf
    ghf_b = ghf.astype(BF)
    keep_o[wide // 2 :] = ghf_b
    send_o[wide // 2 :] = ghf_b


def ffn(part, sc, a, par, w_out, w_up, w_down, og, ids_row, pg, lens):
    width, wide = w_up.shape
    rows = a.shape[2]
    tall = wide // 2 + width
    return call(
        "ffn",
        partial(ffn_kernel, part),
        (a, par, w_out, w_up, w_down, og, ids_row, pg, lens),
        (
            shape((tall, rows)),
            shape((tall, rows)),
            shape((wide, rows)),
            shape((width + PAD, rows)),
            shape((width, rows), F32),
            shape((1, rows), F32),
            shape((width, rows), F32),
            shape((rows, width)),
            shape((8, width), F32),
            shape((width, 8), F32),
        ),
        rows * width * (2 * width + 4 * wide) * 2,
        scalars=sc,
        scratch_shapes=[pltpu.VMEM((width, rows), F32)],
    )


def grad_up_kernel(sc, keep, w_down, dg, after, gu_o, send_o):
    wide, width = w_down.shape
    half = wide // 2
    core = sc[0]
    grad = keep[half:]
    for c, out in ((core, gu_o), (1 - core, send_o)):
        for k in range(half // TILE):
            at = pl.ds(pl.multiple_of(c * half + k * TILE, TILE), TILE)
            out[k * TILE : (k + 1) * TILE] = (nn(w_down[at], grad) * dg[at].astype(F32)).astype(BF)
    send_o[half:] = after[:width]


def grad_up(sc, keep, w_down, dg, after, deps):
    wide, width = w_down.shape
    rows = keep.shape[1]
    return call(
        "grad_up",
        grad_up_kernel,
        (keep, w_down, dg, after),
        (shape((wide // 2, rows)), shape((wide // 2 + width, rows))),
        2 * rows * width * wide,
        scalars=sc,
        deps=deps,
    )


def deal(sc, res, keep_o, send_o):
    dp = keep_o.shape[0]
    bits = dp.bit_length() - 1
    for out, hi in ((keep_o, sc[1]), (send_o, 1 - sc[1])):
        for lo in range(dp):
            out[lo] = res[
                jnp.where(
                    sc[0] == 0,
                    hi * dp + reverse(lo, bits),
                    (lo % 2) * dp + hi + reverse(lo // 2, bits),
                )
            ]


def down_kernel(part, sc, mine, other, keep_o, send_o, row_o, res):
    dp = keep_o.shape[0]
    half = 2 * dp * part
    rows = mine.shape[1]
    grad, grad2 = mine[half:], other[half:]
    for k in range(half // TILE):
        at = slice(k * TILE, (k + 1) * TILE)
        value = nt(mine[at], grad) + nt(other[at], grad2)
        for i in range(TILE // part):
            j, x = divmod(k * TILE // part + i, 2)
            res[x * dp + j] = value[i * part : (i + 1) * part].astype(BF)
    row_o[...] = nt(jnp.ones((8, rows), BF), grad)
    deal(sc, res, keep_o, send_o)


def grad_down(dp, sc, mine, other, width, deps):
    part = width // dp
    rows = mine.shape[1]
    piece = shape((dp, part, width))
    return call(
        "grad_down",
        partial(down_kernel, part),
        (mine, other),
        (piece, piece, shape((8, width), F32)),
        8 * rows * width * dp * part * 2,
        scalars=sc,
        deps=deps,
        scratch_shapes=[pltpu.VMEM((2 * dp, part, width), BF)],
    )


def up_kernel(part, sc, after, gu, other, keep_o, send_o, row_o, res):
    dp = keep_o.shape[0]
    width = dp * part
    half, rows = gu.shape
    ones = jnp.ones((8, rows), BF)
    for x in range(2):
        cut = slice(x * width, (x + 1) * width)
        mine, theirs = gu[cut], other[cut]
        for k in range(width // TILE):
            at = slice(k * TILE, (k + 1) * TILE)
            there = slice(half + k * TILE, half + (k + 1) * TILE)
            value = nt(after[at], mine) + nt(other[there], theirs)
            for i in range(TILE // part):
                res[x * dp + k * TILE // part + i] = value[i * part : (i + 1) * part].astype(BF)
        row_o[x] = nt(ones, mine) + nt(ones, theirs)
    deal(sc, res, keep_o, send_o)


def grad_w_up(dp, sc, after, gu, other, width, deps):
    part = width // dp
    rows = gu.shape[1]
    piece = shape((dp, part, width))
    return call(
        "grad_w_up",
        partial(up_kernel, part),
        (after, gu, other),
        (piece, piece, shape((2, 8, width), F32)),
        8 * rows * width * width * 2,
        scalars=sc,
        deps=deps,
        scratch_shapes=[pltpu.VMEM((2 * dp, part, width), BF)],
    )


def middle_kernel(sc, gu, send, w_up, w_out, na, sa, ghf, par, cols_f, gha_o, gb_o, gm_o, rows_o):
    half = gu.shape[0]
    width = w_out.shape[0]
    core = sc[0]
    cols = par[...].T
    at = pl.ds(pl.multiple_of(core * half, half), half)
    to = pl.ds(pl.multiple_of((1 - core) * half, half), half)
    grad = ghf[...] + nn(w_up[:, at], gu[...]) + nn(w_up[:, to], send[:half])
    normed = na[...]
    four = jnp.concatenate(
        [
            jnp.sum(grad * normed, axis=1, keepdims=True),
            jnp.sum(grad, axis=1, keepdims=True),
            cols_f[:, 0:2],
            jnp.zeros((width, 124), F32),
        ],
        axis=1,
    )
    rows_o[...] = four.T[:8]
    gha = norm_cols_back(grad * cols[:, 3:4], normed, sa[...])
    gha_o[...] = gha
    gb = gha.astype(BF)
    gb_o[...] = gb
    gm_o[...] = nn(w_out[...], gb).astype(BF)


def middle(sc, gu, send, w_up, w_out, na, sa, ghf, par, cols_f, deps):
    width, rows = na.shape
    return call(
        "middle",
        middle_kernel,
        (gu, send, w_up, w_out, na, sa, ghf, par, cols_f),
        (shape((width, rows), F32), shape((width, rows)), shape((width, rows)), shape((8, width), F32)),
        2 * rows * width * (w_up.shape[1] + width),
        scalars=sc,
        deps=deps,
    )


def attn_bwd_kernel(sc, qkv, p, a, gm, gb, d_o, keep_o, send_o):
    first = sc[0] == 0
    for i in range(2):
        at = slice(i * HEAD, (i + 1) * HEAD)
        grad = gm[at]
        inner = jnp.sum(a[0, at].astype(F32) * grad.astype(F32), axis=0, keepdims=True)
        probs = p[i]
        gp = tn(qkv[2, at], grad)
        gs = (probs.astype(F32) * (gp - inner)).astype(BF)
        gq = (nn(qkv[1, at], gs) * 0.125).astype(BF)
        gk = (nt(qkv[0, at], gs) * 0.125).astype(BF)
        gv = nt(grad, probs).astype(BF)
        d_o[0, at] = gq
        d_o[1, at] = gk
        d_o[2, at] = gv
        last = gb[at]
        keep_o[0, at] = jnp.where(first, gq, gv)
        keep_o[1, at] = jnp.where(first, gk, last)
        send_o[0, at] = jnp.where(first, gv, gq)
        send_o[1, at] = jnp.where(first, last, gk)


def attn_bwd(part_no, sc, qkv, p, a, gm, gb, deps):
    rows = p.shape[1]
    width = gm.shape[0]
    half = width // 2
    pairs = half // (2 * HEAD)
    base = part_no * pairs
    block = 2 * HEAD
    row = pl.BlockSpec((block, rows), lambda i: (base + i, 0))
    two = pl.BlockSpec((2, block, rows), lambda i: (0, i, 0))
    return call(
        "attn_bwd",
        attn_bwd_kernel,
        (qkv, p, a, gm, gb),
        (shape((3, half, rows)), shape((2, half, rows)), shape((2, half, rows))),
        2 * rows * rows * half * 4 * 4,
        scalars=sc,
        deps=deps,
        grid=(pairs,),
        in_specs=[
            pl.BlockSpec((3, block, rows), lambda i: (0, base + i, 0)),
            pl.BlockSpec((2, rows, rows), lambda i: (base + i, 0, 0)),
            pl.BlockSpec((1, block, rows), lambda i: (1, base + i, 0)),
            row,
            row,
        ],
        out_specs=(pl.BlockSpec((3, block, rows), lambda i: (0, i, 0)), two, two),
    )


def attn_w_products(part, sc, a, a2, mine, other, res):
    core = sc[0]
    dp = res.shape[0] // 2
    width = dp * part
    ones = jnp.ones((8, a.shape[2]), BF)
    sums = []
    for m in range(2):
        pick_a = 0 if m == 0 else core
        for k in range(width // TILE):
            at = slice(k * TILE, (k + 1) * TILE)
            value = nt(a[pick_a, at], mine[m]) + nt(a2[pick_a, at], other[m])
            for i in range(TILE // part):
                res[m * dp + k * TILE // part + i, :part] = value[i * part : (i + 1) * part].astype(BF)
        sums.append(nt(ones, mine[m]) + nt(ones, other[m]))
    return sums


def attn_w1_kernel(part, sc, a, a2, mine, other, keep_o, send_o, row_o, res):
    sums = attn_w_products(part, sc, a, a2, mine, other, res)
    row_o[0], row_o[1] = sums
    deal(sc, res, keep_o, send_o)


def attn_w2_kernel(
    part, sc, a, a2, mine, other, row1, rows, row_d, row_u, keep_o, send_o, res
):
    core = sc[0]
    dp = keep_o.shape[0]
    width = dp * part
    half = width // 2
    sums = attn_w_products(part, sc, a, a2, mine, other, res)
    m0 = jnp.concatenate([row1[0], sums[0]], axis=1)[0:1]
    m1 = jnp.concatenate([row1[1], sums[1]], axis=1)[0:1]
    zero = jnp.zeros_like(m0)
    first = core == 0
    vectors = jnp.concatenate(
        [
            jnp.where(first, m0, zero),
            jnp.where(first, zero, m0),
            jnp.where(first, zero, m1),
            rows[0:2],
            row_d[0:1],
            rows[2:4],
        ],
        axis=0,
    )
    for j in range(dp):
        ups = []
        for v in range(4):
            x, lane = divmod((j % (dp // 2)) * 4 * part + v * part, width)
            ups.append(row_u[x, 0:1, lane : lane + part])
        ups = jnp.concatenate(ups + [jnp.zeros((4, part), F32)], axis=0)
        ups = jnp.where(core == j // (dp // 2), ups, jnp.zeros_like(ups))
        block = jnp.concatenate([vectors[:, j * part : (j + 1) * part], ups], axis=0)
        block = jnp.concatenate([block, jnp.zeros((PAD, half - part), F32)], axis=1)
        res[j, part:] = block.astype(BF)
        res[dp + j, part:] = jnp.zeros((PAD, half), BF)
    deal(sc, res, keep_o, send_o)


def attn_w(part, sc, a, a2, mine, other, vectors=(), deps=()):
    half = mine.shape[1]
    width = 2 * half
    dp = width // part
    rows = a.shape[2]
    tall = part + (PAD if vectors else 0)
    piece = shape((dp, tall, half))
    outs = (piece, piece) if vectors else (piece, piece, shape((2, 8, half), F32))
    return call(
        "attn_w",
        partial(attn_w2_kernel if vectors else attn_w1_kernel, part),
        (a, a2, mine, other) + tuple(vectors),
        outs,
        8 * rows * width * half * 2,
        scalars=sc,
        deps=deps,
        scratch_shapes=[pltpu.VMEM((2 * dp, tall, half), BF)],
    )


def tokens_kernel(gha, d1, d2, wq, wk, wv, out):
    half = d1.shape[1]
    total = gha[...]
    for i, w in enumerate((wq, wk, wv)):
        total += nn(w[:, :half], d1[i]) + nn(w[:, half:], d2[i])
    out[...] = total.astype(BF).T


def grad_tokens_rows(gha, d1, d2, wq, wk, wv, deps=()):
    width, rows = gha.shape
    return call(
        "grad_tokens",
        tokens_kernel,
        (gha, d1, d2, wq, wk, wv),
        shape((rows, width)),
        6 * rows * width * width,
        deps=deps,
    )


def add_kernel(at, sc, mine, got, keep_o, send_o):
    bit = sc[at]
    keep_o[...] = (mine[bit].astype(F32) + got[bit].astype(F32)).astype(BF)
    send_o[...] = (mine[1 - bit].astype(F32) + got[1 - bit].astype(F32)).astype(BF)


def add_split(at, sc, mine, got, deps=()):
    half = mine.shape[0] // 2
    tail = mine.shape[1:]
    mine, got = mine.reshape((2, half) + tail), got.reshape((2, half) + tail)
    piece = shape((half,) + tail)
    return call("add_split", partial(add_kernel, at), (mine, got), (piece, piece), mine.size, scalars=sc, deps=deps)


def pick(array, index):
    return lax.dynamic_index_in_dim(array, index, 0, keepdims=False)


class Links:
    def __init__(self, dp):
        self.dp = dp
        self.bits = dp.bit_length() - 1
        seq = lax.axis_index("seq")
        place = lax.axis_index("dp")
        self.core = lax.rem(seq, 2)
        self.x = lax.div(seq, 2)
        dp_bits = [lax.rem(lax.div(place, 1 << i), 2) for i in range(self.bits)]
        dp_steps = [(0, 1 << i) for i in range(self.bits)]
        self.steps = list(zip([(2, 0)] + dp_steps, dp_steps + [(2, 0)]))
        pairs = zip([self.x] + dp_bits, dp_bits + [self.x])
        my_bits = [jnp.where(self.core == 0, p, q) for p, q in pairs]
        self.scalars = jnp.stack([self.core] + my_bits).astype(jnp.int32)

    def swap(self, array, first, second):
        perm = []
        for d in range(self.dp):
            for s in range(4):
                ds, dd = second if s % 2 else first
                perm.append((d * 4 + s, (d ^ dd) * 4 + (s ^ ds)))
        return lax.ppermute(array, AXES, perm)

    def flip_core(self, array):
        return self.swap(array, (1, 0), (1, 0))

    def flip_x(self, array):
        return self.swap(array, (2, 0), (2, 0))

    def to_rows(self, array):
        a = array.reshape((2, 2) + array.shape[1:])
        a = jnp.swapaxes(a, 0, 1)
        keep, send = pick(a, self.core), pick(a, 1 - self.core)
        both = jnp.stack([keep, self.flip_core(send)], 1)
        keep, send = pick(both, self.x), pick(both, 1 - self.x)
        return jnp.concatenate([keep, self.flip_x(send)], 0)

    def to_blocks(self, array):
        other = self.flip_x(array[2:])
        pair = jnp.stack([array[:2], other])
        pair = jnp.where(self.x == 0, pair, pair[::-1])
        back = self.flip_core(pair[:, 1])
        rows = jnp.stack([pair[:, 0], back])
        rows = jnp.where(self.core == 0, rows, rows[::-1])
        return jnp.swapaxes(rows, 0, 1).reshape((4,) + array.shape[1:])

    def step(self, at, keep, send, deps=()):
        got = self.swap(send, *self.steps[at])
        if at < self.bits:
            return add_split(at + 2, self.scalars, keep, got, deps)
        return (keep.astype(F32) + got.astype(F32)).astype(BF)[0]

    def gather(self, chunk):
        got = self.flip_x(chunk)
        pair = jnp.where(self.x == 0, jnp.stack([chunk, got]), jnp.stack([got, chunk]))
        got = self.flip_core(pair)
        four = jnp.where(self.core == 0, jnp.stack([pair, got]), jnp.stack([got, pair]))
        return four.reshape((4,) + chunk.shape)


def local(
    dp,
    tokens,
    seg_ids,
    text_len,
    out_grad,
    pooled_grad,
    w_query,
    b_query,
    w_key,
    w_value,
    b_value,
    w_out,
    b_out,
    attn_gain,
    attn_shift,
    w_up,
    b_up,
    w_down,
    b_down,
    ffn_gain,
    ffn_shift,
):
    rows_dev, local_len, width = tokens.shape
    row_len = seg_ids.shape[1]
    links = Links(dp)
    sc = links.scalars
    seq = lax.axis_index("seq")
    wide = w_up.shape[1]
    part = width // dp

    blocks = pick(seg_ids, seq).reshape(4, local_len)
    ids = jnp.stack([pick(blocks, seq ^ k) for k in range(4)]).reshape(row_len)
    lens = jnp.concatenate([pick(text_len, seq), jnp.ones((4,), jnp.int32)]).astype(F32)[:, None]
    pg = jnp.pad(pick(pooled_grad, seq), ((0, 4), (0, 0))).astype(F32)
    par = jnp.concatenate(
        [
            jnp.stack([b_query, b_value, b_out, attn_gain, attn_shift, b_down, ffn_gain, ffn_shift]),
            b_up.reshape(4, width),
            jnp.zeros((4, width), BF),
        ]
    ).astype(F32)

    x = links.to_rows(tokens).reshape(row_len, width)
    og = links.to_rows(out_grad).reshape(row_len, width)

    a, qkv, probs = attn_fwd(x, ids[None, :], ids[:, None], par, w_query, w_key, w_value)
    a2 = links.flip_core(a)
    keep1, send1, dg, after, na, sa, ghf, lay, pool, cols_f = ffn(
        part, sc, a, par, w_out, w_up, w_down, og, ids[None, :], pg, lens
    )
    got1 = links.flip_core(send1)
    gu, send2 = grad_up(sc, keep1, w_down, dg, after, ())
    got2 = links.flip_core(send2)
    last = links.bits
    *down, row_d = grad_down(dp, sc, keep1, got1, width, (gu,))
    *up, row_u = grad_w_up(dp, sc, after, gu, got2, width, (row_d,))
    gha, gb, gm, rows4 = middle(sc, gu, send2, w_up, w_out, na, sa, ghf, par, cols_f, (row_u,))
    down = links.step(0, *down, (rows4,))
    d1, ak1, as1 = attn_bwd(0, sc, qkv, probs, a, gm, gb, (down[0],))
    ag1 = links.flip_core(as1)
    up = links.step(0, *up, (d1,))
    d2, ak2, as2 = attn_bwd(1, sc, qkv, probs, a, gm, gb, (up[0],))
    ag2 = links.flip_core(as2)
    down = links.step(1, *down, (d2,))
    *t1, row1 = attn_w(part, sc, a, a2, ak1, ag1, (), (down[0],))
    up = links.step(1, *up, (row1,))
    t2 = attn_w(part, sc, a, a2, ak2, ag2, (row1, rows4, row_d, row_u), (up[0],))
    for at in range(2, last):
        down = links.step(at, *down, (t2[0],))
    t1 = links.step(0, *t1, (down[0],))
    gx = grad_tokens_rows(gha, d1, d2, w_query, w_key, w_value, (t1[0],))
    tail = gx
    for at in range(2, last):
        up = links.step(at, *up, (tail,))
        tail = up[0]
    t2 = links.step(0, *t2, (tail,))
    tail = t2[0]
    for at in range(1, last):
        t1 = links.step(at, *t1, (tail,))
        t2 = links.step(at, *t2, (t1[0],))
        tail = t2[0]
    down, up = links.step(last, *down), links.step(last, *up)
    t1, t2 = links.step(last, *t1), links.step(last, *t2)

    ffn_all = links.gather(jnp.stack([down, up]))
    pool_rows = jnp.pad(pool[:SEGS].astype(BF).reshape(2 * SEGS, width // 2), ((0, 8), (0, 0)))
    attn_all = links.gather(jnp.concatenate([t1, t2, pool_rows], 0))
    out_down = ffn_all[:, 0].reshape(4 * part, width).astype(F32)
    out_up = ffn_all[:, 1].transpose(1, 0, 2).reshape(part, wide).astype(F32)
    square = jnp.concatenate([attn_all[:, :part], attn_all[:, part : 2 * part]], 2).astype(F32)
    small = attn_all[0::2, 2 * part : 2 * part + PAD, :part].astype(F32)
    pooled = attn_all[:, 2 * part + PAD : 2 * part + PAD + 2 * SEGS].reshape(2, 2, SEGS, width)
    pooled_all = pooled.transpose(1, 0, 2, 3).reshape(4, SEGS, width).astype(F32)
    vec = small[0] + small[1]

    layer_back = links.to_blocks(lay.reshape(4, local_len, width)).astype(F32)
    grad_tokens = links.to_blocks(gx.reshape(4, local_len, width)).astype(F32)
    return (
        layer_back,
        pooled_all,
        grad_tokens,
        square[0],
        vec[0],
        square[1],
        square[2],
        vec[1],
        square[3],
        vec[2],
        vec[3],
        vec[4],
        out_up,
        vec[8:12].reshape(4 * part),
        out_down,
        vec[5],
        vec[6],
        vec[7],
    )


def solution(mesh):
    rows, cols = P("dp", None), P("dp")
    blocks = P("dp", "seq", None)
    return jax.shard_map(
        partial(local, mesh.shape["dp"]),
        mesh=mesh,
        in_specs=(blocks, rows, rows, blocks, P("dp", None, None)) + (P(),) * 15,
        out_specs=(
            blocks,
            P("dp", None, None),
            blocks,
            rows,
            cols,
            rows,
            rows,
            cols,
            rows,
            cols,
            cols,
            cols,
            rows,
            cols,
            rows,
            cols,
            cols,
            cols,
        ),
        check_vma=False,
    )
```

```python
from functools import partial

import jax
import jax.numpy as jnp
from jax import lax
from jax.experimental import pallas as pl
from jax.experimental.pallas import tpu as pltpu
from jax.sharding import PartitionSpec as P

HEAD = 64
SEGS = 4
EPS = 1e-12
PAD = 16
TILE = 384
BF = jnp.bfloat16
F32 = jnp.float32
AXES = ("dp", "seq")
VM = pl.BlockSpec(memory_space=pltpu.VMEM)
SM = pl.BlockSpec(memory_space=pltpu.SMEM)
ANY = pl.BlockSpec(memory_space=pl.ANY)


def dot(a, b, da, db):
    return lax.dot_general(a, b, (((da,), (db,)), ((), ())), preferred_element_type=F32)


def nn(a, b):
    return dot(a, b, 1, 0)


def tn(a, b):
    return dot(a, b, 0, 0)


def nt(a, b):
    return dot(a, b, 1, 1)


def shape(dims, kind=BF):
    return jax.ShapeDtypeStruct(dims, kind)


def call(name, kernel, args, outs, flops, scalars=None, deps=(), scratch=(), vmem=16):
    n, head = len(args), int(scalars is not None)
    nbytes = sum(a.size * a.dtype.itemsize for a in args) + sum(o.size * o.dtype.itemsize for o in outs)

    def body(*refs):
        kernel(*refs[: n + head], *refs[n + head + len(deps) :])

    return pl.pallas_call(
        body,
        out_shape=list(outs),
        in_specs=[SM] * head + [VM] * n + [ANY] * len(deps),
        out_specs=[VM] * len(outs),
        scratch_shapes=list(scratch),
        name=name,
        cost_estimate=pl.CostEstimate(flops=int(flops), bytes_accessed=int(nbytes), transcendentals=0),
        compiler_params=pltpu.CompilerParams(vmem_limit_bytes=vmem * 2**20),
    )(*([scalars] if head else []), *args, *deps)


def reverse(number, bits):
    return sum(((number >> i) & 1) << (bits - 1 - i) for i in range(bits))


def attn_fwd_kernel(xa, xb, ids, par, wq, wk, wv, a_o, qkv_o, e_o, inv_o):
    width, rows = a_o.shape[1] - PAD, a_o.shape[2]
    heads = width // HEAD
    cols = par[...].T
    half = xa.shape[0]
    a_o[0, :width, :half] = xa[...].T
    text = lax.broadcasted_iota(jnp.int32, (PAD, rows), 0)
    same = jnp.where(ids[...] == text, 1.0, 0.0)
    ones = jnp.ones((PAD, rows), BF)
    for i, pad in enumerate((((1.0 - same) * -1e30).astype(BF), same.astype(BF), ones)):
        for h in range(heads):
            qkv_o[i, h, HEAD:] = pad
    a_o[0, width:] = ones
    a_o[1, width:] = ones
    a_o[0, :width, half:] = xb[...].T
    xt = a_o[0, :width]
    for i, w in enumerate((wq, wk, wv)):
        out = tn(w[...], xt)
        if i == 0:
            out = (out + cols[:, 0:1]).astype(BF) * BF(0.125)
        elif i == 2:
            out = out + cols[:, 1:2]
        qkv_o[i, :, :HEAD] = out.astype(BF).reshape(heads, HEAD, rows)
    for h in range(heads):
        s = tn(qkv_o[1, h], qkv_o[0, h])
        e = jnp.exp(s - jnp.max(s, axis=0, keepdims=True)).astype(BF)
        e_o[h] = e
        out = nn(qkv_o[2, h], e)
        inv = 1.0 / out[HEAD : HEAD + 1]
        inv_o[h : h + 1] = inv
        a_o[1, h * HEAD : (h + 1) * HEAD] = (out[:HEAD] * inv).astype(BF)


def attn_fwd(xa, xb, ids, par, wq, wk, wv):
    width = wq.shape[0]
    rows = xa.shape[0] + xb.shape[0]
    heads = width // HEAD
    return call(
        "attn_fwd",
        attn_fwd_kernel,
        (xa, xb, ids, par, wq, wk, wv),
        (
            shape((2, width + PAD, rows)),
            shape((3, heads, HEAD + PAD, rows)),
            shape((heads, rows, rows)),
            shape((heads, rows), F32),
        ),
        6 * rows * width * width + 4 * rows * rows * width * 4,
    )


def norm_cols(h):
    centre = h - jnp.mean(h, axis=0, keepdims=True)
    scale = lax.rsqrt(jnp.mean(centre * centre, axis=0, keepdims=True) + EPS)
    return centre * scale, scale


def norm_cols_back(grad, normed, scale):
    return scale * (
        grad
        - jnp.mean(grad, axis=0, keepdims=True)
        - normed * jnp.mean(grad * normed, axis=0, keepdims=True)
    )


def gelu_both(u):
    phi = 0.5 * lax.erf(u * 0.7071067811865476) + 0.5
    return u * phi, phi + u * (jnp.exp(u * u * -0.5) * 0.3989422804014327)


def split_two(value):
    high = value.astype(BF)
    return high, (value - high.astype(F32)).astype(BF)


def ffn_kernel(
    part, sc, a, par, w_out, w_up, w_down, oga, ogb, ids, pg, lens,
    keep_o, send_o, dg_o, after_o, na_o, sa_o, ghf_o, lay_o, pool_o, cols_o, acc,
):
    width, wide = w_up.shape
    rows = a.shape[2]
    first = sc[0] == 0
    cols = par[...].T
    normed_a, scale_a = norm_cols(
        a[0, :width].astype(F32) + (tn(w_out[...], a[1, :width]) + cols[:, 2:3])
    )
    na_o[...] = normed_a
    sa_o[...] = scale_a
    after = normed_a * cols[:, 3:4] + cols[:, 4:5]
    after_o[:width] = after.astype(BF)
    after_o[width:] = jnp.ones((PAD, rows), BF)
    acc[...] = after + cols[:, 5:6]
    pair = 2 * part
    tiles = wide // TILE
    for i in range(tiles):
        at = slice(i * TILE, (i + 1) * TILE)
        lane, row = divmod(i * TILE, width)
        up = tn(w_up[:, at], after_o[:width]) + cols[row : row + TILE, 8 + lane : 9 + lane]
        hid, slope = gelu_both(up)
        dg_o[at] = slope.astype(BF)
        acc[...] += tn(w_down[at], hid.astype(BF))
        hid = hid.reshape(TILE // (2 * pair), 2, pair, rows)
        zero, one = hid[:, 0].reshape(TILE // 2, rows), hid[:, 1].reshape(TILE // 2, rows)
        half = slice(width + i * TILE // 2, width + (i + 1) * TILE // 2)
        keep_o[half] = jnp.where(first, zero, one).astype(BF)
        send_o[half] = jnp.where(first, one, zero).astype(BF)
    normed_f, scale_f = norm_cols(acc[...])
    layer = normed_f * cols[:, 6:7] + cols[:, 7:8]
    high, low = split_two(layer)
    lay_o[...] = high.T
    text = lax.broadcasted_iota(jnp.int32, (8, rows), 0) + 1
    select = jnp.where(ids[...] == text, 1.0, 0.0).astype(BF)
    pool_o[...] = (nt(select, high) + nt(select, low)) / lens[...]
    high, low = split_two(pg[...] / lens[...])
    half = oga.shape[0]
    grad_out = jnp.concatenate([oga[...].T, ogb[...].T], axis=1).astype(F32) + (
        tn(high, select) + tn(low, select)
    )
    ghf = norm_cols_back(grad_out * cols[:, 6:7], normed_f, scale_f)
    ghf_b = ghf.astype(BF)
    keep_o[:width] = ghf_b
    send_o[:width] = ghf_b
    ghf_o[...] = ghf
    cols_o[:, 0:1] = jnp.sum(grad_out * normed_f, axis=1, keepdims=True)
    cols_o[:, 1:2] = jnp.sum(grad_out, axis=1, keepdims=True)


def ffn(part, sc, a, par, w_out, w_up, w_down, oga, ogb, ids, pg, lens):
    width, wide = w_up.shape
    rows = a.shape[2]
    tall = wide // 2 + width
    return call(
        "ffn",
        partial(ffn_kernel, part),
        (a, par, w_out, w_up, w_down, oga, ogb, ids, pg, lens),
        (
            shape((tall, rows)),
            shape((tall, rows)),
            shape((wide, rows)),
            shape((width + PAD, rows)),
            shape((width, rows), F32),
            shape((1, rows), F32),
            shape((width, rows), F32),
            shape((rows, width)),
            shape((8, width), F32),
            shape((width, 8), F32),
        ),
        rows * width * (2 * width + 4 * wide) * 2,
        scalars=sc,
        scratch=[pltpu.VMEM((width, rows), F32)],
    )


def grad_up_kernel(sc, grad, w_down, dg, after, gu_o, send_o):
    wide, width = w_down.shape
    half = wide // 2
    send_o[:width] = after[:width]
    g = grad[:width]
    tiles = half // TILE
    for c in range(2):
        which = sc[0] if c else 1 - sc[0]
        for k in range(tiles):
            at = pl.ds(pl.multiple_of(which * half + k * TILE, TILE), TILE)
            value = (nn(w_down[at], g) * dg[at].astype(F32)).astype(BF)
            if c == 0:
                send_o[width + k * TILE : width + (k + 1) * TILE] = value
            else:
                gu_o[k * TILE : (k + 1) * TILE] = value


def grad_up(sc, keep, w_down, dg, after, deps):
    wide, width = w_down.shape
    rows = keep.shape[1]
    half = wide // 2
    return call(
        "grad_up",
        grad_up_kernel,
        (keep, w_down, dg, after),
        (shape((half, rows)), shape((half + width, rows))),
        2 * rows * width * wide,
        scalars=sc,
        deps=deps,
    )


def deal(sc, res, keep_o, send_o):
    dp = keep_o.shape[0]
    bits = dp.bit_length() - 1
    for out, hi in ((send_o, 1 - sc[1]), (keep_o, sc[1])):
        for lo in range(dp):
            out[lo] = res[
                jnp.where(
                    sc[0] == 0,
                    hi * dp + reverse(lo, bits),
                    (lo % 2) * dp + hi + reverse(lo // 2, bits),
                )
            ]


def deal_scratch(dp, tall, wide):
    return [pltpu.VMEM((2 * dp, tall, wide), BF)]


def down_kernel(part, sc, mine, other, keep_o, send_o, row_o, res):
    dp = res.shape[0] // 2
    width = dp * part
    half = 2 * width
    rows = mine.shape[1]
    grad, grad2 = mine[:width], other[:width]
    row_o[...] = nt(jnp.ones((8, rows), BF), grad)
    for k in range(half // TILE):
        at = slice(width + k * TILE, width + (k + 1) * TILE)
        value = nt(mine[at], grad) + nt(other[at], grad2)
        for i in range(TILE // part):
            j, x = divmod(k * TILE // part + i, 2)
            res[x * dp + j] = value[i * part : (i + 1) * part].astype(BF)
    deal(sc, res, keep_o, send_o)


def grad_down(dp, sc, mine, other, width, deps):
    part = width // dp
    rows = mine.shape[1]
    piece = shape((dp, part, width))
    return call(
        "grad_down",
        partial(down_kernel, part),
        (mine, other),
        (piece, piece, shape((8, width), F32)),
        8 * rows * width * dp * part * 2,
        scalars=sc,
        deps=deps,
        scratch=deal_scratch(dp, part, width),
    )


def up_kernel(part, sc, after, gu, other, keep_o, send_o, row_o, res):
    dp = res.shape[0] // 2
    width = dp * part
    rows = gu.shape[1]
    ones = jnp.ones((8, rows), BF)
    for x in range(2):
        mine = gu[x * width : (x + 1) * width]
        theirs = other[(1 + x) * width : (2 + x) * width]
        for k in range(width // TILE):
            at = slice(k * TILE, (k + 1) * TILE)
            value = nt(after[at], mine) + nt(other[at], theirs)
            for i in range(TILE // part):
                res[x * dp + k * TILE // part + i] = value[i * part : (i + 1) * part].astype(BF)
        row_o[x] = nt(ones, mine) + nt(ones, theirs)
    deal(sc, res, keep_o, send_o)


def grad_w_up(dp, sc, after, gu, other, width, deps):
    part = width // dp
    rows = gu.shape[1]
    piece = shape((dp, part, width))
    return call(
        "grad_w_up",
        partial(up_kernel, part),
        (after, gu, other),
        (piece, piece, shape((2, 8, width), F32)),
        8 * rows * width * width * 2,
        scalars=sc,
        deps=deps,
        scratch=deal_scratch(dp, part, width),
    )


def middle_kernel(sc, gu, send, w_up, w_out, na, sa, ghf, par, cols_f, gha_o, gb_o, gm_o, rows_o):
    half = gu.shape[0]
    width = w_out.shape[0]
    core = sc[0]
    cols = par[...].T
    at = pl.ds(pl.multiple_of(core * half, half), half)
    to = pl.ds(pl.multiple_of((1 - core) * half, half), half)
    grad = nn(w_up[:, at], gu[...]) + nn(w_up[:, to], send[width:])
    grad = grad + ghf[...]
    normed = na[...]
    gha = norm_cols_back(grad * cols[:, 3:4], normed, sa[...])
    gb = gha.astype(BF)
    gb_o[...] = gb
    gha_o[...] = gha
    gm_o[...] = nn(w_out[...], gb).astype(BF)
    four = jnp.concatenate(
        [
            jnp.sum(grad * normed, axis=1, keepdims=True),
            jnp.sum(grad, axis=1, keepdims=True),
            cols_f[:, 0:2],
            jnp.zeros((width, 124), F32),
        ],
        axis=1,
    )
    rows_o[...] = four.T[:8]


def middle(sc, gu, send, w_up, w_out, na, sa, ghf, par, cols_f, deps):
    width, rows = na.shape
    return call(
        "middle",
        middle_kernel,
        (gu, send, w_up, w_out, na, sa, ghf, par, cols_f),
        (shape((width, rows), F32), shape((width, rows)), shape((width, rows)), shape((8, width), F32)),
        2 * rows * width * (w_up.shape[1] + width),
        scalars=sc,
        deps=deps,
    )


def attn_bwd_kernel(base, sc, gm, gb, inv, a, qkv, e, d_o, keep_o, send_o, g_all):
    first = sc[0] == 0
    heads = e.shape[0] // 2
    rows = gm.shape[1]
    zero = jnp.zeros((PAD - 3, rows), BF)
    for i in range(heads):
        h = base * heads + i
        at = slice(h * HEAD, (h + 1) * HEAD)
        out = slice(i * HEAD, (i + 1) * HEAD)
        grad = (gm[at].astype(F32) * inv[h : h + 1]).astype(BF)
        inner = -jnp.sum(a[1, at].astype(F32) * grad.astype(F32), axis=0, keepdims=True)
        high, low = split_two(inner)
        mid, low = split_two(inner - high.astype(F32))
        g_all[i, :HEAD] = grad
        g_all[i, HEAD:] = jnp.concatenate([high, mid, low, zero], axis=0)
        probs = e[h]
        diff = tn(qkv[2, h], g_all[i])
        gs = (probs.astype(F32) * diff).astype(BF)
        gq = (nn(qkv[1, h, :HEAD], gs) * 0.125).astype(BF)
        gk = nt(qkv[0, h, :HEAD], gs).astype(BF)
        gv = nt(g_all[i, :HEAD], probs).astype(BF)
        d_o[0, out] = gq
        d_o[1, out] = gk
        d_o[2, out] = gv
        last = gb[at]
        keep_o[0, out] = jnp.where(first, gq, gv)
        keep_o[1, out] = jnp.where(first, gk, last)
        send_o[0, out] = jnp.where(first, gv, gq)
        send_o[1, out] = jnp.where(first, last, gk)


def attn_bwd(base, sc, qkv, e, inv, a, gm, gb, deps):
    heads, rows = inv.shape
    width = gm.shape[0]
    half = width // 2
    return call(
        "attn_bwd",
        partial(attn_bwd_kernel, base),
        (gm, gb, inv, a, qkv, e),
        (shape((3, half, rows)), shape((2, half, rows)), shape((2, half, rows))),
        2 * rows * rows * half * 4 * 4,
        scalars=sc,
        deps=deps,
        scratch=[pltpu.VMEM((heads // 2, HEAD + PAD, rows), BF)],
    )


def attn_w_products(part, sc, a, a2, mine, other, res):
    core = sc[0]
    dp = res.shape[0] // 2
    width = dp * part
    ones = jnp.ones((8, a.shape[2]), BF)
    sums = []
    for m in range(2):
        pick_a = 0 if m == 0 else core
        left, right = mine[m], other[m]
        sums.append(nt(ones, left) + nt(ones, right))
        for k in range(width // TILE):
            at = slice(k * TILE, (k + 1) * TILE)
            value = nt(a[pick_a, at], left) + nt(a2[pick_a, at], right)
            for i in range(TILE // part):
                res[m * dp + k * TILE // part + i, :part] = value[i * part : (i + 1) * part].astype(BF)
    return sums


def attn_w1_kernel(part, sc, mine, other, a, a2, keep_o, send_o, row_o, res):
    sums = attn_w_products(part, sc, a, a2, mine, other, res)
    row_o[0], row_o[1] = sums
    deal(sc, res, keep_o, send_o)


def attn_w2_kernel(
    part, sc, mine, other, a, a2, row1, rows, row_d, row_u, keep_o, send_o, res
):
    core = sc[0]
    dp = res.shape[0] // 2
    width = dp * part
    half = width // 2
    sums = attn_w_products(part, sc, a, a2, mine, other, res)
    m0 = jnp.concatenate([row1[0], sums[0]], axis=1)[0:1]
    m1 = jnp.concatenate([row1[1], sums[1]], axis=1)[0:1]
    zero = jnp.zeros_like(m0)
    first = core == 0
    vectors = jnp.concatenate(
        [
            jnp.where(first, m0, zero),
            jnp.where(first, zero, m0),
            jnp.where(first, zero, m1),
            rows[0:2],
            row_d[0:1],
            rows[2:4],
        ],
        axis=0,
    )
    for j in range(dp):
        ups = []
        for v in range(4):
            x, lane = divmod((j % (dp // 2)) * 4 * part + v * part, width)
            ups.append(row_u[x, 0:1, lane : lane + part])
        ups = jnp.concatenate(ups + [jnp.zeros((4, part), F32)], axis=0)
        ups = jnp.where(core == j // (dp // 2), ups, jnp.zeros_like(ups))
        block = jnp.concatenate([vectors[:, j * part : (j + 1) * part], ups], axis=0)
        block = jnp.concatenate([block, jnp.zeros((PAD, half - part), F32)], axis=1)
        res[j, part:] = block.astype(BF)
        res[dp + j, part:] = jnp.zeros((PAD, half), BF)
    deal(sc, res, keep_o, send_o)


def attn_w(part, sc, a, a2, mine, other, vectors=(), deps=()):
    half = mine.shape[1]
    width = 2 * half
    dp = width // part
    rows = a.shape[2]
    tall = part + (PAD if vectors else 0)
    piece = shape((dp, tall, half))
    outs = (piece, piece) if vectors else (piece, piece, shape((2, 8, half), F32))
    return call(
        "attn_w",
        partial(attn_w2_kernel if vectors else attn_w1_kernel, part),
        (mine, other, a, a2) + tuple(vectors),
        outs,
        8 * rows * width * half * 2,
        scalars=sc,
        deps=deps,
        scratch=deal_scratch(dp, tall, half),
    )


def tokens_kernel(sc, d1, d2, gha, wq, wk, wv, out):
    width, rows = gha.shape
    half = d1.shape[1]
    total = None
    for i, w in enumerate((wq, wk, wv)):
        value = nn(w[:, :half], d1[i]) + nn(w[:, half:], d2[i])
        total = value if total is None else total + value
    out[...] = (total + gha[...]).astype(BF).T


def grad_tokens_rows(sc, gha, d1, d2, wq, wk, wv, deps=()):
    width, rows = gha.shape
    return call(
        "grad_tokens",
        tokens_kernel,
        (d1, d2, gha, wq, wk, wv),
        (shape((rows, width)),),
        6 * rows * width * width,
        scalars=sc,
        deps=deps,
    )


def add_kernel(at, sc, mine, got, keep_o, send_o):
    bit = sc[at]
    for out, b in ((send_o, 1 - bit), (keep_o, bit)):
        for i in range(out.shape[0]):
            out[i] = (mine[b, i].astype(F32) + got[b, i].astype(F32)).astype(BF)


def add_split(at, sc, mine, got, deps=()):
    half = mine.shape[0] // 2
    tail = mine.shape[1:]
    mine, got = mine.reshape((2, half) + tail), got.reshape((2, half) + tail)
    piece = shape((half,) + tail)
    return call("add_split", partial(add_kernel, at), (mine, got), (piece, piece), mine.size, scalars=sc, deps=deps)


def pick(array, index):
    return lax.dynamic_index_in_dim(array, index, 0, keepdims=False)


class Links:
    def __init__(self, dp):
        self.dp = dp
        self.bits = dp.bit_length() - 1
        seq = lax.axis_index("seq")
        place = lax.axis_index("dp")
        self.core = lax.rem(seq, 2)
        self.x = lax.div(seq, 2)
        dp_bits = [lax.rem(lax.div(place, 1 << i), 2) for i in range(self.bits)]
        dp_steps = [(0, 1 << i) for i in range(self.bits)]
        self.steps = list(zip([(2, 0)] + dp_steps, dp_steps + [(2, 0)]))
        pairs = zip([self.x] + dp_bits, dp_bits + [self.x])
        my_bits = [jnp.where(self.core == 0, p, q) for p, q in pairs]
        self.scalars = jnp.stack([self.core] + my_bits).astype(jnp.int32)

    def swap(self, array, first, second):
        perm = []
        for d in range(self.dp):
            for s in range(4):
                ds, dd = second if s % 2 else first
                perm.append((d * 4 + s, (d ^ dd) * 4 + (s ^ ds)))
        return lax.ppermute(array, AXES, perm)

    def flip_core(self, array):
        return self.swap(array, (1, 0), (1, 0))

    def flip_x(self, array):
        return self.swap(array, (2, 0), (2, 0))

    def to_rows(self, array):
        a = array.reshape((2, 2) + array.shape[1:])
        a = jnp.swapaxes(a, 0, 1)
        keep, send = pick(a, self.core), pick(a, 1 - self.core)
        both = jnp.stack([keep, self.flip_core(send)], 1)
        keep, send = pick(both, self.x), pick(both, 1 - self.x)
        return [v.reshape(-1, array.shape[-1]) for v in (keep, self.flip_x(send))]

    def to_blocks(self, array):
        other = self.flip_x(array[2:])
        pair = jnp.stack([array[:2], other])
        pair = jnp.where(self.x == 0, pair, pair[::-1])
        back = self.flip_core(pair[:, 1])
        rows = jnp.stack([pair[:, 0], back])
        rows = jnp.where(self.core == 0, rows, rows[::-1])
        return jnp.swapaxes(rows, 0, 1).reshape((4,) + array.shape[1:])

    def step(self, at, keep, send, deps=()):
        got = self.swap(send, *self.steps[at])
        if at < self.bits:
            return add_split(at + 2, self.scalars, keep, got, deps)
        return (keep.astype(F32) + got.astype(F32)).astype(BF)[0]

    def gather(self, chunk):
        got = self.flip_x(chunk)
        pair = jnp.where(self.x == 0, jnp.stack([chunk, got]), jnp.stack([got, chunk]))
        got = self.flip_core(pair)
        four = jnp.where(self.core == 0, jnp.stack([pair, got]), jnp.stack([got, pair]))
        return four.reshape((4,) + chunk.shape)


def local(
    dp,
    tokens,
    seg_ids,
    text_len,
    out_grad,
    pooled_grad,
    w_query,
    b_query,
    w_key,
    w_value,
    b_value,
    w_out,
    b_out,
    attn_gain,
    attn_shift,
    w_up,
    b_up,
    w_down,
    b_down,
    ffn_gain,
    ffn_shift,
):
    rows_dev, local_len, width = tokens.shape
    row_len = seg_ids.shape[1]
    links = Links(dp)
    sc = links.scalars
    seq = lax.axis_index("seq")
    wide = w_up.shape[1]
    part = width // dp

    blocks = pick(seg_ids, seq).reshape(4, local_len)
    ids = jnp.stack([pick(blocks, seq ^ k) for k in range(4)]).reshape(row_len)
    lens = jnp.concatenate([pick(text_len, seq), jnp.ones((4,), jnp.int32)]).astype(F32)[:, None]
    pg = jnp.pad(pick(pooled_grad, seq), ((0, 4), (0, 0))).astype(F32)
    par = jnp.concatenate(
        [
            jnp.stack([b_query, b_value, b_out, attn_gain, attn_shift, b_down, ffn_gain, ffn_shift]),
            b_up.reshape(4, width),
            jnp.zeros((4, width), BF),
        ]
    ).astype(F32)

    x = links.to_rows(tokens)
    og = links.to_rows(out_grad)

    a, qkv, probs, inv = attn_fwd(*x, ids[None, :], par, w_query, w_key, w_value)
    a2 = links.flip_core(a)
    keep1, send1, dg, after, na, sa, ghf, lay, pool, cols_f = ffn(
        part, sc, a, par, w_out, w_up, w_down, *og, ids[None, :], pg, lens
    )
    got1 = links.flip_core(send1)
    gu, send2 = grad_up(sc, keep1, w_down, dg, after, ())
    got2 = links.flip_core(send2)
    last = links.bits
    *down, row_d = grad_down(dp, sc, keep1, got1, width, (gu,))
    *up, row_u = grad_w_up(dp, sc, after, gu, got2, width, (row_d,))
    gha, gb, gm, rows4 = middle(sc, gu, send2, w_up, w_out, na, sa, ghf, par, cols_f, (row_u,))
    down = links.step(0, *down, (rows4,))
    d1, ak1, as1 = attn_bwd(0, sc, qkv, probs, inv, a, gm, gb, (down[0],))
    ag1 = links.flip_core(as1)
    up = links.step(0, *up, (d1,))
    d2, ak2, as2 = attn_bwd(1, sc, qkv, probs, inv, a, gm, gb, (up[0],))
    ag2 = links.flip_core(as2)
    down = links.step(1, *down, (d2,))
    *t1, row1 = attn_w(part, sc, a, a2, ak1, ag1, (), (down[0],))
    up = links.step(1, *up, (row1,))
    t2 = attn_w(part, sc, a, a2, ak2, ag2, (row1, rows4, row_d, row_u), (up[0],))
    for at in range(2, last):
        down = links.step(at, *down, (t2[0],))
    t1 = links.step(0, *t1, (down[0],))
    (gx,) = grad_tokens_rows(sc, gha, d1, d2, w_query, w_key, w_value, (t1[0],))
    tail = gx
    for at in range(2, last):
        up = links.step(at, *up, (tail,))
        tail = up[0]
    t2 = links.step(0, *t2, (tail,))
    tail = t2[0]
    for at in range(1, last):
        t1 = links.step(at, *t1, (tail,))
        t2 = links.step(at, *t2, (t1[0],))
        tail = t2[0]
    down, up = links.step(last, *down), links.step(last, *up)
    t1, t2 = links.step(last, *t1), links.step(last, *t2)

    ffn_all = links.gather(jnp.stack([down, up]))
    pool_rows = jnp.pad(pool[:SEGS].astype(BF).reshape(2 * SEGS, width // 2), ((0, 8), (0, 0)))
    attn_all = links.gather(jnp.concatenate([t1, t2, pool_rows], 0))
    out_down = ffn_all[:, 0].reshape(4 * part, width).astype(F32)
    out_up = ffn_all[:, 1].transpose(1, 0, 2).reshape(part, wide).astype(F32)
    square = jnp.concatenate([attn_all[:, :part], attn_all[:, part : 2 * part]], 2).astype(F32)
    small = attn_all[0::2, 2 * part : 2 * part + PAD, :part].astype(F32)
    pooled = attn_all[:, 2 * part + PAD : 2 * part + PAD + 2 * SEGS].reshape(2, 2, SEGS, width)
    pooled_all = pooled.transpose(1, 0, 2, 3).reshape(4, SEGS, width).astype(F32)
    vec = small[0] + small[1]

    layer_back = links.to_blocks(lay.reshape(4, local_len, width)).astype(F32)
    grad_tokens = links.to_blocks(gx.reshape(4, local_len, width)).astype(F32)
    return (
        layer_back,
        pooled_all,
        grad_tokens,
        square[0],
        vec[0],
        square[1],
        square[2],
        vec[1],
        square[3],
        vec[2],
        vec[3],
        vec[4],
        out_up,
        vec[8:12].reshape(4 * part),
        out_down,
        vec[5],
        vec[6],
        vec[7],
    )


def solution(mesh):
    rows, cols = P("dp", None), P("dp")
    blocks = P("dp", "seq", None)
    return jax.shard_map(
        partial(local, mesh.shape["dp"]),
        mesh=mesh,
        in_specs=(blocks, rows, rows, blocks, P("dp", None, None)) + (P(),) * 15,
        out_specs=(
            blocks,
            P("dp", None, None),
            blocks,
            rows,
            cols,
            rows,
            rows,
            cols,
            rows,
            cols,
            cols,
            cols,
            rows,
            cols,
            rows,
            cols,
            cols,
            cols,
        ),
        check_vma=False,
    )
```

```python
from functools import partial

import jax
import jax.numpy as jnp
from jax import lax
from jax.experimental import pallas as pl
from jax.experimental.pallas import tpu as pltpu
from jax.sharding import PartitionSpec as P

HEAD = 64
SEGS = 4
EPS = 1e-12
PAD = 16
TILE = 384
VMEM_MIB = 12
BF = jnp.bfloat16
F32 = jnp.float32
AXES = ("dp", "seq")
VM = pl.BlockSpec(memory_space=pltpu.VMEM)
ANY = pl.BlockSpec(memory_space=pl.ANY)


def dot(a, b, da, db):
    return lax.dot_general(a, b, (((da,), (db,)), ((), ())), preferred_element_type=F32)


def nn(a, b):
    return dot(a, b, 1, 0)


def tn(a, b):
    return dot(a, b, 0, 0)


def nt(a, b):
    return dot(a, b, 1, 1)


def shape(dims, kind=BF):
    return jax.ShapeDtypeStruct(dims, kind)


def orders_of(dp):
    n = dp.bit_length()
    if n == 4:
        return (
            ((1, 0, 3, 2), (2, 1, 0, 3)),
            ((0, 1, 2, 3), (3, 0, 2, 1)),
            ((2, 1, 0, 3), (1, 2, 3, 0)),
        )
    plain = (tuple(range(n)), tuple(range(1, n)) + (0,))
    return (plain, plain, plain)


def my_place(dp, order):
    seq, place = lax.axis_index("seq"), lax.axis_index("dp")
    core, x = lax.rem(seq, 2), lax.div(seq, 2)
    bits = [x] + [lax.rem(lax.div(place, 1 << i), 2) for i in range(dp.bit_length() - 1)]
    steps = [jnp.where(core == 0, bits[p], bits[q]) for p, q in zip(*order)] if order else []
    return [core] + steps + [x]


def call(name, kernel, args, outs, dp=None, order=None, after=(), far=(), scratch=(), final=False, vmem=VMEM_MIB):
    n = len(args)
    if not final:
        outs = [pltpu.VMEM(o.shape, o.dtype) if pinned(o) else o for o in outs]
    outs = list(outs)
    args = [
        pltpu.with_memory_space_constraint(a, pltpu.HBM if i in far else pltpu.VMEM)
        if i in far or pinned(a)
        else a
        for i, a in enumerate(args)
    ]
    after = [pltpu.with_memory_space_constraint(a, pltpu.VMEM) if pinned(a) else a for a in after]

    def body(*refs):
        own = refs[:n] + refs[n + len(after) :]
        mark = own[n + len(outs)]
        mark[...] = jnp.zeros(mark.shape, mark.dtype)
        first = [my_place(dp, order)] if dp else []
        kernel(*first, *own[: n + len(outs)], *own[n + len(outs) + 1 :])

    return pl.pallas_call(
        body,
        out_shape=outs + [shape((8, 128), F32)],
        in_specs=[ANY if i in far else VM for i in range(n)] + [VM] * len(after),
        out_specs=[VM] * (len(outs) + 1),
        scratch_shapes=list(scratch),
        name=name,
        compiler_params=pltpu.CompilerParams(vmem_limit_bytes=vmem * 2**20),
    )(*args, *after)


def pinned(array):
    return array.size * array.dtype.itemsize > 2**18


def attn_fwd_kernel(
    place, x, x_x, x_c, x_d, ids, par, wq, wk, wv, a_o, qkv_o, e_o, inv_o
):
    core = place[0]
    width, rows = a_o.shape[1] - PAD, a_o.shape[2]
    heads = width // HEAD
    cols = par[...].T
    text = lax.broadcasted_iota(jnp.int32, (PAD, rows), 0)
    same = jnp.where(ids[...] == text, 1.0, 0.0)
    ones = jnp.ones((PAD, rows), BF)
    for i, pad in enumerate((((1.0 - same) * -1e30).astype(BF), same.astype(BF), ones)):
        for h in range(heads):
            qkv_o[i, h, HEAD:] = pad
    a_o[0, width:] = ones
    a_o[1, width:] = ones
    block = rows // 4
    for i, value in enumerate((x[0], x_c[0], x_x[core], x_d[0])):
        a_o[0, :width, i * block : (i + 1) * block] = value.T
    xt = a_o[0, :width]
    for i, w in enumerate((wq, wk, wv)):
        out = tn(w[...], xt)
        if i == 0:
            out = (out + cols[:, 0:1]).astype(BF) * BF(0.125)
        elif i == 2:
            out = out + cols[:, 1:2]
        qkv_o[i, :, :HEAD] = out.astype(BF).reshape(heads, HEAD, rows)
    for h in range(heads):
        s = tn(qkv_o[1, h], qkv_o[0, h])
        e = jnp.exp(s - jnp.max(s, axis=0, keepdims=True)).astype(BF)
        e_o[h] = e
        out = nn(qkv_o[2, h], e)
        inv = 1.0 / out[HEAD : HEAD + 1]
        inv_o[h : h + 1] = inv
        a_o[1, h * HEAD : (h + 1) * HEAD] = (out[:HEAD] * inv).astype(BF)


def attn_fwd(dp, x, ids, par, wq, wk, wv):
    width = wq.shape[0]
    rows = ids.shape[1]
    heads = width // HEAD
    return call(
        "attn_fwd",
        attn_fwd_kernel,
        (*x, ids, par, wq, wk, wv),
        (
            shape((2, width + PAD, rows)),
            shape((3, heads, HEAD + PAD, rows)),
            shape((heads, rows, rows)),
            shape((heads, rows), F32),
        ),
        dp=dp,
    )


def norm_cols(h):
    centre = h - jnp.mean(h, axis=0, keepdims=True)
    scale = lax.rsqrt(jnp.mean(centre * centre, axis=0, keepdims=True) + EPS)
    return centre * scale, scale


def norm_cols_back(grad, normed, scale):
    return scale * (
        grad
        - jnp.mean(grad, axis=0, keepdims=True)
        - normed * jnp.mean(grad * normed, axis=0, keepdims=True)
    )


def gelu_both(u):
    phi = 0.5 * lax.erf(u * 0.7071067811865476) + 0.5
    return u * phi, phi + u * (jnp.exp(u * u * -0.5) * 0.3989422804014327)


def split_two(value):
    high = value.astype(BF)
    return high, (value - high.astype(F32)).astype(BF)


def ffn_kernel(
    part, sc, a, par, w_out, w_up, w_down, og, og_x, og_c, og_d, ids, pg, lens,
    keep_o, send_o, dg_o, after_o, na_o, sa_o, ghf_o, near_o, far_o, pool_o, cols_o, acc,
):
    width, wide = w_up.shape
    rows = a.shape[2]
    first = sc[0] == 0
    cols = par[...].T
    normed_a, scale_a = norm_cols(
        a[0, :width].astype(F32) + (tn(w_out[...], a[1, :width]) + cols[:, 2:3])
    )
    na_o[...] = normed_a
    sa_o[...] = scale_a
    after = normed_a * cols[:, 3:4] + cols[:, 4:5]
    after_o[:width] = after.astype(BF)
    after_o[width:] = jnp.ones((PAD, rows), BF)
    acc[...] = after + cols[:, 5:6]
    pair = 2 * part
    tiles = wide // TILE
    for i in range(tiles):
        at = slice(i * TILE, (i + 1) * TILE)
        lane, row = divmod(i * TILE, width)
        up = tn(w_up[:, at], after_o[:width]) + cols[row : row + TILE, 8 + lane : 9 + lane]
        hid, slope = gelu_both(up)
        dg_o[at] = slope.astype(BF)
        acc[...] += tn(w_down[at], hid.astype(BF))
        hid = hid.reshape(TILE // (2 * pair), 2, pair, rows)
        zero, one = hid[:, 0].reshape(TILE // 2, rows), hid[:, 1].reshape(TILE // 2, rows)
        half = slice(width + i * TILE // 2, width + (i + 1) * TILE // 2)
        keep_o[half] = jnp.where(first, zero, one).astype(BF)
        send_o[half] = jnp.where(first, one, zero).astype(BF)
    normed_f, scale_f = norm_cols(acc[...])
    layer = normed_f * cols[:, 6:7] + cols[:, 7:8]
    high, low = split_two(layer)
    block = rows // 4
    for i in range(4):
        (near_o, far_o)[i // 2][i % 2] = high[:, i * block : (i + 1) * block].T
    text = lax.broadcasted_iota(jnp.int32, (8, rows), 0) + 1
    select = jnp.where(ids[...] == text, 1.0, 0.0).astype(BF)
    pool_o[...] = (nt(select, high) + nt(select, low)) / lens[...]
    high, low = split_two(pg[...] / lens[...])
    blocks = (og[0], og_c[0], og_x[sc[0]], og_d[0])
    grad_out = jnp.concatenate([v.T for v in blocks], axis=1).astype(F32) + (
        tn(high, select) + tn(low, select)
    )
    ghf = norm_cols_back(grad_out * cols[:, 6:7], normed_f, scale_f)
    ghf_b = ghf.astype(BF)
    keep_o[:width] = ghf_b
    send_o[:width] = ghf_b
    ghf_o[...] = ghf
    cols_o[:, 0:1] = jnp.sum(grad_out * normed_f, axis=1, keepdims=True)
    cols_o[:, 1:2] = jnp.sum(grad_out, axis=1, keepdims=True)


def ffn(dp, a, par, w_out, w_up, w_down, og, ids, pg, lens):
    width, wide = w_up.shape
    part = width // dp
    rows = a.shape[2]
    tall = wide // 2 + width
    return call(
        "ffn",
        partial(ffn_kernel, part),
        (a, par, w_out, w_up, w_down, *og, ids, pg, lens),
        (
            shape((tall, rows)),
            shape((tall, rows)),
            shape((wide, rows)),
            shape((width + PAD, rows)),
            shape((width, rows), F32),
            shape((1, rows), F32),
            shape((width, rows), F32),
            shape((2, rows // 4, width)),
            shape((2, rows // 4, width)),
            shape((8, width), F32),
            shape((width, 8), F32),
        ),
        dp=dp,
        scratch=[pltpu.VMEM((width, rows), F32)],
    )


def grad_up_kernel(sc, grad, w_down, dg, after, gu_o, send_o):
    wide, width = w_down.shape
    half = wide // 2
    send_o[:width] = after[:width]
    g = grad[:width]
    tiles = half // TILE
    for c in range(2):
        which = sc[0] if c else 1 - sc[0]
        for k in range(tiles):
            at = pl.ds(pl.multiple_of(which * half + k * TILE, TILE), TILE)
            value = (nn(w_down[at], g) * dg[at].astype(F32)).astype(BF)
            if c == 0:
                send_o[width + k * TILE : width + (k + 1) * TILE] = value
            else:
                gu_o[k * TILE : (k + 1) * TILE] = value


def grad_up(dp, keep, w_down, dg, aug, after):
    wide, width = w_down.shape
    rows = keep.shape[1]
    half = wide // 2
    return call(
        "grad_up",
        grad_up_kernel,
        (keep, w_down, dg, aug),
        (shape((half, rows)), shape((half + width, rows))),
        dp=dp,
        after=after,
    )


def deal(sc, order, res, keep_o, send_o):
    dp = keep_o.shape[0]
    n = dp.bit_length()
    weight = [dp] + [1 << i for i in range(n - 1)]
    for out, top in ((send_o, 1 - sc[1]), (keep_o, sc[1])):
        for low in range(dp):
            where = [
                top * weight[o[0]] + sum(((low >> (n - 1 - k)) & 1) * weight[o[k]] for k in range(1, n))
                for o in order
            ]
            out[low] = res[jnp.where(sc[0] == 0, *where)]


def deal_scratch(dp, tall, wide):
    return [pltpu.VMEM((2 * dp, tall, wide), BF)]


def down_kernel(part, order, sc, mine, other, keep_o, send_o, row_o, res):
    dp = res.shape[0] // 2
    width = dp * part
    half = 2 * width
    rows = mine.shape[1]
    grad, grad2 = mine[:width], other[:width]
    row_o[...] = nt(jnp.ones((8, rows), BF), grad)
    for k in range(half // TILE):
        at = slice(width + k * TILE, width + (k + 1) * TILE)
        value = nt(mine[at], grad) + nt(other[at], grad2)
        for i in range(TILE // part):
            j, x = divmod(k * TILE // part + i, 2)
            res[x * dp + j] = value[i * part : (i + 1) * part].astype(BF)
    deal(sc, order, res, keep_o, send_o)


def grad_down(dp, order, mine, other, width, after):
    part = width // dp
    rows = mine.shape[1]
    piece = shape((dp, part, width))
    return call(
        "grad_down",
        partial(down_kernel, part, order),
        (mine, other),
        (piece, piece, shape((8, width), F32)),
        dp=dp,
        order=order,
        after=after,
        scratch=deal_scratch(dp, part, width),
    )


def up_kernel(part, order, sc, after, gu, other, keep_o, send_o, res):
    dp = res.shape[0] // 2
    width = dp * part
    for x in range(2):
        mine = gu[x * width : (x + 1) * width]
        theirs = other[(1 + x) * width : (2 + x) * width]
        for k in range(width // TILE):
            at = slice(k * TILE, (k + 1) * TILE)
            value = nt(after[at], mine) + nt(other[at], theirs)
            for i in range(TILE // part):
                res[x * dp + k * TILE // part + i] = value[i * part : (i + 1) * part].astype(BF)
    deal(sc, order, res, keep_o, send_o)


def grad_w_up(dp, order, aug, gu, other, width, after):
    part = width // dp
    piece = shape((dp, part, width))
    return call(
        "grad_w_up",
        partial(up_kernel, part, order),
        (aug, gu, other),
        (piece, piece),
        dp=dp,
        order=order,
        after=after,
        scratch=deal_scratch(dp, part, width),
    )


def bias_up_kernel(gu, other, row_o):
    width = row_o.shape[2]
    ones = jnp.ones((8, gu.shape[1]), BF)
    for x in range(2):
        row_o[x] = nt(ones, gu[x * width : (x + 1) * width]) + nt(ones, other[(1 + x) * width : (2 + x) * width])


def bias_up(gu, other, width, after):
    return call("bias_up", bias_up_kernel, (gu, other), (shape((2, 8, width), F32),), after=after)


def middle_kernel(sc, gu, send, w_up, w_out, na, sa, ghf, par, cols_f, gha_o, gb_o, gm_o, rows_o):
    half = gu.shape[0]
    width = w_out.shape[0]
    core = sc[0]
    cols = par[...].T
    at = pl.ds(pl.multiple_of(core * half, half), half)
    to = pl.ds(pl.multiple_of((1 - core) * half, half), half)
    grad = nn(w_up[:, at], gu[...]) + nn(w_up[:, to], send[width:])
    grad = grad + ghf[...]
    normed = na[...]
    gha = norm_cols_back(grad * cols[:, 3:4], normed, sa[...])
    gb = gha.astype(BF)
    gb_o[...] = gb
    gha_o[...] = gha
    gm_o[...] = nn(w_out[...], gb).astype(BF)
    four = jnp.concatenate(
        [
            jnp.sum(grad * normed, axis=1, keepdims=True),
            jnp.sum(grad, axis=1, keepdims=True),
            cols_f[:, 0:2],
            jnp.zeros((width, 124), F32),
        ],
        axis=1,
    )
    rows_o[...] = four.T[:8]


def middle(dp, gu, send, w_up, w_out, na, sa, ghf, par, cols_f, after):
    width, rows = na.shape
    return call(
        "middle",
        middle_kernel,
        (gu, send, w_up, w_out, na, sa, ghf, par, cols_f),
        (shape((width, rows), F32), shape((width, rows)), shape((width, rows)), shape((8, width), F32)),
        dp=dp,
        after=after,
    )


def attn_bwd_kernel(sc, gm, gb, inv, a, qkv, e, d_o, keep_o, send_o, send2_o, g_all):
    first = sc[0] == 0
    heads = e.shape[0]
    rows = gm.shape[1]
    zero = jnp.zeros((PAD - 3, rows), BF)
    for h in range(heads):
        at = slice(h * HEAD, (h + 1) * HEAD)
        grad = (gm[at].astype(F32) * inv[h : h + 1]).astype(BF)
        inner = -jnp.sum(a[1, at].astype(F32) * grad.astype(F32), axis=0, keepdims=True)
        high, low = split_two(inner)
        mid, low = split_two(inner - high.astype(F32))
        g_all[h, :HEAD] = grad
        g_all[h, HEAD:] = jnp.concatenate([high, mid, low, zero], axis=0)
        probs = e[h]
        diff = tn(qkv[2, h], g_all[h])
        gs = (probs.astype(F32) * diff).astype(BF)
        gq = (nn(qkv[1, h, :HEAD], gs) * 0.125).astype(BF)
        gk = nt(qkv[0, h, :HEAD], gs).astype(BF)
        gv = nt(g_all[h, :HEAD], probs).astype(BF)
        d_o[0, at] = gq
        d_o[1, at] = gk
        d_o[2, at] = gv
        last = gb[at]
        keep_o[0, at] = jnp.where(first, gq, gv)
        keep_o[1, at] = jnp.where(first, gk, last)
        send_o[at] = jnp.where(first, gv, gq)
        send2_o[at] = jnp.where(first, last, gk)


def attn_bwd(dp, qkv, e, inv, a, gm, gb, after):
    heads, rows = inv.shape
    width = gm.shape[0]
    return call(
        "attn_bwd",
        attn_bwd_kernel,
        (gm, gb, inv, a, qkv, e),
        (shape((3, width, rows)), shape((2, width, rows)), shape((width, rows)), shape((width, rows))),
        dp=dp,
        after=after,
        scratch=[pltpu.VMEM((heads, HEAD + PAD, rows), BF)],
    )


def attn_w_kernel(part, order, sc, mine, other, other2, a, a2, rows, row_d, row_u, keep_o, send_o, res):
    core = sc[0]
    dp = keep_o.shape[0]
    width = dp * part
    ones = jnp.ones((8, a.shape[2]), BF)
    sums = []
    for m in range(2):
        pick_a = 0 if m == 0 else core
        left, right = mine[m], (other, other2)[m][...]
        sums.append((nt(ones, left) + nt(ones, right))[0:1])
        for k in range(width // TILE):
            at = slice(k * TILE, (k + 1) * TILE)
            value = nt(a[pick_a, at], left) + nt(a2[pick_a, at], right)
            for i in range(TILE // part):
                res[m * dp + k * TILE // part + i, :part] = value[i * part : (i + 1) * part].astype(BF)
    m0, m1 = sums
    zero = jnp.zeros_like(m0)
    first = core == 0
    vectors = jnp.concatenate(
        [
            jnp.where(first, m0, zero),
            jnp.where(first, zero, m0),
            jnp.where(first, zero, m1),
            rows[0:2],
            row_d[0:1],
            rows[2:4],
        ],
        axis=0,
    )
    for j in range(dp):
        ups = []
        for v in range(4):
            x, lane = divmod((j % (dp // 2)) * 4 * part + v * part, width)
            ups.append(row_u[x, 0:1, lane : lane + part])
        ups = jnp.concatenate(ups + [jnp.zeros((4, part), F32)], axis=0)
        ups = jnp.where(core == j // (dp // 2), ups, jnp.zeros_like(ups))
        block = jnp.concatenate([vectors[:, j * part : (j + 1) * part], ups], axis=0)
        block = jnp.concatenate([block, jnp.zeros((PAD, width - part), F32)], axis=1)
        res[j, part:] = block.astype(BF)
        res[dp + j, part:] = jnp.zeros((PAD, width), BF)
    deal(sc, order, res, keep_o, send_o)


def attn_w(dp, order, a, a2, mine, other, vectors, after):
    width = mine.shape[1]
    part = width // dp
    rows = a.shape[2]
    piece = shape((dp, part + PAD, width))
    return call(
        "attn_w",
        partial(attn_w_kernel, part, order),
        (mine, *other, a, a2) + tuple(vectors),
        (piece, piece),
        dp=dp,
        order=order,
        after=after,
        scratch=deal_scratch(dp, part + PAD, width),
    )


def tokens_kernel(d, gha, wq, wk, wv, near_o, far_o):
    total = nn(wq[...], d[0]) + nn(wk[...], d[1]) + nn(wv[...], d[2])
    total = (total + gha[...]).astype(BF)
    block = total.shape[1] // 4
    for i in range(4):
        (near_o, far_o)[i // 2][i % 2] = total[:, i * block : (i + 1) * block].T


def grad_tokens_rows(gha, d, wq, wk, wv, after):
    width, rows = gha.shape
    return call(
        "grad_tokens",
        tokens_kernel,
        (d, gha, wq, wk, wv),
        (shape((2, rows // 4, width)), shape((2, rows // 4, width))),
        after=after,
    )


def add_kernel(at, n, sc, *refs):
    bit = sc[at]
    mine, got, (keep_o, send_o) = refs[:n], refs[n : 2 * n], refs[2 * n :]
    for out, b in ((send_o, 1 - bit), (keep_o, bit)):
        for i in range(out.shape[0]):
            for k in range(n):
                to = (i, k) if n > 1 else i
                out[to] = (mine[k][b, i].astype(F32) + got[k][b, i].astype(F32)).astype(BF)


def add_split(dp, order, at, mine, got, after=()):
    n = len(mine)
    half = mine[0].shape[0] // 2
    tail = mine[0].shape[1:]
    args = [v.reshape((2, half) + tail) for v in (*mine, *got)]
    piece = shape((half,) + ((n,) if n > 1 else ()) + tail)
    return call("add_split", partial(add_kernel, at, n), args, (piece, piece), dp=dp, order=order, after=after)


def last_add_kernel(mine, got, *refs):
    value = (mine[0].astype(F32) + got[0].astype(F32)).astype(BF)
    if len(refs) == 1:
        refs[0][...] = value
    else:
        pool, out = refs
        tall = value.shape[0]
        out[:tall] = value
        out[tall:] = jnp.concatenate([pool[...], jnp.zeros_like(pool[...])], axis=0).astype(BF)


def last_add(mine, got, pool=None, after=()):
    dims = mine.shape[1:]
    if pool is not None:
        dims = (dims[0] + 2 * pool.shape[0],) + dims[1:]
    args = (mine, got) + (() if pool is None else (pool,))
    return call("last_add", last_add_kernel, args, (shape(dims),), after=after)


def front_kernel(place, tokens, tx_o, tc_o, t_o, sems):
    core, across = place[0], place[-1]
    starts = (2 * (1 - across), 2 * across + 1 - core, 2 * across + core)
    copies = []
    for i, (begin, out) in enumerate(zip(starts, (tx_o, tc_o, t_o))):
        copies.append(pltpu.make_async_copy(tokens.at[pl.ds(begin, out.shape[0])], out, sems.at[i]))
        copies[-1].start()
    for copy in copies:
        copy.wait()


def front(dp, tokens, after=()):
    two, one = shape((2,) + tokens.shape[1:]), shape((1,) + tokens.shape[1:])
    return call(
        "front", front_kernel, (tokens,), (two, one, one),
        dp=dp, after=after, far=(0,), scratch=[pltpu.SemaphoreType.DMA((3,))],
    )


def prep_kernel(place, *refs):
    far, (ids_o, lens_o, pg_o, par_o), near, sems = refs[:12], refs[12:16], refs[16:-1], refs[-1]
    copies = [pltpu.make_async_copy(p, q, sems.at[i]) for i, (p, q) in enumerate(zip(far, near))]
    for copy in copies:
        copy.start()
    for copy in copies:
        copy.wait()
    seg, text_len, pg, *biases = near
    own = 2 * place[-1] + place[0]
    block = ids_o.shape[1] // 4

    def chosen(index, items):
        value = items[0]
        for i in range(1, 4):
            value = jnp.where(index == i, items[i], value)
        return value

    row = chosen(own, [seg[i : i + 1] for i in range(4)])
    parts = [row[:, i * block : (i + 1) * block] for i in range(4)]
    for k in range(4):
        ids_o[:, k * block : (k + 1) * block] = chosen(own ^ k, parts)
    row = chosen(own, [text_len[i : i + 1] for i in range(4)]).astype(F32)
    at = lax.broadcasted_iota(jnp.int32, (8, SEGS), 0)
    column = jnp.where(at == lax.broadcasted_iota(jnp.int32, (8, SEGS), 1), row, 0.0)
    column = jnp.sum(column, axis=1, keepdims=True)
    lens_o[...] = jnp.where(lax.broadcasted_iota(jnp.int32, (8, 1), 0) < SEGS, column, 1.0)
    pg_o[:SEGS] = pg[own].astype(F32)
    pg_o[SEGS:] = jnp.zeros_like(pg_o[SEGS:])
    width = par_o.shape[1]
    for i, bias in enumerate(biases):
        for k in range(bias.shape[0] // width):
            par_o[i + k] = bias[k * width : (k + 1) * width].astype(F32)
    par_o[12:] = jnp.zeros_like(par_o[12:])


def prep(dp, seg, text_len, pg, biases, after):
    width = pg.shape[2]
    return call(
        "prep", prep_kernel, (seg, text_len, pg, *biases),
        (shape((1, seg.shape[1]), jnp.int32), shape((8, 1), F32), shape((8, width), F32), shape((16, width), F32)),
        dp=dp, after=after, far=tuple(range(12)),
        scratch=[pltpu.VMEM(v.shape, v.dtype) for v in (seg, text_len, pg, *biases)]
        + [pltpu.SemaphoreType.DMA((12,))],
    )


def load_kernel(*refs):
    sems, n = refs[-1], len(refs) // 2
    copies = [pltpu.make_async_copy(p, q, sems.at[i]) for i, (p, q) in enumerate(zip(refs[:n], refs[n:-1]))]
    for copy in copies:
        copy.start()
    for copy in copies:
        copy.wait()


def load(arrays, after):
    n = len(arrays)
    return call(
        "load", load_kernel, arrays, [shape(v.shape, v.dtype) for v in arrays],
        after=after, far=tuple(range(n)), scratch=[pltpu.SemaphoreType.DMA((n,))],
    )


def other_core_kernel(place, pair, out):
    out[0] = pair[1 - place[0]]


def other_core(dp, pair, after=()):
    return call("other_core", other_core_kernel, (pair,), (shape((1,) + pair.shape[1:]),), dp=dp, after=after)


def pack_kernel(at, one, two, out):
    out[0] = one[...] if at is None else one[at]
    out[1] = two[...] if at is None else two[at]


def pack(one, two, at=None, after=()):
    dims = one.shape if at is None else one.shape[1:]
    return call("pack", partial(pack_kernel, at), (one, two), (shape((2,) + dims),), after=after)


def rows_out_kernel(place, near, near_x, back, out):
    core, across = place[0], place[-1]
    out[2 * across + core] = near[0].astype(F32)
    out[2 * (1 - across) + core] = near_x[0].astype(F32)
    out[2 * across + 1 - core] = back[0].astype(F32)
    out[2 * (1 - across) + 1 - core] = back[1].astype(F32)


def finish_kernel(place, parts, own, got_x, got_c, *refs):
    outs, all_four = refs[:-1], refs[-1]
    core, across = place[0], place[-1]
    all_four[2 * core + across] = own[...]
    all_four[2 * core + 1 - across] = got_x[...]
    all_four[2 * (1 - core) + across] = got_c[0]
    all_four[2 * (1 - core) + 1 - across] = got_c[1]
    parts(all_four, *outs)


def finish_down_parts(four, down_o):
    down_o[...] = four[...].astype(F32)


def finish_up_parts(four, up_o):
    width = four.shape[2]
    for q in range(4):
        up_o[:, q * width : (q + 1) * width] = four[q].astype(F32)


def finish_attn_parts(four, q_o, k_o, v_o, o_o, vec_o, pool_o):
    part = q_o.shape[0]
    for q, out in enumerate((q_o, k_o, v_o, o_o)):
        out[...] = four[q, :part].astype(F32)
        pool_o[2 * (q % 2) + q // 2] = four[q, part + PAD : part + PAD + SEGS].astype(F32)
    vec_o[...] = four[0, part : part + PAD, :part].astype(F32) + four[2, part : part + PAD, :part].astype(F32)


def pick(array, index):
    return lax.dynamic_index_in_dim(array, index, 0, keepdims=False)


class Links:
    def __init__(self, dp):
        self.dp = dp
        self.bits = dp.bit_length() - 1
        dp_steps = [(0, 1 << i) for i in range(self.bits)]
        self.axes = [(2, 0)] + dp_steps

    def swap(self, array, first, second):
        perm = []
        for d in range(self.dp):
            for s in range(4):
                ds, dd = second if s % 2 else first
                perm.append((d * 4 + s, (d ^ dd) * 4 + (s ^ ds)))
        return lax.ppermute(array, AXES, perm)

    def flip_core(self, array):
        return self.swap(array, (1, 0), (1, 0))

    def flip_x(self, array):
        return self.swap(array, (2, 0), (2, 0))

    def send(self, order, at, array):
        return self.swap(array, *(self.axes[o[at]] for o in order))


def local(
    dp,
    tokens,
    seg_ids,
    text_len,
    out_grad,
    pooled_grad,
    w_query,
    b_query,
    w_key,
    w_value,
    b_value,
    w_out,
    b_out,
    attn_gain,
    attn_shift,
    w_up,
    b_up,
    w_down,
    b_down,
    ffn_gain,
    ffn_shift,
):
    rows_dev, local_len, width = tokens.shape
    links = Links(dp)
    wide = w_up.shape[1]
    part = width // dp

    tx, tc, t_own, mark = front(dp, tokens)
    tx, tc = links.flip_x(tx), links.flip_core(tc)
    biases = (b_query, b_value, b_out, attn_gain, attn_shift, b_down, ffn_gain, ffn_shift, b_up)
    ids, lens, pg, par, mark = prep(dp, seg_ids, text_len, pooled_grad, biases, (mark,))
    ox, oc, o_own, mark = front(dp, out_grad, (mark,))
    w_query, w_key, w_value, w_out, w_up, w_down, mark = load(
        (w_query, w_key, w_value, w_out, w_up, w_down), (mark,)
    )
    td, mark = other_core(dp, tx, (mark,))
    x = (t_own, tx, tc, links.flip_core(td))
    ox, oc, _ = lax.optimization_barrier((ox, oc, mark))
    ox, oc = links.flip_x(ox), links.flip_core(oc)
    a, qkv, probs, inv, mark = attn_fwd(dp, x, ids, par, w_query, w_key, w_value)
    a2 = links.flip_core(a)
    od, _ = other_core(dp, ox, (mark,))
    og = (o_own, ox, oc, links.flip_core(od))
    keep1, send1, dg, aug, na, sa, ghf, l_near, l_far, pool, cols_f, mark = ffn(
        dp, a, par, w_out, w_up, w_down, og, ids, pg, lens
    )
    got1 = links.flip_core(send1)
    l_x = links.flip_x(l_far)
    gu, send2, mark = grad_up(dp, keep1, w_down, dg, aug, (mark,))
    got2 = links.flip_core(send2)
    o_down, o_up, o_attn = orders_of(dp)
    groups = {}

    def begin(name, order, kept, sent):
        groups[name] = [order, 0, kept, links.send(order, 0, sent)]

    def advance(name, mark):
        order, at, kept, got = groups[name]
        kept, sent, mark = add_split(dp, order, at + 2, (kept,), (got,), (mark,))
        groups[name] = [order, at + 1, kept, links.send(order, at + 1, sent)]
        return mark

    def last(name, mark, extra=None):
        order, at, kept, got = groups[name]
        value, mark = last_add(kept, got, extra, after=(mark,))
        groups[name] = [value, links.flip_x(value)]
        return mark

    def spread(name, mark):
        own, across = groups[name]
        pair, mark = pack(own, across, after=(mark,))
        groups[name] = [own, across, links.flip_core(pair)]
        return mark

    def finish(name, parts, outs, mark):
        return call(
            "finish_" + name,
            lambda place, *refs: finish_kernel(place, parts, *refs),
            groups[name],
            outs,
            dp=dp,
            final=True,
            after=(mark,),
            scratch=[pltpu.VMEM((4,) + groups[name][0].shape, BF)],
        )

    dk, ds, row_d, mark = grad_down(dp, o_down, keep1, got1, width, (mark,))
    begin("down", o_down, dk, ds)
    gha, gb, gm, rows4, mark = middle(dp, gu, send2, w_up, w_out, na, sa, ghf, par, cols_f, (mark,))
    d, ak, send3, send4, mark = attn_bwd(dp, qkv, probs, inv, a, gm, gb, (mark,))
    got3 = links.flip_core(send3), links.flip_core(send4)
    l_pair, mark = pack(l_near, l_x, 1, (mark,))
    l_back = links.flip_core(l_pair)
    g_near, g_far, mark = grad_tokens_rows(gha, d, w_query, w_key, w_value, (mark,))
    g_x = links.flip_x(g_far)
    mark = advance("down", mark)
    row_u, mark = bias_up(gu, got2, width, (mark,))
    tk, ts, mark = attn_w(dp, o_attn, a, a2, ak, got3, (rows4, row_d, row_u), (mark,))
    begin("attn", o_attn, tk, ts)
    uk, us, mark = grad_w_up(dp, o_up, aug, gu, got2, width, (mark,))
    begin("up", o_up, uk, us)
    if links.bits == 3:
        turns = (
            "attn",
            "down",
            "rows",
            "up",
            "down",
            "lay",
            "attn",
            "up",
            "down.",
            "attn",
            "grad",
            "down:",
            "up",
            "attn.",
            "fin",
            "up.",
            "attn:",
            "up:",
        )
    else:
        turns = ("down", "attn", "up") * links.bits
        turns += ("down.", "attn.", "up.", "down:", "attn:", "up:", "rows", "lay", "grad", "fin")
    def rows_out(*args):
        *arrays, mark = args
        return call(
            "rows_out", rows_out_kernel, arrays, (shape(tokens.shape, F32),), dp=dp, final=True, after=(mark,)
        )

    done = {"down": 1, "attn": 0, "up": 0}
    for turn in turns:
        name = turn.strip(".:")
        if turn == "rows":
            g_pair, mark = pack(g_near, g_x, 1, (mark,))
            g_back = links.flip_core(g_pair)
        elif turn == "lay":
            layer_back, mark = rows_out(l_near, l_x, l_back, mark)
        elif turn == "grad":
            grad_tokens, mark = rows_out(g_near, g_x, g_back, mark)
        elif turn == "fin":
            out_down, mark = finish("down", finish_down_parts, (shape((4, part, width), F32),), mark)
        elif turn.endswith("."):
            mark = last(name, mark, pool if name == "attn" else None)
        elif turn.endswith(":"):
            mark = spread(name, mark)
        elif done[name] < links.bits:
            done[name] += 1
            mark = advance(name, mark)
    out_down = out_down.reshape(4 * part, width)
    out_up, mark = finish("up", finish_up_parts, (shape((part, wide), F32),), mark)
    square = shape((part, width), F32)
    *square, vec, pooled_all, mark = finish(
        "attn",
        finish_attn_parts,
        (square, square, square, square, shape((PAD, part), F32), shape((4, SEGS, width), F32)),
        mark,
    )
    return (
        layer_back,
        pooled_all,
        grad_tokens,
        square[0],
        vec[0],
        square[1],
        square[2],
        vec[1],
        square[3],
        vec[2],
        vec[3],
        vec[4],
        out_up,
        vec[8:12].reshape(4 * part),
        out_down,
        vec[5],
        vec[6],
        vec[7],
    )


def solution(mesh):
    rows, cols = P("dp", None), P("dp")
    blocks = P("dp", "seq", None)
    return jax.shard_map(
        partial(local, mesh.shape["dp"]),
        mesh=mesh,
        in_specs=(blocks, rows, rows, blocks, P("dp", None, None)) + (P(),) * 15,
        out_specs=(
            blocks,
            P("dp", None, None),
            blocks,
            rows,
            cols,
            rows,
            rows,
            cols,
            rows,
            cols,
            cols,
            cols,
            rows,
            cols,
            rows,
            cols,
            cols,
            cols,
        ),
        check_vma=False,
    )
```

```python
from functools import partial

import jax
import jax.numpy as jnp
from jax import lax
from jax.experimental import pallas as pl
from jax.experimental.pallas import tpu as pltpu
from jax.sharding import PartitionSpec as P

HEAD = 64
SEGS = 4
EPS = 1e-12
PAD = 16
TILE = 384
VMEM_MIB = 12
BF = jnp.bfloat16
F32 = jnp.float32
AXES = ("dp", "seq")
VM = pl.BlockSpec(memory_space=pltpu.VMEM)
ANY = pl.BlockSpec(memory_space=pl.ANY)


def dot(a, b, da, db):
    return lax.dot_general(a, b, (((da,), (db,)), ((), ())), preferred_element_type=F32)


def nn(a, b):
    return dot(a, b, 1, 0)


def tn(a, b):
    return dot(a, b, 0, 0)


def nt(a, b):
    return dot(a, b, 1, 1)


def shape(dims, kind=BF):
    return jax.ShapeDtypeStruct(dims, kind)


def orders_of(dp):
    n = dp.bit_length()
    if n == 4:
        return (
            ((2, 0, 3, 1), (1, 0, 2, 3)),
            ((0, 3, 1, 2), (1, 0, 2, 3)),
            ((1, 2, 3, 0), (2, 1, 0, 3)),
        )
    plain = (tuple(range(n)), tuple(range(1, n)) + (0,))
    return (plain, plain, plain)


def my_place(dp, order):
    seq, place = lax.axis_index("seq"), lax.axis_index("dp")
    core, x = lax.rem(seq, 2), lax.div(seq, 2)
    bits = [x] + [lax.rem(lax.div(place, 1 << i), 2) for i in range(dp.bit_length() - 1)]
    steps = [jnp.where(core == 0, bits[p], bits[q]) for p, q in zip(*order)] if order else []
    return [core] + steps + [x]


def call(name, kernel, args, outs, dp=None, order=None, after=(), far=(), scratch=(), final=False, vmem=VMEM_MIB):
    n = len(args)
    if not final:
        outs = [pltpu.VMEM(o.shape, o.dtype) if pinned(o) else o for o in outs]
    outs = list(outs)
    args = [
        pltpu.with_memory_space_constraint(a, pltpu.HBM if i in far else pltpu.VMEM)
        if i in far or pinned(a)
        else a
        for i, a in enumerate(args)
    ]
    after = [pltpu.with_memory_space_constraint(a, pltpu.VMEM) if pinned(a) else a for a in after]

    def body(*refs):
        own = refs[:n] + refs[n + len(after) :]
        mark = own[n + len(outs)]
        mark[...] = jnp.zeros(mark.shape, mark.dtype)
        first = [my_place(dp, order)] if dp else []
        kernel(*first, *own[: n + len(outs)], *own[n + len(outs) + 1 :])

    return pl.pallas_call(
        body,
        out_shape=outs + [shape((8, 128), F32)],
        in_specs=[ANY if i in far else VM for i in range(n)] + [VM] * len(after),
        out_specs=[VM] * (len(outs) + 1),
        scratch_shapes=list(scratch),
        name=name,
        compiler_params=pltpu.CompilerParams(vmem_limit_bytes=vmem * 2**20),
    )(*args, *after)


def pinned(array):
    return array.size * array.dtype.itemsize > 2**18


def attn_fwd_kernel(
    place, x, x_x, x_c, x_d, ids, par, wq, wk, wv, a_o, qkv_o, e_o, inv_o
):
    core = place[0]
    width, rows = a_o.shape[1] - PAD, a_o.shape[2]
    heads = width // HEAD
    cols = par[...].T
    text = lax.broadcasted_iota(jnp.int32, (PAD, rows), 0)
    same = jnp.where(ids[...] == text, 1.0, 0.0)
    ones = jnp.ones((PAD, rows), BF)
    for i, pad in enumerate((((1.0 - same) * -1e30).astype(BF), same.astype(BF), ones)):
        for h in range(heads):
            qkv_o[i, h, HEAD:] = pad
    a_o[0, width:] = ones
    a_o[1, width:] = ones
    block = rows // 4
    for i, value in enumerate((x[0], x_c[0], x_x[core], x_d[0])):
        a_o[0, :width, i * block : (i + 1) * block] = value.T
    xt = a_o[0, :width]
    for i, w in enumerate((wq, wk, wv)):
        out = tn(w[...], xt)
        if i == 0:
            out = (out + cols[:, 0:1]).astype(BF) * BF(0.125)
        elif i == 2:
            out = out + cols[:, 1:2]
        qkv_o[i, :, :HEAD] = out.astype(BF).reshape(heads, HEAD, rows)
    for h in range(heads):
        s = tn(qkv_o[1, h], qkv_o[0, h])
        e = jnp.exp(s - jnp.max(s, axis=0, keepdims=True)).astype(BF)
        e_o[h] = e
        out = nn(qkv_o[2, h], e)
        inv = 1.0 / out[HEAD : HEAD + 1]
        inv_o[h : h + 1] = inv
        a_o[1, h * HEAD : (h + 1) * HEAD] = (out[:HEAD] * inv).astype(BF)


def attn_fwd(dp, x, ids, par, wq, wk, wv):
    width = wq.shape[0]
    rows = ids.shape[1]
    heads = width // HEAD
    return call(
        "attn_fwd",
        attn_fwd_kernel,
        (*x, ids, par, wq, wk, wv),
        (
            shape((2, width + PAD, rows)),
            shape((3, heads, HEAD + PAD, rows)),
            shape((heads, rows, rows)),
            shape((heads, rows), F32),
        ),
        dp=dp,
    )


def norm_cols(h):
    centre = h - jnp.mean(h, axis=0, keepdims=True)
    scale = lax.rsqrt(jnp.mean(centre * centre, axis=0, keepdims=True) + EPS)
    return centre * scale, scale


def norm_cols_back(grad, normed, scale):
    return scale * (
        grad
        - jnp.mean(grad, axis=0, keepdims=True)
        - normed * jnp.mean(grad * normed, axis=0, keepdims=True)
    )


def gelu_both(u):
    phi = 0.5 * lax.erf(u * 0.7071067811865476) + 0.5
    return u * phi, phi + u * (jnp.exp(u * u * -0.5) * 0.3989422804014327)


def split_two(value):
    high = value.astype(BF)
    return high, (value - high.astype(F32)).astype(BF)


def ffn_kernel(
    part, sc, a, par, w_out, w_up, w_down, og, og_x, og_c, og_d, ids, pg, lens,
    keep_o, send_o, dg_o, after_o, na_o, sa_o, ghf_o, near_o, far_o, pool_o, cols_o, acc,
):
    width, wide = w_up.shape
    rows = a.shape[2]
    first = sc[0] == 0
    cols = par[...].T
    normed_a, scale_a = norm_cols(
        a[0, :width].astype(F32) + (tn(w_out[...], a[1, :width]) + cols[:, 2:3])
    )
    na_o[...] = normed_a
    sa_o[...] = scale_a
    after = normed_a * cols[:, 3:4] + cols[:, 4:5]
    after_o[:width] = after.astype(BF)
    after_o[width:] = jnp.ones((PAD, rows), BF)
    acc[...] = after + cols[:, 5:6]
    pair = 2 * part
    tiles = wide // TILE
    for i in range(tiles):
        at = slice(i * TILE, (i + 1) * TILE)
        lane, row = divmod(i * TILE, width)
        up = tn(w_up[:, at], after_o[:width]) + cols[row : row + TILE, 8 + lane : 9 + lane]
        hid, slope = gelu_both(up)
        dg_o[at] = slope.astype(BF)
        acc[...] += tn(w_down[at], hid.astype(BF))
        hid = hid.reshape(TILE // (2 * pair), 2, pair, rows)
        zero, one = hid[:, 0].reshape(TILE // 2, rows), hid[:, 1].reshape(TILE // 2, rows)
        half = slice(width + i * TILE // 2, width + (i + 1) * TILE // 2)
        keep_o[half] = jnp.where(first, zero, one).astype(BF)
        send_o[half] = jnp.where(first, one, zero).astype(BF)
    normed_f, scale_f = norm_cols(acc[...])
    layer = normed_f * cols[:, 6:7] + cols[:, 7:8]
    high, low = split_two(layer)
    block = rows // 4
    for i in range(4):
        (near_o, far_o)[i // 2][i % 2] = high[:, i * block : (i + 1) * block].T
    text = lax.broadcasted_iota(jnp.int32, (8, rows), 0) + 1
    select = jnp.where(ids[...] == text, 1.0, 0.0).astype(BF)
    pool_o[...] = (nt(select, high) + nt(select, low)) / lens[...]
    high, low = split_two(pg[...] / lens[...])
    blocks = (og[0], og_c[0], og_x[sc[0]], og_d[0])
    grad_out = jnp.concatenate([v.T for v in blocks], axis=1).astype(F32) + (
        tn(high, select) + tn(low, select)
    )
    ghf = norm_cols_back(grad_out * cols[:, 6:7], normed_f, scale_f)
    ghf_b = ghf.astype(BF)
    keep_o[:width] = ghf_b
    send_o[:width] = ghf_b
    ghf_o[...] = ghf
    cols_o[:, 0:1] = jnp.sum(grad_out * normed_f, axis=1, keepdims=True)
    cols_o[:, 1:2] = jnp.sum(grad_out, axis=1, keepdims=True)


def ffn(dp, a, par, w_out, w_up, w_down, og, ids, pg, lens):
    width, wide = w_up.shape
    part = width // dp
    rows = a.shape[2]
    tall = wide // 2 + width
    return call(
        "ffn",
        partial(ffn_kernel, part),
        (a, par, w_out, w_up, w_down, *og, ids, pg, lens),
        (
            shape((tall, rows)),
            shape((tall, rows)),
            shape((wide, rows)),
            shape((width + PAD, rows)),
            shape((width, rows), F32),
            shape((1, rows), F32),
            shape((width, rows), F32),
            shape((2, rows // 4, width)),
            shape((2, rows // 4, width)),
            shape((8, width), F32),
            shape((width, 8), F32),
        ),
        dp=dp,
        scratch=[pltpu.VMEM((width, rows), F32)],
    )


def grad_up_kernel(sc, grad, w_down, dg, after, gu_o, send_o):
    wide, width = w_down.shape
    half = wide // 2
    send_o[:width] = after[:width]
    g = grad[:width]
    tiles = half // TILE
    for c in range(2):
        which = sc[0] if c else 1 - sc[0]
        for k in range(tiles):
            at = pl.ds(pl.multiple_of(which * half + k * TILE, TILE), TILE)
            value = (nn(w_down[at], g) * dg[at].astype(F32)).astype(BF)
            if c == 0:
                send_o[width + k * TILE : width + (k + 1) * TILE] = value
            else:
                gu_o[k * TILE : (k + 1) * TILE] = value


def grad_up(dp, keep, w_down, dg, aug, after):
    wide, width = w_down.shape
    rows = keep.shape[1]
    half = wide // 2
    return call(
        "grad_up",
        grad_up_kernel,
        (keep, w_down, dg, aug),
        (shape((half, rows)), shape((half + width, rows))),
        dp=dp,
        after=after,
    )


def deal(sc, order, res, keep_o, send_o):
    dp = keep_o.shape[0]
    n = dp.bit_length()
    weight = [dp] + [1 << i for i in range(n - 1)]
    for out, top in ((send_o, 1 - sc[1]), (keep_o, sc[1])):
        for low in range(dp):
            where = [
                top * weight[o[0]] + sum(((low >> (n - 1 - k)) & 1) * weight[o[k]] for k in range(1, n))
                for o in order
            ]
            out[low] = res[jnp.where(sc[0] == 0, *where)]


def deal_scratch(dp, tall, wide):
    return [pltpu.VMEM((2 * dp, tall, wide), BF)]


def down_kernel(part, order, sc, mine, other, keep_o, send_o, row_o, res):
    dp = res.shape[0] // 2
    width = dp * part
    half = 2 * width
    rows = mine.shape[1]
    grad, grad2 = mine[:width], other[:width]
    row_o[...] = nt(jnp.ones((8, rows), BF), grad)
    for k in range(half // TILE):
        at = slice(width + k * TILE, width + (k + 1) * TILE)
        value = nt(mine[at], grad) + nt(other[at], grad2)
        for i in range(TILE // part):
            j, x = divmod(k * TILE // part + i, 2)
            res[x * dp + j] = value[i * part : (i + 1) * part].astype(BF)
    deal(sc, order, res, keep_o, send_o)


def grad_down(dp, order, mine, other, width, after):
    part = width // dp
    rows = mine.shape[1]
    piece = shape((dp, part, width))
    return call(
        "grad_down",
        partial(down_kernel, part, order),
        (mine, other),
        (piece, piece, shape((8, width), F32)),
        dp=dp,
        order=order,
        after=after,
        scratch=deal_scratch(dp, part, width),
    )


def up_kernel(part, order, sc, after, gu, other, keep_o, send_o, res):
    dp = res.shape[0] // 2
    width = dp * part
    for x in range(2):
        mine = gu[x * width : (x + 1) * width]
        theirs = other[(1 + x) * width : (2 + x) * width]
        for k in range(width // TILE):
            at = slice(k * TILE, (k + 1) * TILE)
            value = nt(after[at], mine) + nt(other[at], theirs)
            for i in range(TILE // part):
                res[x * dp + k * TILE // part + i] = value[i * part : (i + 1) * part].astype(BF)
    deal(sc, order, res, keep_o, send_o)


def grad_w_up(dp, order, aug, gu, other, width, after):
    part = width // dp
    piece = shape((dp, part, width))
    return call(
        "grad_w_up",
        partial(up_kernel, part, order),
        (aug, gu, other),
        (piece, piece),
        dp=dp,
        order=order,
        after=after,
        scratch=deal_scratch(dp, part, width),
    )


def bias_up_kernel(gu, other, row_o):
    width = row_o.shape[2]
    ones = jnp.ones((8, gu.shape[1]), BF)
    for x in range(2):
        row_o[x] = nt(ones, gu[x * width : (x + 1) * width]) + nt(ones, other[(1 + x) * width : (2 + x) * width])


def bias_up(gu, other, width, after):
    return call("bias_up", bias_up_kernel, (gu, other), (shape((2, 8, width), F32),), after=after)


def middle_kernel(sc, gu, send, w_up, w_out, na, sa, ghf, par, cols_f, gha_o, gb_o, gm_o, rows_o):
    half = gu.shape[0]
    width = w_out.shape[0]
    core = sc[0]
    cols = par[...].T
    at = pl.ds(pl.multiple_of(core * half, half), half)
    to = pl.ds(pl.multiple_of((1 - core) * half, half), half)
    grad = nn(w_up[:, at], gu[...]) + nn(w_up[:, to], send[width:])
    grad = grad + ghf[...]
    normed = na[...]
    gha = norm_cols_back(grad * cols[:, 3:4], normed, sa[...])
    gb = gha.astype(BF)
    gb_o[...] = gb
    gha_o[...] = gha
    gm_o[...] = nn(w_out[...], gb).astype(BF)
    four = jnp.concatenate(
        [
            jnp.sum(grad * normed, axis=1, keepdims=True),
            jnp.sum(grad, axis=1, keepdims=True),
            cols_f[:, 0:2],
            jnp.zeros((width, 124), F32),
        ],
        axis=1,
    )
    rows_o[...] = four.T[:8]


def middle(dp, gu, send, w_up, w_out, na, sa, ghf, par, cols_f, after):
    width, rows = na.shape
    return call(
        "middle",
        middle_kernel,
        (gu, send, w_up, w_out, na, sa, ghf, par, cols_f),
        (shape((width, rows), F32), shape((width, rows)), shape((width, rows)), shape((8, width), F32)),
        dp=dp,
        after=after,
    )


def attn_bwd_kernel(sc, gm, gb, inv, a, qkv, e, d_o, keep_o, send_o, send2_o, g_all):
    first = sc[0] == 0
    heads = e.shape[0]
    rows = gm.shape[1]
    zero = jnp.zeros((PAD - 3, rows), BF)
    for h in range(heads):
        at = slice(h * HEAD, (h + 1) * HEAD)
        grad = (gm[at].astype(F32) * inv[h : h + 1]).astype(BF)
        inner = -jnp.sum(a[1, at].astype(F32) * grad.astype(F32), axis=0, keepdims=True)
        high, low = split_two(inner)
        mid, low = split_two(inner - high.astype(F32))
        g_all[h, :HEAD] = grad
        g_all[h, HEAD:] = jnp.concatenate([high, mid, low, zero], axis=0)
        probs = e[h]
        diff = tn(qkv[2, h], g_all[h])
        gs = (probs.astype(F32) * diff).astype(BF)
        gq = (nn(qkv[1, h, :HEAD], gs) * 0.125).astype(BF)
        gk = nt(qkv[0, h, :HEAD], gs).astype(BF)
        gv = nt(g_all[h, :HEAD], probs).astype(BF)
        d_o[0, at] = gq
        d_o[1, at] = gk
        d_o[2, at] = gv
        last = gb[at]
        keep_o[0, at] = jnp.where(first, gq, gv)
        keep_o[1, at] = jnp.where(first, gk, last)
        send_o[at] = jnp.where(first, gv, gq)
        send2_o[at] = jnp.where(first, last, gk)


def attn_bwd(dp, qkv, e, inv, a, gm, gb, after):
    heads, rows = inv.shape
    width = gm.shape[0]
    return call(
        "attn_bwd",
        attn_bwd_kernel,
        (gm, gb, inv, a, qkv, e),
        (shape((3, width, rows)), shape((2, width, rows)), shape((width, rows)), shape((width, rows))),
        dp=dp,
        after=after,
        scratch=[pltpu.VMEM((heads, HEAD + PAD, rows), BF)],
    )


def attn_w_kernel(part, sc, mine, other, other2, a, a2, rows, row_d, row_u, res):
    core = sc[0]
    dp = res.shape[0] // 2
    width = dp * part
    ones = jnp.ones((8, a.shape[2]), BF)
    sums = []
    for m in range(2):
        pick_a = 0 if m == 0 else core
        left, right = mine[m], (other, other2)[m][...]
        sums.append((nt(ones, left) + nt(ones, right))[0:1])
        for k in range(width // TILE):
            at = slice(k * TILE, (k + 1) * TILE)
            value = nt(a[pick_a, at], left) + nt(a2[pick_a, at], right)
            for i in range(TILE // part):
                res[m * dp + k * TILE // part + i, :part] = value[i * part : (i + 1) * part].astype(BF)
    m0, m1 = sums
    zero = jnp.zeros_like(m0)
    first = core == 0
    vectors = jnp.concatenate(
        [
            jnp.where(first, m0, zero),
            jnp.where(first, zero, m0),
            jnp.where(first, zero, m1),
            rows[0:2],
            row_d[0:1],
            rows[2:4],
        ],
        axis=0,
    )
    for j in range(dp):
        ups = []
        for v in range(4):
            x, lane = divmod((j % (dp // 2)) * 4 * part + v * part, width)
            ups.append(row_u[x, 0:1, lane : lane + part])
        ups = jnp.concatenate(ups + [jnp.zeros((4, part), F32)], axis=0)
        ups = jnp.where(core == j // (dp // 2), ups, jnp.zeros_like(ups))
        block = jnp.concatenate([vectors[:, j * part : (j + 1) * part], ups], axis=0)
        block = jnp.concatenate([block, jnp.zeros((PAD, width - part), F32)], axis=1)
        res[j, part:] = block.astype(BF)
        res[dp + j, part:] = jnp.zeros((PAD, width), BF)


def attn_w(dp, a, a2, mine, other, vectors, after):
    width = mine.shape[1]
    part = width // dp
    rows = a.shape[2]
    return call(
        "attn_w",
        partial(attn_w_kernel, part),
        (mine, *other, a, a2) + tuple(vectors),
        (shape((2 * dp, part + PAD, width)),),
        dp=dp,
        after=after,
    )


def deal_kernel(order, sc, res, keep_o, send_o):
    deal(sc, order, res, keep_o, send_o)


def dealt(dp, order, res, after):
    piece = shape((dp,) + res.shape[1:])
    return call("dealt", partial(deal_kernel, order), (res,), (piece, piece), dp=dp, order=order, after=after)


def tokens_kernel(d, gha, wq, wk, wv, near_o, far_o):
    total = nn(wq[...], d[0]) + nn(wk[...], d[1]) + nn(wv[...], d[2])
    total = (total + gha[...]).astype(BF)
    block = total.shape[1] // 4
    for i in range(4):
        (near_o, far_o)[i // 2][i % 2] = total[:, i * block : (i + 1) * block].T


def grad_tokens_rows(gha, d, wq, wk, wv, after):
    width, rows = gha.shape
    return call(
        "grad_tokens",
        tokens_kernel,
        (d, gha, wq, wk, wv),
        (shape((2, rows // 4, width)), shape((2, rows // 4, width))),
        after=after,
    )


def add_kernel(at, n, sc, *refs):
    bit = sc[at]
    mine, got, (keep_o, send_o) = refs[:n], refs[n : 2 * n], refs[2 * n :]
    for out, b in ((send_o, 1 - bit), (keep_o, bit)):
        for i in range(out.shape[0]):
            for k in range(n):
                to = (i, k) if n > 1 else i
                out[to] = (mine[k][b, i].astype(F32) + got[k][b, i].astype(F32)).astype(BF)


def add_split(dp, order, at, mine, got, after=()):
    n = len(mine)
    half = mine[0].shape[0] // 2
    tail = mine[0].shape[1:]
    args = [v.reshape((2, half) + tail) for v in (*mine, *got)]
    piece = shape((half,) + ((n,) if n > 1 else ()) + tail)
    return call("add_split", partial(add_kernel, at, n), args, (piece, piece), dp=dp, order=order, after=after)


def last_add_kernel(mine, got, *refs):
    value = (mine[0].astype(F32) + got[0].astype(F32)).astype(BF)
    if len(refs) == 1:
        refs[0][...] = value
    else:
        pool, out = refs
        tall = value.shape[0]
        out[:tall] = value
        out[tall:] = jnp.concatenate([pool[...], jnp.zeros_like(pool[...])], axis=0).astype(BF)


def last_add(mine, got, pool=None, after=()):
    dims = mine.shape[1:]
    if pool is not None:
        dims = (dims[0] + 2 * pool.shape[0],) + dims[1:]
    args = (mine, got) + (() if pool is None else (pool,))
    return call("last_add", last_add_kernel, args, (shape(dims),), after=after)


def front_kernel(place, tokens, tx_o, tc_o, t_o, sems):
    core, across = place[0], place[-1]
    starts = (2 * (1 - across), 2 * across + 1 - core, 2 * across + core)
    copies = []
    for i, (begin, out) in enumerate(zip(starts, (tx_o, tc_o, t_o))):
        copies.append(pltpu.make_async_copy(tokens.at[pl.ds(begin, out.shape[0])], out, sems.at[i]))
        copies[-1].start()
    for copy in copies:
        copy.wait()


def front(dp, tokens, after=()):
    two, one = shape((2,) + tokens.shape[1:]), shape((1,) + tokens.shape[1:])
    return call(
        "front", front_kernel, (tokens,), (two, one, one),
        dp=dp, after=after, far=(0,), scratch=[pltpu.SemaphoreType.DMA((3,))],
    )


def prep_kernel(place, *refs):
    far, (ids_o, lens_o, pg_o, par_o), near, sems = refs[:12], refs[12:16], refs[16:-1], refs[-1]
    copies = [pltpu.make_async_copy(p, q, sems.at[i]) for i, (p, q) in enumerate(zip(far, near))]
    for copy in copies:
        copy.start()
    for copy in copies:
        copy.wait()
    seg, text_len, pg, *biases = near
    own = 2 * place[-1] + place[0]
    block = ids_o.shape[1] // 4

    def chosen(index, items):
        value = items[0]
        for i in range(1, 4):
            value = jnp.where(index == i, items[i], value)
        return value

    row = chosen(own, [seg[i : i + 1] for i in range(4)])
    parts = [row[:, i * block : (i + 1) * block] for i in range(4)]
    for k in range(4):
        ids_o[:, k * block : (k + 1) * block] = chosen(own ^ k, parts)
    row = chosen(own, [text_len[i : i + 1] for i in range(4)]).astype(F32)
    at = lax.broadcasted_iota(jnp.int32, (8, SEGS), 0)
    column = jnp.where(at == lax.broadcasted_iota(jnp.int32, (8, SEGS), 1), row, 0.0)
    column = jnp.sum(column, axis=1, keepdims=True)
    lens_o[...] = jnp.where(lax.broadcasted_iota(jnp.int32, (8, 1), 0) < SEGS, column, 1.0)
    pg_o[:SEGS] = pg[own].astype(F32)
    pg_o[SEGS:] = jnp.zeros_like(pg_o[SEGS:])
    width = par_o.shape[1]
    for i, bias in enumerate(biases):
        for k in range(bias.shape[0] // width):
            par_o[i + k] = bias[k * width : (k + 1) * width].astype(F32)
    par_o[12:] = jnp.zeros_like(par_o[12:])


def prep(dp, seg, text_len, pg, biases, after):
    width = pg.shape[2]
    return call(
        "prep", prep_kernel, (seg, text_len, pg, *biases),
        (shape((1, seg.shape[1]), jnp.int32), shape((8, 1), F32), shape((8, width), F32), shape((16, width), F32)),
        dp=dp, after=after, far=tuple(range(12)),
        scratch=[pltpu.VMEM(v.shape, v.dtype) for v in (seg, text_len, pg, *biases)]
        + [pltpu.SemaphoreType.DMA((12,))],
    )


def load_kernel(*refs):
    sems, n = refs[-1], len(refs) // 2
    copies = [pltpu.make_async_copy(p, q, sems.at[i]) for i, (p, q) in enumerate(zip(refs[:n], refs[n:-1]))]
    for copy in copies:
        copy.start()
    for copy in copies:
        copy.wait()


def load(arrays, after):
    n = len(arrays)
    return call(
        "load", load_kernel, arrays, [shape(v.shape, v.dtype) for v in arrays],
        after=after, far=tuple(range(n)), scratch=[pltpu.SemaphoreType.DMA((n,))],
    )


def other_core_kernel(place, pair, out):
    out[0] = pair[1 - place[0]]


def other_core(dp, pair, after=()):
    return call("other_core", other_core_kernel, (pair,), (shape((1,) + pair.shape[1:]),), dp=dp, after=after)


def pack_kernel(at, one, two, out):
    out[0] = one[...] if at is None else one[at]
    out[1] = two[...] if at is None else two[at]


def pack(one, two, at=None, after=()):
    dims = one.shape if at is None else one.shape[1:]
    return call("pack", partial(pack_kernel, at), (one, two), (shape((2,) + dims),), after=after)


def rows_out_kernel(place, near, near_x, back, out):
    core, across = place[0], place[-1]
    out[2 * across + core] = near[0].astype(F32)
    out[2 * (1 - across) + core] = near_x[0].astype(F32)
    out[2 * across + 1 - core] = back[0].astype(F32)
    out[2 * (1 - across) + 1 - core] = back[1].astype(F32)


def finish_kernel(place, parts, own, got_x, got_c, *refs):
    outs, all_four = refs[:-1], refs[-1]
    core, across = place[0], place[-1]
    all_four[2 * core + across] = own[...]
    all_four[2 * core + 1 - across] = got_x[...]
    all_four[2 * (1 - core) + across] = got_c[0]
    all_four[2 * (1 - core) + 1 - across] = got_c[1]
    parts(all_four, *outs)


def finish_down_parts(four, down_o):
    down_o[...] = four[...].astype(F32)


def finish_up_parts(four, up_o):
    width = four.shape[2]
    for q in range(4):
        up_o[:, q * width : (q + 1) * width] = four[q].astype(F32)


def finish_attn_parts(four, q_o, k_o, v_o, o_o, vec_o, pool_o):
    part = q_o.shape[0]
    for q, out in enumerate((q_o, k_o, v_o, o_o)):
        out[...] = four[q, :part].astype(F32)
        pool_o[2 * (q % 2) + q // 2] = four[q, part + PAD : part + PAD + SEGS].astype(F32)
    vec_o[...] = four[0, part : part + PAD, :part].astype(F32) + four[2, part : part + PAD, :part].astype(F32)


def pick(array, index):
    return lax.dynamic_index_in_dim(array, index, 0, keepdims=False)


class Links:
    def __init__(self, dp):
        self.dp = dp
        self.bits = dp.bit_length() - 1
        dp_steps = [(0, 1 << i) for i in range(self.bits)]
        self.axes = [(2, 0)] + dp_steps

    def swap(self, array, first, second):
        perm = []
        for d in range(self.dp):
            for s in range(4):
                ds, dd = second if s % 2 else first
                perm.append((d * 4 + s, (d ^ dd) * 4 + (s ^ ds)))
        return lax.ppermute(array, AXES, perm)

    def flip_core(self, array):
        return self.swap(array, (1, 0), (1, 0))

    def flip_x(self, array):
        return self.swap(array, (2, 0), (2, 0))

    def send(self, order, at, array):
        return self.swap(array, *(self.axes[o[at]] for o in order))


def local(
    dp,
    tokens,
    seg_ids,
    text_len,
    out_grad,
    pooled_grad,
    w_query,
    b_query,
    w_key,
    w_value,
    b_value,
    w_out,
    b_out,
    attn_gain,
    attn_shift,
    w_up,
    b_up,
    w_down,
    b_down,
    ffn_gain,
    ffn_shift,
):
    rows_dev, local_len, width = tokens.shape
    links = Links(dp)
    wide = w_up.shape[1]
    part = width // dp

    tx, tc, t_own, mark = front(dp, tokens)
    tx, tc = links.flip_x(tx), links.flip_core(tc)
    biases = (b_query, b_value, b_out, attn_gain, attn_shift, b_down, ffn_gain, ffn_shift, b_up)
    ids, lens, pg, par, mark = prep(dp, seg_ids, text_len, pooled_grad, biases, (mark,))
    ox, oc, o_own, mark = front(dp, out_grad, (mark,))
    w_query, w_key, w_value, w_out, w_up, w_down, mark = load(
        (w_query, w_key, w_value, w_out, w_up, w_down), (mark,)
    )
    td, mark = other_core(dp, tx, (mark,))
    x = (t_own, tx, tc, links.flip_core(td))
    ox, oc, _ = lax.optimization_barrier((ox, oc, mark))
    ox, oc = links.flip_x(ox), links.flip_core(oc)
    a, qkv, probs, inv, mark = attn_fwd(dp, x, ids, par, w_query, w_key, w_value)
    a2 = links.flip_core(a)
    od, _ = other_core(dp, ox, (mark,))
    og = (o_own, ox, oc, links.flip_core(od))
    keep1, send1, dg, aug, na, sa, ghf, l_near, l_far, pool, cols_f, mark = ffn(
        dp, a, par, w_out, w_up, w_down, og, ids, pg, lens
    )
    got1 = links.flip_core(send1)
    l_x = links.flip_x(l_far)
    gu, send2, mark = grad_up(dp, keep1, w_down, dg, aug, (mark,))
    got2 = links.flip_core(send2)
    o_down, o_up, o_attn = orders_of(dp)
    groups = {}

    def begin(name, order, kept, sent):
        groups[name] = [order, 0, kept, links.send(order, 0, sent)]

    def advance(name, mark):
        order, at, kept, got = groups[name]
        kept, sent, mark = add_split(dp, order, at + 2, (kept,), (got,), (mark,))
        groups[name] = [order, at + 1, kept, links.send(order, at + 1, sent)]
        return mark

    def last(name, mark, extra=None):
        order, at, kept, got = groups[name]
        value, mark = last_add(kept, got, extra, after=(mark,))
        groups[name] = [value, links.flip_x(value)]
        return mark

    def spread(name, mark):
        own, across = groups[name]
        pair, mark = pack(own, across, after=(mark,))
        groups[name] = [own, across, links.flip_core(pair)]
        return mark

    def finish(name, parts, outs, mark):
        return call(
            "finish_" + name,
            lambda place, *refs: finish_kernel(place, parts, *refs),
            groups[name],
            outs,
            dp=dp,
            final=True,
            after=(mark,),
            scratch=[pltpu.VMEM((4,) + groups[name][0].shape, BF)],
        )

    dk, ds, row_d, mark = grad_down(dp, o_down, keep1, got1, width, (mark,))
    begin("down", o_down, dk, ds)
    uk, us, mark = grad_w_up(dp, o_up, aug, gu, got2, width, (mark,))
    begin("up", o_up, uk, us)
    gha, gb, gm, rows4, mark = middle(dp, gu, send2, w_up, w_out, na, sa, ghf, par, cols_f, (mark,))
    d, ak, send3, send4, mark = attn_bwd(dp, qkv, probs, inv, a, gm, gb, (mark,))
    got3 = links.flip_core(send3), links.flip_core(send4)
    g_near, g_far, mark = grad_tokens_rows(gha, d, w_query, w_key, w_value, (mark,))
    g_x = links.flip_x(g_far)
    row_u, mark = bias_up(gu, got2, width, (mark,))
    products, mark = attn_w(dp, a, a2, ak, got3, (rows4, row_d, row_u), (mark,))
    mark = advance("down", mark)
    mark = advance("up", mark)
    tk, ts, mark = dealt(dp, o_attn, products, (mark,))
    begin("attn", o_attn, tk, ts)
    if links.bits == 3:
        turns = (
            "attn",
            "rows",
            "down",
            "up",
            "grad",
            "attn",
            "down",
            "up",
            "lay",
            "attn",
            "down.",
            "layer",
            "up.",
            "attn.",
            "down:",
            "up:",
            "attn:",
            "fin",
        )
    else:
        turns = ("down", "attn", "up") * links.bits
        turns += ("down.", "attn.", "up.", "down:", "attn:", "up:", "rows", "lay", "layer", "grad", "fin")
    def rows_out(*args):
        *arrays, mark = args
        return call(
            "rows_out", rows_out_kernel, arrays, (shape(tokens.shape, F32),), dp=dp, final=True, after=(mark,)
        )

    done = {"down": 1, "attn": 0, "up": 1}
    for turn in turns:
        name = turn.strip(".:")
        if turn == "rows":
            g_pair, mark = pack(g_near, g_x, 1, (mark,))
            g_back = links.flip_core(g_pair)
        elif turn == "lay":
            l_pair, mark = pack(l_near, l_x, 1, (mark,))
            l_back = links.flip_core(l_pair)
        elif turn == "layer":
            layer_back, mark = rows_out(l_near, l_x, l_back, mark)
        elif turn == "grad":
            grad_tokens, mark = rows_out(g_near, g_x, g_back, mark)
        elif turn == "fin":
            out_down, mark = finish("down", finish_down_parts, (shape((4, part, width), F32),), mark)
        elif turn.endswith("."):
            mark = last(name, mark, pool if name == "attn" else None)
        elif turn.endswith(":"):
            mark = spread(name, mark)
        elif done[name] < links.bits:
            done[name] += 1
            mark = advance(name, mark)
    out_down = out_down.reshape(4 * part, width)
    out_up, mark = finish("up", finish_up_parts, (shape((part, wide), F32),), mark)
    square = shape((part, width), F32)
    *square, vec, pooled_all, mark = finish(
        "attn",
        finish_attn_parts,
        (square, square, square, square, shape((PAD, part), F32), shape((4, SEGS, width), F32)),
        mark,
    )
    return (
        layer_back,
        pooled_all,
        grad_tokens,
        square[0],
        vec[0],
        square[1],
        square[2],
        vec[1],
        square[3],
        vec[2],
        vec[3],
        vec[4],
        out_up,
        vec[8:12].reshape(4 * part),
        out_down,
        vec[5],
        vec[6],
        vec[7],
    )


def solution(mesh):
    rows, cols = P("dp", None), P("dp")
    blocks = P("dp", "seq", None)
    return jax.shard_map(
        partial(local, mesh.shape["dp"]),
        mesh=mesh,
        in_specs=(blocks, rows, rows, blocks, P("dp", None, None)) + (P(),) * 15,
        out_specs=(
            blocks,
            P("dp", None, None),
            blocks,
            rows,
            cols,
            rows,
            rows,
            cols,
            rows,
            cols,
            cols,
            cols,
            rows,
            cols,
            rows,
            cols,
            cols,
            cols,
        ),
        check_vma=False,
    )
```

```python
from functools import partial

import jax
import jax.numpy as jnp
from jax import lax
from jax.experimental import pallas as pl
from jax.experimental.pallas import tpu as pltpu
from jax.sharding import PartitionSpec as P

HEAD = 64
SEGS = 4
EPS = 1e-12
PAD = 16
TILE = 384
VMEM_MIB = 12
BF = jnp.bfloat16
F32 = jnp.float32
AXES = ("dp", "seq")
VM = pl.BlockSpec(memory_space=pltpu.VMEM)
ANY = pl.BlockSpec(memory_space=pl.ANY)


def dot(a, b, da, db):
    return lax.dot_general(a, b, (((da,), (db,)), ((), ())), preferred_element_type=F32)


def nn(a, b):
    return dot(a, b, 1, 0)


def tn(a, b):
    return dot(a, b, 0, 0)


def nt(a, b):
    return dot(a, b, 1, 1)


def shape(dims, kind=BF):
    return jax.ShapeDtypeStruct(dims, kind)


def orders_of(dp):
    n = dp.bit_length()
    if n == 4:
        return (
            ((2, 0, 3, 1), (1, 0, 2, 3)),
            ((0, 3, 1, 2), (1, 0, 2, 3)),
            ((1, 2, 3, 0), (2, 1, 0, 3)),
        )
    plain = (tuple(range(n)), tuple(range(1, n)) + (0,))
    return (plain, plain, plain)


def my_place(dp, order):
    seq, place = lax.axis_index("seq"), lax.axis_index("dp")
    core, x = lax.rem(seq, 2), lax.div(seq, 2)
    bits = [x] + [lax.rem(lax.div(place, 1 << i), 2) for i in range(dp.bit_length() - 1)]
    steps = [jnp.where(core == 0, bits[p], bits[q]) for p, q in zip(*order)] if order else []
    return [core] + steps + [x]


def call(name, kernel, args, outs, dp=None, order=None, after=(), far=(), scratch=(), final=False, vmem=VMEM_MIB):
    n = len(args)
    if not final:
        outs = [pltpu.VMEM(o.shape, o.dtype) if pinned(o) else o for o in outs]
    outs = list(outs)
    args = [
        pltpu.with_memory_space_constraint(a, pltpu.HBM if i in far else pltpu.VMEM)
        if i in far or pinned(a)
        else a
        for i, a in enumerate(args)
    ]
    after = [pltpu.with_memory_space_constraint(a, pltpu.VMEM) if pinned(a) else a for a in after]

    def body(*refs):
        own = refs[:n] + refs[n + len(after) :]
        mark = own[n + len(outs)]
        mark[...] = jnp.zeros(mark.shape, mark.dtype)
        first = [my_place(dp, order)] if dp else []
        kernel(*first, *own[: n + len(outs)], *own[n + len(outs) + 1 :])

    return pl.pallas_call(
        body,
        out_shape=outs + [shape((8, 128), F32)],
        in_specs=[ANY if i in far else VM for i in range(n)] + [VM] * len(after),
        out_specs=[VM] * (len(outs) + 1),
        scratch_shapes=list(scratch),
        name=name,
        compiler_params=pltpu.CompilerParams(vmem_limit_bytes=vmem * 2**20),
    )(*args, *after)


def pinned(array):
    return array.size * array.dtype.itemsize > 2**18


def attn_fwd_kernel(
    place, x, x_x, x_c, x_d, ids, par, wq, wk, wv, a_o, qkv_o, e_o, inv_o
):
    width, rows = a_o.shape[1] - PAD, a_o.shape[2]
    heads = width // HEAD
    cols = par[...].T
    text = lax.broadcasted_iota(jnp.int32, (PAD, rows), 0)
    same = jnp.where(ids[...] == text, 1.0, 0.0)
    ones = jnp.ones((PAD, rows), BF)
    for i, pad in enumerate((((1.0 - same) * -1e30).astype(BF), same.astype(BF), ones)):
        for h in range(heads):
            qkv_o[i, h, HEAD:] = pad
    a_o[0, width:] = ones
    a_o[1, width:] = ones
    block = rows // 4
    for i, value in enumerate((x[0], x_c[0], x_x[0], x_d[0])):
        a_o[0, :width, i * block : (i + 1) * block] = value.T
    xt = a_o[0, :width]
    for i, w in enumerate((wq, wk, wv)):
        out = tn(w[...], xt)
        if i == 0:
            out = (out + cols[:, 0:1]).astype(BF) * BF(0.125)
        elif i == 2:
            out = out + cols[:, 1:2]
        qkv_o[i, :, :HEAD] = out.astype(BF).reshape(heads, HEAD, rows)
    for h in range(heads):
        s = tn(qkv_o[1, h], qkv_o[0, h])
        e = jnp.exp(s - jnp.max(s, axis=0, keepdims=True)).astype(BF)
        e_o[h] = e
        out = nn(qkv_o[2, h], e)
        inv = 1.0 / out[HEAD : HEAD + 1]
        inv_o[h : h + 1] = inv
        a_o[1, h * HEAD : (h + 1) * HEAD] = (out[:HEAD] * inv).astype(BF)


def attn_fwd(dp, x, ids, par, wq, wk, wv):
    width = wq.shape[0]
    rows = ids.shape[1]
    heads = width // HEAD
    return call(
        "attn_fwd",
        attn_fwd_kernel,
        (*x, ids, par, wq, wk, wv),
        (
            shape((2, width + PAD, rows)),
            shape((3, heads, HEAD + PAD, rows)),
            shape((heads, rows, rows)),
            shape((heads, rows), F32),
        ),
        dp=dp,
    )


def norm_cols(h):
    centre = h - jnp.mean(h, axis=0, keepdims=True)
    scale = lax.rsqrt(jnp.mean(centre * centre, axis=0, keepdims=True) + EPS)
    return centre * scale, scale


def norm_cols_back(grad, normed, scale):
    return scale * (
        grad
        - jnp.mean(grad, axis=0, keepdims=True)
        - normed * jnp.mean(grad * normed, axis=0, keepdims=True)
    )


def gelu_both(u):
    phi = 0.5 * lax.erf(u * 0.7071067811865476) + 0.5
    return u * phi, phi + u * (jnp.exp(u * u * -0.5) * 0.3989422804014327)


def split_two(value):
    high = value.astype(BF)
    return high, (value - high.astype(F32)).astype(BF)


def ffn_kernel(
    part, sc, a, par, w_out, w_up, w_down, og, og_x, og_c, og_d, ids, pg, lens,
    keep_o, send_o, dg_o, after_o, na_o, sa_o, ghf_o, near_o, far_o, pool_o, cols_o, acc,
):
    width, wide = w_up.shape
    rows = a.shape[2]
    first = sc[0] == 0
    cols = par[...].T
    normed_a, scale_a = norm_cols(
        a[0, :width].astype(F32) + (tn(w_out[...], a[1, :width]) + cols[:, 2:3])
    )
    na_o[...] = normed_a
    sa_o[...] = scale_a
    after = normed_a * cols[:, 3:4] + cols[:, 4:5]
    after_o[:width] = after.astype(BF)
    after_o[width:] = jnp.ones((PAD, rows), BF)
    acc[...] = after + cols[:, 5:6]
    pair = 2 * part
    tiles = wide // TILE
    for i in range(tiles):
        at = slice(i * TILE, (i + 1) * TILE)
        lane, row = divmod(i * TILE, width)
        up = tn(w_up[:, at], after_o[:width]) + cols[row : row + TILE, 8 + lane : 9 + lane]
        hid, slope = gelu_both(up)
        dg_o[at] = slope.astype(BF)
        acc[...] += tn(w_down[at], hid.astype(BF))
        hid = hid.reshape(TILE // (2 * pair), 2, pair, rows)
        zero, one = hid[:, 0].reshape(TILE // 2, rows), hid[:, 1].reshape(TILE // 2, rows)
        half = slice(width + i * TILE // 2, width + (i + 1) * TILE // 2)
        keep_o[half] = jnp.where(first, zero, one).astype(BF)
        send_o[half] = jnp.where(first, one, zero).astype(BF)
    normed_f, scale_f = norm_cols(acc[...])
    layer = normed_f * cols[:, 6:7] + cols[:, 7:8]
    high, low = split_two(layer)
    block = rows // 4
    for i in range(4):
        (near_o, far_o)[i // 2][i % 2] = high[:, i * block : (i + 1) * block].T
    text = lax.broadcasted_iota(jnp.int32, (8, rows), 0) + 1
    select = jnp.where(ids[...] == text, 1.0, 0.0).astype(BF)
    pool_o[...] = (nt(select, high) + nt(select, low)) / lens[...]
    high, low = split_two(pg[...] / lens[...])
    blocks = (og[0], og_c[0], og_x[0], og_d[0])
    grad_out = jnp.concatenate([v.T for v in blocks], axis=1).astype(F32) + (
        tn(high, select) + tn(low, select)
    )
    ghf = norm_cols_back(grad_out * cols[:, 6:7], normed_f, scale_f)
    ghf_b = ghf.astype(BF)
    keep_o[:width] = ghf_b
    send_o[:width] = ghf_b
    send_o[width + wide // 2 :] = jnp.zeros((PAD, rows), BF)
    ghf_o[...] = ghf
    cols_o[:, 0:1] = jnp.sum(grad_out * normed_f, axis=1, keepdims=True)
    cols_o[:, 1:2] = jnp.sum(grad_out, axis=1, keepdims=True)


def ffn(dp, a, par, w_out, w_up, w_down, og, ids, pg, lens):
    width, wide = w_up.shape
    part = width // dp
    rows = a.shape[2]
    tall = wide // 2 + width
    return call(
        "ffn",
        partial(ffn_kernel, part),
        (a, par, w_out, w_up, w_down, *og, ids, pg, lens),
        (
            shape((tall, rows)),
            shape((tall + PAD, rows)),
            shape((wide, rows)),
            shape((width + PAD, rows)),
            shape((width, rows), F32),
            shape((1, rows), F32),
            shape((width, rows), F32),
            shape((2, rows // 4, width)),
            shape((2, rows // 4, width)),
            shape((8, width), F32),
            shape((width, 8), F32),
        ),
        dp=dp,
        scratch=[pltpu.VMEM((width, rows), F32)],
    )


def grad_up_kernel(sc, grad, w_down, dg, after, gu_o, send_o):
    wide, width = w_down.shape
    half = wide // 2
    send_o[: width + PAD] = after[...]
    g = grad[:width]
    tiles = half // TILE
    for c in range(2):
        which = sc[0] if c else 1 - sc[0]
        for k in range(tiles):
            at = pl.ds(pl.multiple_of(which * half + k * TILE, TILE), TILE)
            value = (nn(w_down[at], g) * dg[at].astype(F32)).astype(BF)
            if c == 0:
                send_o[width + PAD + k * TILE : width + PAD + (k + 1) * TILE] = value
            else:
                gu_o[k * TILE : (k + 1) * TILE] = value


def grad_up(dp, keep, w_down, dg, aug, after):
    wide, width = w_down.shape
    rows = keep.shape[1]
    half = wide // 2
    return call(
        "grad_up",
        grad_up_kernel,
        (keep, w_down, dg, aug),
        (shape((half, rows)), shape((half + width + PAD, rows))),
        dp=dp,
        after=after,
    )


def deal(sc, order, res, keep_o, send_o):
    dp = keep_o.shape[0]
    n = dp.bit_length()
    weight = [dp] + [1 << i for i in range(n - 1)]
    for out, top in ((send_o, 1 - sc[1]), (keep_o, sc[1])):
        for low in range(dp):
            where = [
                top * weight[o[0]] + sum(((low >> (n - 1 - k)) & 1) * weight[o[k]] for k in range(1, n))
                for o in order
            ]
            out[low] = res[jnp.where(sc[0] == 0, *where)]


def deal_scratch(dp, tall, wide):
    return [pltpu.VMEM((2 * dp, tall, wide), BF)]


def down_kernel(part, order, sc, mine, other, keep_o, send_o, row_o, res):
    dp = res.shape[0] // 2
    width = dp * part
    half = 2 * width
    rows = mine.shape[1]
    grad, grad2 = mine[:width], other[:width]
    row_o[...] = nt(jnp.ones((8, rows), BF), grad)
    for k in range(half // TILE):
        at = slice(width + k * TILE, width + (k + 1) * TILE)
        value = nt(mine[at], grad) + nt(other[at], grad2)
        for i in range(TILE // part):
            j, x = divmod(k * TILE // part + i, 2)
            res[x * dp + j] = value[i * part : (i + 1) * part].astype(BF)
    deal(sc, order, res, keep_o, send_o)


def grad_down(dp, order, mine, other, width, after):
    part = width // dp
    rows = mine.shape[1]
    piece = shape((dp, part, width))
    return call(
        "grad_down",
        partial(down_kernel, part, order),
        (mine, other),
        (piece, piece, shape((8, width), F32)),
        dp=dp,
        order=order,
        after=after,
        scratch=deal_scratch(dp, part, width),
    )


def up_kernel(part, order, sc, after, gu, other, keep_o, send_o, row_o, res):
    dp = keep_o.shape[0]
    width = dp * part
    top = width + PAD
    for x in range(2):
        mine = gu[x * width : (x + 1) * width]
        theirs = other[top + x * width : top + (x + 1) * width]
        for k in range(width // TILE):
            at = slice(k * TILE, (k + 1) * TILE + (PAD if (k + 1) * TILE == width else 0))
            value = nt(after[at], mine) + nt(other[at], theirs)
            for i in range(TILE // part):
                res[x * dp + k * TILE // part + i] = value[i * part : (i + 1) * part].astype(BF)
        row_o[x] = value[TILE : TILE + 8]
    deal(sc, order, res, keep_o, send_o)


def grad_w_up(dp, order, aug, gu, other, width, after):
    part = width // dp
    piece = shape((dp, part, width))
    return call(
        "grad_w_up",
        partial(up_kernel, part, order),
        (aug, gu, other),
        (piece, piece, shape((2, 8, width), F32)),
        dp=dp,
        order=order,
        after=after,
        scratch=deal_scratch(dp, part, width),
    )


def middle_kernel(sc, gu, send, w_up, w_out, na, sa, ghf, par, cols_f, gha_o, gb_o, gm_o, rows_o):
    half = gu.shape[0]
    width = w_out.shape[0]
    core = sc[0]
    cols = par[...].T
    at = pl.ds(pl.multiple_of(core * half, half), half)
    to = pl.ds(pl.multiple_of((1 - core) * half, half), half)
    grad = nn(w_up[:, at], gu[...]) + nn(w_up[:, to], send[width + PAD :])
    grad = grad + ghf[...]
    normed = na[...]
    gha = norm_cols_back(grad * cols[:, 3:4], normed, sa[...])
    gb = gha.astype(BF)
    gb_o[...] = gb
    gha_o[...] = gha
    gm_o[...] = nn(w_out[...], gb).astype(BF)
    four = jnp.concatenate(
        [
            jnp.sum(grad * normed, axis=1, keepdims=True),
            jnp.sum(grad, axis=1, keepdims=True),
            cols_f[:, 0:2],
            jnp.zeros((width, 124), F32),
        ],
        axis=1,
    )
    rows_o[...] = four.T[:8]


def middle(dp, gu, send, w_up, w_out, na, sa, ghf, par, cols_f, after):
    width, rows = na.shape
    return call(
        "middle",
        middle_kernel,
        (gu, send, w_up, w_out, na, sa, ghf, par, cols_f),
        (shape((width, rows), F32), shape((width, rows)), shape((width, rows)), shape((8, width), F32)),
        dp=dp,
        after=after,
    )


def attn_bwd_kernel(sc, gm, gb, inv, a, qkv, e, d_o, keep_o, send_o, send2_o, g_all):
    first = sc[0] == 0
    heads = e.shape[0]
    rows = gm.shape[1]
    zero = jnp.zeros((PAD - 3, rows), BF)
    for h in range(heads):
        at = slice(h * HEAD, (h + 1) * HEAD)
        grad = (gm[at].astype(F32) * inv[h : h + 1]).astype(BF)
        inner = -jnp.sum(a[1, at].astype(F32) * grad.astype(F32), axis=0, keepdims=True)
        high, low = split_two(inner)
        mid, low = split_two(inner - high.astype(F32))
        g_all[h, :HEAD] = grad
        g_all[h, HEAD:] = jnp.concatenate([high, mid, low, zero], axis=0)
        probs = e[h]
        diff = tn(qkv[2, h], g_all[h])
        gs = (probs.astype(F32) * diff).astype(BF)
        gq = (nn(qkv[1, h, :HEAD], gs) * 0.125).astype(BF)
        gk = nt(qkv[0, h, :HEAD], gs).astype(BF)
        gv = nt(g_all[h, :HEAD], probs).astype(BF)
        d_o[0, at] = gq
        d_o[1, at] = gk
        d_o[2, at] = gv
        last = gb[at]
        keep_o[0, at] = jnp.where(first, gq, gv)
        keep_o[1, at] = jnp.where(first, gk, last)
        send_o[at] = jnp.where(first, gv, gq)
        send2_o[at] = jnp.where(first, last, gk)


def attn_bwd(dp, qkv, e, inv, a, gm, gb, after):
    heads, rows = inv.shape
    width = gm.shape[0]
    return call(
        "attn_bwd",
        attn_bwd_kernel,
        (gm, gb, inv, a, qkv, e),
        (shape((3, width, rows)), shape((2, width, rows)), shape((width, rows)), shape((width, rows))),
        dp=dp,
        after=after,
        scratch=[pltpu.VMEM((heads, HEAD + PAD, rows), BF)],
    )


def attn_w_kernel(part, sc, mine, other, other2, a, a2, rows, row_d, row_u, res):
    core = sc[0]
    dp = res.shape[0] // 2
    width = dp * part
    sums = []
    for m in range(2):
        pick_a = 0 if m == 0 else core
        left, right = mine[m], (other, other2)[m][...]
        for k in range(width // TILE):
            at = slice(k * TILE, (k + 1) * TILE + (PAD if (k + 1) * TILE == width else 0))
            value = nt(a[pick_a, at], left) + nt(a2[pick_a, at], right)
            for i in range(TILE // part):
                res[m * dp + k * TILE // part + i, :part] = value[i * part : (i + 1) * part].astype(BF)
        sums.append(value[TILE : TILE + 1])
    m0, m1 = sums
    zero = jnp.zeros_like(m0)
    first = core == 0
    vectors = jnp.concatenate(
        [
            jnp.where(first, m0, zero),
            jnp.where(first, zero, m0),
            jnp.where(first, zero, m1),
            rows[0:2],
            row_d[0:1],
            rows[2:4],
        ],
        axis=0,
    )
    for j in range(dp):
        ups = []
        for v in range(4):
            x, lane = divmod((j % (dp // 2)) * 4 * part + v * part, width)
            ups.append(row_u[x, 0:1, lane : lane + part])
        ups = jnp.concatenate(ups + [jnp.zeros((4, part), F32)], axis=0)
        ups = jnp.where(core == j // (dp // 2), ups, jnp.zeros_like(ups))
        block = jnp.concatenate([vectors[:, j * part : (j + 1) * part], ups], axis=0)
        block = jnp.concatenate([block, jnp.zeros((PAD, width - part), F32)], axis=1)
        res[j, part:] = block.astype(BF)
        res[dp + j, part:] = jnp.zeros((PAD, width), BF)


def attn_w(dp, a, a2, mine, other, vectors, after):
    width = mine.shape[1]
    part = width // dp
    rows = a.shape[2]
    return call(
        "attn_w",
        partial(attn_w_kernel, part),
        (mine, *other, a, a2) + tuple(vectors),
        (shape((2 * dp, part + PAD, width)),),
        dp=dp,
        after=after,
    )


def deal_kernel(order, sc, res, keep_o, send_o):
    deal(sc, order, res, keep_o, send_o)


def dealt(dp, order, res, after):
    piece = shape((dp,) + res.shape[1:])
    return call("dealt", partial(deal_kernel, order), (res,), (piece, piece), dp=dp, order=order, after=after)


def tokens_kernel(d, gha, wq, wk, wv, near_o, far_o):
    total = nn(wq[...], d[0]) + nn(wk[...], d[1]) + nn(wv[...], d[2])
    total = (total + gha[...]).astype(BF)
    block = total.shape[1] // 4
    for i in range(4):
        (near_o, far_o)[i // 2][i % 2] = total[:, i * block : (i + 1) * block].T


def grad_tokens_rows(gha, d, wq, wk, wv, after):
    width, rows = gha.shape
    return call(
        "grad_tokens",
        tokens_kernel,
        (d, gha, wq, wk, wv),
        (shape((2, rows // 4, width)), shape((2, rows // 4, width))),
        after=after,
    )


def add_kernel(at, n, sc, *refs):
    bit = sc[at]
    mine, got, (keep_o, send_o) = refs[:n], refs[n : 2 * n], refs[2 * n :]
    for out, b in ((send_o, 1 - bit), (keep_o, bit)):
        for i in range(out.shape[0]):
            for k in range(n):
                to = (i, k) if n > 1 else i
                out[to] = (mine[k][b, i].astype(F32) + got[k][b, i].astype(F32)).astype(BF)


def add_split(dp, order, at, mine, got, after=()):
    n = len(mine)
    half = mine[0].shape[0] // 2
    tail = mine[0].shape[1:]
    args = [v.reshape((2, half) + tail) for v in (*mine, *got)]
    piece = shape((half,) + ((n,) if n > 1 else ()) + tail)
    return call("add_split", partial(add_kernel, at, n), args, (piece, piece), dp=dp, order=order, after=after)


def last_add_kernel(mine, got, *refs):
    value = (mine[0].astype(F32) + got[0].astype(F32)).astype(BF)
    if len(refs) == 1:
        refs[0][...] = value
    else:
        pool, out = refs
        tall = value.shape[0]
        out[:tall] = value
        out[tall:] = jnp.concatenate([pool[...], jnp.zeros_like(pool[...])], axis=0).astype(BF)


def last_add(mine, got, pool=None, after=()):
    dims = mine.shape[1:]
    if pool is not None:
        dims = (dims[0] + 2 * pool.shape[0],) + dims[1:]
    args = (mine, got) + (() if pool is None else (pool,))
    return call("last_add", last_add_kernel, args, (shape(dims),), after=after)


def front_kernel(place, tokens, *refs):
    outs, sems = refs[:-1], refs[-1]
    own = 2 * place[-1] + place[0]
    copies = []
    for k, out in enumerate(outs):
        copies.append(pltpu.make_async_copy(tokens.at[pl.ds(own ^ k, 1)], out, sems.at[k]))
        copies[-1].start()
    for copy in copies:
        copy.wait()


def front(dp, tokens, after=()):
    one = shape((1,) + tokens.shape[1:])
    return call(
        "front", front_kernel, (tokens,), (one, one, one, one),
        dp=dp, after=after, far=(0,), scratch=[pltpu.SemaphoreType.DMA((4,))],
    )


def prep_kernel(place, *refs):
    far, (ids_o, lens_o, pg_o, par_o), near, sems = refs[:12], refs[12:16], refs[16:-1], refs[-1]
    copies = [pltpu.make_async_copy(p, q, sems.at[i]) for i, (p, q) in enumerate(zip(far, near))]
    for copy in copies:
        copy.start()
    for copy in copies:
        copy.wait()
    seg, text_len, pg, *biases = near
    own = 2 * place[-1] + place[0]
    block = ids_o.shape[1] // 4

    def chosen(index, items):
        value = items[0]
        for i in range(1, 4):
            value = jnp.where(index == i, items[i], value)
        return value

    row = chosen(own, [seg[i : i + 1] for i in range(4)])
    parts = [row[:, i * block : (i + 1) * block] for i in range(4)]
    for k in range(4):
        ids_o[:, k * block : (k + 1) * block] = chosen(own ^ k, parts)
    row = chosen(own, [text_len[i : i + 1] for i in range(4)]).astype(F32)
    at = lax.broadcasted_iota(jnp.int32, (8, SEGS), 0)
    column = jnp.where(at == lax.broadcasted_iota(jnp.int32, (8, SEGS), 1), row, 0.0)
    column = jnp.sum(column, axis=1, keepdims=True)
    lens_o[...] = jnp.where(lax.broadcasted_iota(jnp.int32, (8, 1), 0) < SEGS, column, 1.0)
    pg_o[:SEGS] = pg[own].astype(F32)
    pg_o[SEGS:] = jnp.zeros_like(pg_o[SEGS:])
    width = par_o.shape[1]
    for i, bias in enumerate(biases):
        for k in range(bias.shape[0] // width):
            par_o[i + k] = bias[k * width : (k + 1) * width].astype(F32)
    par_o[12:] = jnp.zeros_like(par_o[12:])


def prep(dp, seg, text_len, pg, biases, after):
    width = pg.shape[2]
    return call(
        "prep", prep_kernel, (seg, text_len, pg, *biases),
        (shape((1, seg.shape[1]), jnp.int32), shape((8, 1), F32), shape((8, width), F32), shape((16, width), F32)),
        dp=dp, after=after, far=tuple(range(12)),
        scratch=[pltpu.VMEM(v.shape, v.dtype) for v in (seg, text_len, pg, *biases)]
        + [pltpu.SemaphoreType.DMA((12,))],
    )


def load_kernel(*refs):
    sems, n = refs[-1], len(refs) // 2
    copies = [pltpu.make_async_copy(p, q, sems.at[i]) for i, (p, q) in enumerate(zip(refs[:n], refs[n:-1]))]
    for copy in copies:
        copy.start()
    for copy in copies:
        copy.wait()


def load(arrays, after):
    n = len(arrays)
    return call(
        "load", load_kernel, arrays, [shape(v.shape, v.dtype) for v in arrays],
        after=after, far=tuple(range(n)), scratch=[pltpu.SemaphoreType.DMA((n,))],
    )


def pack_kernel(at, one, two, out):
    out[0] = one[...] if at is None else one[at]
    out[1] = two[...] if at is None else two[at]


def pack(one, two, at=None, after=()):
    dims = one.shape if at is None else one.shape[1:]
    return call("pack", partial(pack_kernel, at), (one, two), (shape((2,) + dims),), after=after)


def rows_out_kernel(place, near, near_x, back, out):
    core, across = place[0], place[-1]
    out[2 * across + core] = near[0].astype(F32)
    out[2 * (1 - across) + core] = near_x[0].astype(F32)
    out[2 * across + 1 - core] = back[0].astype(F32)
    out[2 * (1 - across) + 1 - core] = back[1].astype(F32)


def finish_kernel(place, parts, own, got_x, got_c, *refs):
    outs, all_four = refs[:-1], refs[-1]
    core, across = place[0], place[-1]
    all_four[2 * core + across] = own[...]
    all_four[2 * core + 1 - across] = got_x[...]
    all_four[2 * (1 - core) + across] = got_c[0]
    all_four[2 * (1 - core) + 1 - across] = got_c[1]
    parts(all_four, *outs)


def finish_down_parts(four, down_o):
    down_o[...] = four[...].astype(F32)


def finish_up_parts(four, up_o):
    width = four.shape[2]
    for q in range(4):
        up_o[:, q * width : (q + 1) * width] = four[q].astype(F32)


def finish_attn_parts(four, q_o, k_o, v_o, o_o, vec_o, pool_o):
    part = q_o.shape[0]
    for q, out in enumerate((q_o, k_o, v_o, o_o)):
        out[...] = four[q, :part].astype(F32)
        pool_o[2 * (q % 2) + q // 2] = four[q, part + PAD : part + PAD + SEGS].astype(F32)
    vec_o[...] = four[0, part : part + PAD, :part].astype(F32) + four[2, part : part + PAD, :part].astype(F32)


def pick(array, index):
    return lax.dynamic_index_in_dim(array, index, 0, keepdims=False)


class Links:
    def __init__(self, dp):
        self.dp = dp
        self.bits = dp.bit_length() - 1
        dp_steps = [(0, 1 << i) for i in range(self.bits)]
        self.axes = [(2, 0)] + dp_steps

    def swap(self, array, first, second):
        perm = []
        for d in range(self.dp):
            for s in range(4):
                ds, dd = second if s % 2 else first
                perm.append((d * 4 + s, (d ^ dd) * 4 + (s ^ ds)))
        return lax.ppermute(array, AXES, perm)

    def flip_core(self, array):
        return self.swap(array, (1, 0), (1, 0))

    def flip_both(self, array):
        return self.swap(array, (3, 0), (3, 0))

    def flip_x(self, array):
        return self.swap(array, (2, 0), (2, 0))

    def send(self, order, at, array):
        return self.swap(array, *(self.axes[o[at]] for o in order))


def local(
    dp,
    tokens,
    seg_ids,
    text_len,
    out_grad,
    pooled_grad,
    w_query,
    b_query,
    w_key,
    w_value,
    b_value,
    w_out,
    b_out,
    attn_gain,
    attn_shift,
    w_up,
    b_up,
    w_down,
    b_down,
    ffn_gain,
    ffn_shift,
):
    rows_dev, local_len, width = tokens.shape
    links = Links(dp)
    wide = w_up.shape[1]
    part = width // dp

    t_own, *sent, mark = front(dp, tokens)
    x = (t_own, links.flip_x(sent[1]), links.flip_core(sent[0]), links.flip_both(sent[2]))
    biases = (b_query, b_value, b_out, attn_gain, attn_shift, b_down, ffn_gain, ffn_shift, b_up)
    ids, lens, pg, par, mark = prep(dp, seg_ids, text_len, pooled_grad, biases, (mark,))
    w_query, w_key, w_value, w_out, w_up, w_down, mark = load(
        (w_query, w_key, w_value, w_out, w_up, w_down), (mark,)
    )
    o_own, *o_sent, mark = front(dp, out_grad, (mark,))
    *o_sent, _ = lax.optimization_barrier((*o_sent, x[1]))
    og = (o_own, links.flip_x(o_sent[1]), links.flip_core(o_sent[0]), links.flip_both(o_sent[2]))
    a, qkv, probs, inv, mark = attn_fwd(dp, x, ids, par, w_query, w_key, w_value)
    a2 = links.flip_core(a)
    keep1, send1, dg, aug, na, sa, ghf, l_near, l_far, pool, cols_f, mark = ffn(
        dp, a, par, w_out, w_up, w_down, og, ids, pg, lens
    )
    got1 = links.flip_core(send1)
    l_x = links.flip_x(l_far)
    gu, send2, mark = grad_up(dp, keep1, w_down, dg, aug, (mark,))
    got2 = links.flip_core(send2)
    o_down, o_up, o_attn = orders_of(dp)
    groups = {}

    def begin(name, order, kept, sent):
        groups[name] = [order, 0, kept, links.send(order, 0, sent)]

    def advance(name, mark):
        order, at, kept, got = groups[name]
        kept, sent, mark = add_split(dp, order, at + 2, (kept,), (got,), (mark,))
        groups[name] = [order, at + 1, kept, links.send(order, at + 1, sent)]
        return mark

    def last(name, mark, extra=None):
        order, at, kept, got = groups[name]
        value, mark = last_add(kept, got, extra, after=(mark,))
        groups[name] = [value, links.flip_x(value)]
        return mark

    def spread(name, mark):
        own, across = groups[name]
        pair, mark = pack(own, across, after=(mark,))
        groups[name] = [own, across, links.flip_core(pair)]
        return mark

    def finish(name, parts, outs, mark):
        return call(
            "finish_" + name,
            lambda place, *refs: finish_kernel(place, parts, *refs),
            groups[name],
            outs,
            dp=dp,
            final=True,
            after=(mark,),
            scratch=[pltpu.VMEM((4,) + groups[name][0].shape, BF)],
        )

    dk, ds, row_d, mark = grad_down(dp, o_down, keep1, got1, width, (mark,))
    begin("down", o_down, dk, ds)
    uk, us, row_u, mark = grad_w_up(dp, o_up, aug, gu, got2, width, (mark,))
    begin("up", o_up, uk, us)
    gha, gb, gm, rows4, mark = middle(dp, gu, send2, w_up, w_out, na, sa, ghf, par, cols_f, (mark,))
    d, ak, send3, send4, mark = attn_bwd(dp, qkv, probs, inv, a, gm, gb, (mark,))
    got3 = links.flip_core(send3), links.flip_core(send4)
    g_near, g_far, mark = grad_tokens_rows(gha, d, w_query, w_key, w_value, (mark,))
    g_x = links.flip_x(g_far)
    products, mark = attn_w(dp, a, a2, ak, got3, (rows4, row_d, row_u), (mark,))
    mark = advance("down", mark)
    mark = advance("up", mark)
    tk, ts, mark = dealt(dp, o_attn, products, (mark,))
    begin("attn", o_attn, tk, ts)
    if links.bits == 3:
        turns = (
            "attn",
            "rows",
            "down",
            "up",
            "grad",
            "attn",
            "down",
            "up",
            "lay",
            "attn",
            "down.",
            "layer",
            "up.",
            "attn.",
            "down:",
            "up:",
            "attn:",
            "fin",
        )
    else:
        turns = ("down", "attn", "up") * links.bits
        turns += ("down.", "attn.", "up.", "down:", "attn:", "up:", "rows", "lay", "layer", "grad", "fin")
    def rows_out(*args):
        *arrays, mark = args
        return call(
            "rows_out", rows_out_kernel, arrays, (shape(tokens.shape, F32),), dp=dp, final=True, after=(mark,)
        )

    done = {"down": 1, "attn": 0, "up": 1}
    for turn in turns:
        name = turn.strip(".:")
        if turn == "rows":
            g_pair, mark = pack(g_near, g_x, 1, (mark,))
            g_back = links.flip_core(g_pair)
        elif turn == "lay":
            l_pair, mark = pack(l_near, l_x, 1, (mark,))
            l_back = links.flip_core(l_pair)
        elif turn == "layer":
            layer_back, mark = rows_out(l_near, l_x, l_back, mark)
        elif turn == "grad":
            grad_tokens, mark = rows_out(g_near, g_x, g_back, mark)
        elif turn == "fin":
            out_down, mark = finish("down", finish_down_parts, (shape((4, part, width), F32),), mark)
        elif turn.endswith("."):
            mark = last(name, mark, pool if name == "attn" else None)
        elif turn.endswith(":"):
            mark = spread(name, mark)
        elif done[name] < links.bits:
            done[name] += 1
            mark = advance(name, mark)
    out_down = out_down.reshape(4 * part, width)
    out_up, mark = finish("up", finish_up_parts, (shape((part, wide), F32),), mark)
    square = shape((part, width), F32)
    *square, vec, pooled_all, mark = finish(
        "attn",
        finish_attn_parts,
        (square, square, square, square, shape((PAD, part), F32), shape((4, SEGS, width), F32)),
        mark,
    )
    return (
        layer_back,
        pooled_all,
        grad_tokens,
        square[0],
        vec[0],
        square[1],
        square[2],
        vec[1],
        square[3],
        vec[2],
        vec[3],
        vec[4],
        out_up,
        vec[8:12].reshape(4 * part),
        out_down,
        vec[5],
        vec[6],
        vec[7],
    )


def solution(mesh):
    rows, cols = P("dp", None), P("dp")
    blocks = P("dp", "seq", None)
    return jax.shard_map(
        partial(local, mesh.shape["dp"]),
        mesh=mesh,
        in_specs=(blocks, rows, rows, blocks, P("dp", None, None)) + (P(),) * 15,
        out_specs=(
            blocks,
            P("dp", None, None),
            blocks,
            rows,
            cols,
            rows,
            rows,
            cols,
            rows,
            cols,
            cols,
            cols,
            rows,
            cols,
            rows,
            cols,
            cols,
            cols,
        ),
        check_vma=False,
    )
```

```python
from functools import partial

import jax
import jax.numpy as jnp
from jax import lax
from jax.experimental import pallas as pl
from jax.experimental.pallas import tpu as pltpu
from jax.sharding import PartitionSpec as P

HEAD = 64
SEGS = 4
EPS = 1e-12
PAD = 16
TILE = 384
VMEM_MIB = 12
BF = jnp.bfloat16
F32 = jnp.float32
AXES = ("dp", "seq")
VM = pl.BlockSpec(memory_space=pltpu.VMEM)
ANY = pl.BlockSpec(memory_space=pl.ANY)


def dot(a, b, da, db):
    return lax.dot_general(a, b, (((da,), (db,)), ((), ())), preferred_element_type=F32)


def nn(a, b):
    return dot(a, b, 1, 0)


def tn(a, b):
    return dot(a, b, 0, 0)


def nt(a, b):
    return dot(a, b, 1, 1)


def shape(dims, kind=BF):
    return jax.ShapeDtypeStruct(dims, kind)


def orders_of(dp):
    n = dp.bit_length()
    if n == 4:
        return (
            ((1, 0, 2, 3), (2, 0, 3, 1)),
            ((2, 0, 1, 3), (0, 3, 1, 2)),
            ((2, 1, 0, 3), (1, 0, 3, 2)),
        )
    plain = (tuple(range(n)), tuple(range(1, n)) + (0,))
    return (plain, plain, plain)


def my_place(dp, order):
    seq, place = lax.axis_index("seq"), lax.axis_index("dp")
    core, x = lax.rem(seq, 2), lax.div(seq, 2)
    bits = [x] + [lax.rem(lax.div(place, 1 << i), 2) for i in range(dp.bit_length() - 1)]
    steps = [jnp.where(core == 0, bits[p], bits[q]) for p, q in zip(*order)] if order else []
    return [core] + steps + [x]


def call(name, kernel, args, outs, dp=None, order=None, after=(), far=(), scratch=(), final=False, vmem=VMEM_MIB):
    n = len(args)
    if not final:
        outs = [pltpu.VMEM(o.shape, o.dtype) if pinned(o) else o for o in outs]
    outs = list(outs)
    args = [
        pltpu.with_memory_space_constraint(a, pltpu.HBM if i in far else pltpu.VMEM)
        if i in far or pinned(a)
        else a
        for i, a in enumerate(args)
    ]
    after = [pltpu.with_memory_space_constraint(a, pltpu.VMEM) if pinned(a) else a for a in after]

    def body(*refs):
        own = refs[:n] + refs[n + len(after) :]
        mark = own[n + len(outs)]
        mark[...] = jnp.zeros(mark.shape, mark.dtype)
        first = [my_place(dp, order)] if dp else []
        kernel(*first, *own[: n + len(outs)], *own[n + len(outs) + 1 :])

    return pl.pallas_call(
        body,
        out_shape=outs + [shape((8, 128), F32)],
        in_specs=[ANY if i in far else VM for i in range(n)] + [VM] * len(after),
        out_specs=[VM] * (len(outs) + 1),
        scratch_shapes=list(scratch),
        name=name,
        compiler_params=pltpu.CompilerParams(vmem_limit_bytes=vmem * 2**20),
    )(*args, *after)


def pinned(array):
    return array.size * array.dtype.itemsize > 2**18


def attn_fwd_kernel(
    place, x, x_x, x_c, x_d, ids, par, wq, wk, wv, a_o, qkv_o, e_o, inv_o
):
    width, rows = a_o.shape[1] - PAD, a_o.shape[2]
    heads = width // HEAD
    cols = par[...].T
    text = lax.broadcasted_iota(jnp.int32, (PAD, rows), 0)
    same = jnp.where(ids[...] == text, 1.0, 0.0)
    ones = jnp.ones((PAD, rows), BF)
    for i, pad in enumerate((((1.0 - same) * -1e30).astype(BF), same.astype(BF), ones)):
        for h in range(heads):
            qkv_o[i, h, HEAD:] = pad
    a_o[0, width:] = ones
    a_o[1, width:] = ones
    block = rows // 4
    for i, value in enumerate((x[0], x_c[0], x_x[0], x_d[0])):
        a_o[0, :width, i * block : (i + 1) * block] = value.T
    xt = a_o[0, :width]
    for i, w in enumerate((wq, wk, wv)):
        out = tn(w[...], xt)
        if i == 0:
            out = (out + cols[:, 0:1]).astype(BF) * BF(0.125)
        elif i == 2:
            out = out + cols[:, 1:2]
        qkv_o[i, :, :HEAD] = out.astype(BF).reshape(heads, HEAD, rows)
    for h in range(heads):
        s = tn(qkv_o[1, h], qkv_o[0, h])
        e = jnp.exp(s - jnp.max(s, axis=0, keepdims=True)).astype(BF)
        e_o[h] = e
        out = nn(qkv_o[2, h], e)
        inv = 1.0 / out[HEAD : HEAD + 1]
        inv_o[h : h + 1] = inv
        a_o[1, h * HEAD : (h + 1) * HEAD] = (out[:HEAD] * inv).astype(BF)


def attn_fwd(dp, x, ids, par, wq, wk, wv):
    width = wq.shape[0]
    rows = ids.shape[1]
    heads = width // HEAD
    return call(
        "attn_fwd",
        attn_fwd_kernel,
        (*x, ids, par, wq, wk, wv),
        (
            shape((2, width + PAD, rows)),
            shape((3, heads, HEAD + PAD, rows)),
            shape((heads, rows, rows)),
            shape((heads, rows), F32),
        ),
        dp=dp,
    )


def norm_cols(h):
    centre = h - jnp.mean(h, axis=0, keepdims=True)
    scale = lax.rsqrt(jnp.mean(centre * centre, axis=0, keepdims=True) + EPS)
    return centre * scale, scale


def norm_cols_back(grad, normed, scale):
    return scale * (
        grad
        - jnp.mean(grad, axis=0, keepdims=True)
        - normed * jnp.mean(grad * normed, axis=0, keepdims=True)
    )


def gelu_both(u):
    phi = 0.5 * lax.erf(u * 0.7071067811865476) + 0.5
    return u * phi, phi + u * (jnp.exp(u * u * -0.5) * 0.3989422804014327)


def split_two(value):
    high = value.astype(BF)
    return high, (value - high.astype(F32)).astype(BF)


def ffn_kernel(
    part, sc, a, par, w_out, w_up, w_down, og, og_x, og_c, og_d, ids, pg, lens,
    keep_o, send_o, dg_o, after_o, na_o, sa_o, ghf_o, near_o, far_o, pool_o, cols_o, acc,
):
    width, wide = w_up.shape
    rows = a.shape[2]
    first = sc[0] == 0
    cols = par[...].T
    normed_a, scale_a = norm_cols(
        a[0, :width].astype(F32) + (tn(w_out[...], a[1, :width]) + cols[:, 2:3])
    )
    na_o[...] = normed_a
    sa_o[...] = scale_a
    after = normed_a * cols[:, 3:4] + cols[:, 4:5]
    after_o[:width] = after.astype(BF)
    after_o[width:] = jnp.ones((PAD, rows), BF)
    acc[...] = after + cols[:, 5:6]
    pair = 2 * part
    tiles = wide // TILE
    for i in range(tiles):
        at = slice(i * TILE, (i + 1) * TILE)
        lane, row = divmod(i * TILE, width)
        up = tn(w_up[:, at], after_o[:width]) + cols[row : row + TILE, 8 + lane : 9 + lane]
        hid, slope = gelu_both(up)
        dg_o[at] = slope.astype(BF)
        acc[...] += tn(w_down[at], hid.astype(BF))
        hid = hid.reshape(TILE // (2 * pair), 2, pair, rows)
        zero, one = hid[:, 0].reshape(TILE // 2, rows), hid[:, 1].reshape(TILE // 2, rows)
        half = slice(width + i * TILE // 2, width + (i + 1) * TILE // 2)
        keep_o[half] = jnp.where(first, zero, one).astype(BF)
        send_o[half] = jnp.where(first, one, zero).astype(BF)
    normed_f, scale_f = norm_cols(acc[...])
    layer = normed_f * cols[:, 6:7] + cols[:, 7:8]
    high, low = split_two(layer)
    block = rows // 4
    for i in range(4):
        (near_o, far_o)[i // 2][i % 2] = high[:, i * block : (i + 1) * block].T
    text = lax.broadcasted_iota(jnp.int32, (8, rows), 0) + 1
    select = jnp.where(ids[...] == text, 1.0, 0.0).astype(BF)
    pool_o[...] = (nt(select, high) + nt(select, low)) / lens[...]
    high, low = split_two(pg[...] / lens[...])
    blocks = (og[0], og_c[0], og_x[0], og_d[0])
    grad_out = jnp.concatenate([v.T for v in blocks], axis=1).astype(F32) + (
        tn(high, select) + tn(low, select)
    )
    ghf = norm_cols_back(grad_out * cols[:, 6:7], normed_f, scale_f)
    ghf_b = ghf.astype(BF)
    keep_o[:width] = ghf_b
    send_o[:width] = ghf_b
    send_o[width + wide // 2 :] = jnp.zeros((PAD, rows), BF)
    ghf_o[...] = ghf
    cols_o[:, 0:1] = jnp.sum(grad_out * normed_f, axis=1, keepdims=True)
    cols_o[:, 1:2] = jnp.sum(grad_out, axis=1, keepdims=True)


def ffn(dp, a, par, w_out, w_up, w_down, og, ids, pg, lens):
    width, wide = w_up.shape
    part = width // dp
    rows = a.shape[2]
    tall = wide // 2 + width
    return call(
        "ffn",
        partial(ffn_kernel, part),
        (a, par, w_out, w_up, w_down, *og, ids, pg, lens),
        (
            shape((tall, rows)),
            shape((tall + PAD, rows)),
            shape((wide, rows)),
            shape((width + PAD, rows)),
            shape((width, rows), F32),
            shape((1, rows), F32),
            shape((width, rows), F32),
            shape((2, rows // 4, width)),
            shape((2, rows // 4, width)),
            shape((8, width), F32),
            shape((width, 8), F32),
        ),
        dp=dp,
        scratch=[pltpu.VMEM((width, rows), F32)],
    )


def grad_up_kernel(sc, grad, w_down, dg, after, gu_o, send_o):
    wide, width = w_down.shape
    half = wide // 2
    send_o[: width + PAD] = after[...]
    g = grad[:width]
    tiles = half // TILE
    for c in range(2):
        which = sc[0] if c else 1 - sc[0]
        for k in range(tiles):
            at = pl.ds(pl.multiple_of(which * half + k * TILE, TILE), TILE)
            value = (nn(w_down[at], g) * dg[at].astype(F32)).astype(BF)
            if c == 0:
                send_o[width + PAD + k * TILE : width + PAD + (k + 1) * TILE] = value
            else:
                gu_o[k * TILE : (k + 1) * TILE] = value


def grad_up(dp, keep, w_down, dg, aug, after):
    wide, width = w_down.shape
    rows = keep.shape[1]
    half = wide // 2
    return call(
        "grad_up",
        grad_up_kernel,
        (keep, w_down, dg, aug),
        (shape((half, rows)), shape((half + width + PAD, rows))),
        dp=dp,
        after=after,
    )


def deal(sc, order, res, keep_o, send_o):
    dp = keep_o.shape[0]
    n = dp.bit_length()
    weight = [dp] + [1 << i for i in range(n - 1)]
    for out, top in ((send_o, 1 - sc[1]), (keep_o, sc[1])):
        for low in range(dp):
            where = [
                top * weight[o[0]] + sum(((low >> (n - 1 - k)) & 1) * weight[o[k]] for k in range(1, n))
                for o in order
            ]
            out[low] = res[jnp.where(sc[0] == 0, *where)]


def deal_scratch(dp, tall, wide):
    return [pltpu.VMEM((2 * dp, tall, wide), BF)]


def down_kernel(part, order, sc, mine, other, keep_o, send_o, row_o, res):
    dp = res.shape[0] // 2
    width = dp * part
    half = 2 * width
    rows = mine.shape[1]
    grad, grad2 = mine[:width], other[:width]
    row_o[...] = nt(jnp.ones((8, rows), BF), grad)
    for k in range(half // TILE):
        at = slice(width + k * TILE, width + (k + 1) * TILE)
        value = nt(mine[at], grad) + nt(other[at], grad2)
        for i in range(TILE // part):
            j, x = divmod(k * TILE // part + i, 2)
            res[x * dp + j] = value[i * part : (i + 1) * part].astype(BF)
    deal(sc, order, res, keep_o, send_o)


def grad_down(dp, order, mine, other, width, after):
    part = width // dp
    rows = mine.shape[1]
    piece = shape((dp, part, width))
    return call(
        "grad_down",
        partial(down_kernel, part, order),
        (mine, other),
        (piece, piece, shape((8, width), F32)),
        dp=dp,
        order=order,
        after=after,
        scratch=deal_scratch(dp, part, width),
    )


def up_kernel(part, order, sc, after, gu, other, keep_o, send_o, row_o, res):
    dp = keep_o.shape[0]
    width = dp * part
    top = width + PAD
    for x in range(2):
        mine = gu[x * width : (x + 1) * width]
        theirs = other[top + x * width : top + (x + 1) * width]
        for k in range(width // TILE):
            at = slice(k * TILE, (k + 1) * TILE + (PAD if (k + 1) * TILE == width else 0))
            value = nt(after[at], mine) + nt(other[at], theirs)
            for i in range(TILE // part):
                res[x * dp + k * TILE // part + i] = value[i * part : (i + 1) * part].astype(BF)
        row_o[x] = value[TILE : TILE + 8]
    deal(sc, order, res, keep_o, send_o)


def grad_w_up(dp, order, aug, gu, other, width, after):
    part = width // dp
    piece = shape((dp, part, width))
    return call(
        "grad_w_up",
        partial(up_kernel, part, order),
        (aug, gu, other),
        (piece, piece, shape((2, 8, width), F32)),
        dp=dp,
        order=order,
        after=after,
        scratch=deal_scratch(dp, part, width),
    )


def middle_kernel(sc, gu, send, w_up, w_out, na, sa, ghf, par, cols_f, gha_o, gb_o, gm_o, rows_o):
    half = gu.shape[0]
    width = w_out.shape[0]
    core = sc[0]
    cols = par[...].T
    at = pl.ds(pl.multiple_of(core * half, half), half)
    to = pl.ds(pl.multiple_of((1 - core) * half, half), half)
    grad = nn(w_up[:, at], gu[...]) + nn(w_up[:, to], send[width + PAD :])
    grad = grad + ghf[...]
    normed = na[...]
    gha = norm_cols_back(grad * cols[:, 3:4], normed, sa[...])
    gb = gha.astype(BF)
    gb_o[...] = gb
    gha_o[...] = gha
    gm_o[...] = nn(w_out[...], gb).astype(BF)
    four = jnp.concatenate(
        [
            jnp.sum(grad * normed, axis=1, keepdims=True),
            jnp.sum(grad, axis=1, keepdims=True),
            cols_f[:, 0:2],
            jnp.zeros((width, 124), F32),
        ],
        axis=1,
    )
    rows_o[...] = four.T[:8]


def middle(dp, gu, send, w_up, w_out, na, sa, ghf, par, cols_f, after):
    width, rows = na.shape
    return call(
        "middle",
        middle_kernel,
        (gu, send, w_up, w_out, na, sa, ghf, par, cols_f),
        (shape((width, rows), F32), shape((width, rows)), shape((width, rows)), shape((8, width), F32)),
        dp=dp,
        after=after,
    )


def attn_bwd_kernel(sc, gm, gb, inv, a, qkv, e, d_o, keep_o, send_o, send2_o, g_all):
    first = sc[0] == 0
    heads = e.shape[0]
    rows = gm.shape[1]
    zero = jnp.zeros((PAD - 3, rows), BF)
    for h in range(heads):
        at = slice(h * HEAD, (h + 1) * HEAD)
        grad = (gm[at].astype(F32) * inv[h : h + 1]).astype(BF)
        inner = -jnp.sum(a[1, at].astype(F32) * grad.astype(F32), axis=0, keepdims=True)
        high, low = split_two(inner)
        mid, low = split_two(inner - high.astype(F32))
        g_all[h, :HEAD] = grad
        g_all[h, HEAD:] = jnp.concatenate([high, mid, low, zero], axis=0)
        probs = e[h]
        diff = tn(qkv[2, h], g_all[h])
        gs = (probs.astype(F32) * diff).astype(BF)
        gq = (nn(qkv[1, h, :HEAD], gs) * 0.125).astype(BF)
        gk = nt(qkv[0, h, :HEAD], gs).astype(BF)
        gv = nt(g_all[h, :HEAD], probs).astype(BF)
        d_o[0, at] = gq
        d_o[1, at] = gk
        d_o[2, at] = gv
        last = gb[at]
        keep_o[0, at] = jnp.where(first, gq, gv)
        keep_o[1, at] = jnp.where(first, gk, last)
        send_o[at] = jnp.where(first, gv, gq)
        send2_o[at] = jnp.where(first, last, gk)


def attn_bwd(dp, qkv, e, inv, a, gm, gb, after):
    heads, rows = inv.shape
    width = gm.shape[0]
    return call(
        "attn_bwd",
        attn_bwd_kernel,
        (gm, gb, inv, a, qkv, e),
        (shape((3, width, rows)), shape((2, width, rows)), shape((width, rows)), shape((width, rows))),
        dp=dp,
        after=after,
        scratch=[pltpu.VMEM((heads, HEAD + PAD, rows), BF)],
    )


def attn_w_kernel(part, sc, mine, other, other2, a, a2, rows, row_d, row_u, res):
    core = sc[0]
    dp = res.shape[0] // 2
    width = dp * part
    sums = []
    for m in range(2):
        pick_a = 0 if m == 0 else core
        left, right = mine[m], (other, other2)[m][...]
        for k in range(width // TILE):
            at = slice(k * TILE, (k + 1) * TILE + (PAD if (k + 1) * TILE == width else 0))
            value = nt(a[pick_a, at], left) + nt(a2[pick_a, at], right)
            for i in range(TILE // part):
                res[m * dp + k * TILE // part + i, :part] = value[i * part : (i + 1) * part].astype(BF)
        sums.append(value[TILE : TILE + 1])
    m0, m1 = sums
    zero = jnp.zeros_like(m0)
    first = core == 0
    vectors = jnp.concatenate(
        [
            jnp.where(first, m0, zero),
            jnp.where(first, zero, m0),
            jnp.where(first, zero, m1),
            rows[0:2],
            row_d[0:1],
            rows[2:4],
        ],
        axis=0,
    )
    for j in range(dp):
        ups = []
        for v in range(4):
            x, lane = divmod((j % (dp // 2)) * 4 * part + v * part, width)
            ups.append(row_u[x, 0:1, lane : lane + part])
        ups = jnp.concatenate(ups + [jnp.zeros((4, part), F32)], axis=0)
        ups = jnp.where(core == j // (dp // 2), ups, jnp.zeros_like(ups))
        block = jnp.concatenate([vectors[:, j * part : (j + 1) * part], ups], axis=0)
        block = jnp.concatenate([block, jnp.zeros((PAD, width - part), F32)], axis=1)
        res[j, part:] = block.astype(BF)
        res[dp + j, part:] = jnp.zeros((PAD, width), BF)


def attn_w(dp, a, a2, mine, other, vectors, after):
    width = mine.shape[1]
    part = width // dp
    rows = a.shape[2]
    return call(
        "attn_w",
        partial(attn_w_kernel, part),
        (mine, *other, a, a2) + tuple(vectors),
        (shape((2 * dp, part + PAD, width)),),
        dp=dp,
        after=after,
    )


def deal_kernel(order, sc, res, keep_o, send_o):
    deal(sc, order, res, keep_o, send_o)


def dealt(dp, order, res, after):
    piece = shape((dp,) + res.shape[1:])
    return call("dealt", partial(deal_kernel, order), (res,), (piece, piece), dp=dp, order=order, after=after)


def tokens_kernel(d, gha, wq, wk, wv, near_o, far_o):
    total = nn(wq[...], d[0]) + nn(wk[...], d[1]) + nn(wv[...], d[2])
    total = (total + gha[...]).astype(BF)
    block = total.shape[1] // 4
    for i in range(4):
        (near_o, far_o)[i // 2][i % 2] = total[:, i * block : (i + 1) * block].T


def grad_tokens_rows(gha, d, wq, wk, wv, after):
    width, rows = gha.shape
    return call(
        "grad_tokens",
        tokens_kernel,
        (d, gha, wq, wk, wv),
        (shape((2, rows // 4, width)), shape((2, rows // 4, width))),
        after=after,
    )


def add_kernel(at, n, sc, *refs):
    bit = sc[at]
    mine, got, (keep_o, send_o) = refs[:n], refs[n : 2 * n], refs[2 * n :]
    for out, b in ((send_o, 1 - bit), (keep_o, bit)):
        for i in range(out.shape[0]):
            for k in range(n):
                to = (i, k) if n > 1 else i
                out[to] = (mine[k][b, i].astype(F32) + got[k][b, i].astype(F32)).astype(BF)


def add_split(dp, order, at, mine, got, after=()):
    n = len(mine)
    half = mine[0].shape[0] // 2
    tail = mine[0].shape[1:]
    args = [v.reshape((2, half) + tail) for v in (*mine, *got)]
    piece = shape((half,) + ((n,) if n > 1 else ()) + tail)
    return call("add_split", partial(add_kernel, at, n), args, (piece, piece), dp=dp, order=order, after=after)


def last_add_kernel(mine, got, *refs):
    value = (mine[0].astype(F32) + got[0].astype(F32)).astype(BF)
    if len(refs) == 1:
        refs[0][...] = value
    else:
        pool, out = refs
        tall = value.shape[0]
        out[:tall] = value
        out[tall:] = jnp.concatenate([pool[...], jnp.zeros_like(pool[...])], axis=0).astype(BF)


def last_add(mine, got, pool=None, after=()):
    dims = mine.shape[1:]
    if pool is not None:
        dims = (dims[0] + 2 * pool.shape[0],) + dims[1:]
    args = (mine, got) + (() if pool is None else (pool,))
    return call("last_add", last_add_kernel, args, (shape(dims),), after=after)


def front_kernel(place, tokens, *refs):
    outs, sems = refs[:-1], refs[-1]
    own = 2 * place[-1] + place[0]
    copies = []
    for k, out in enumerate(outs):
        copies.append(pltpu.make_async_copy(tokens.at[pl.ds(own ^ k, 1)], out, sems.at[k]))
        copies[-1].start()
    for copy in copies:
        copy.wait()


def front(dp, tokens, after=()):
    one = shape((1,) + tokens.shape[1:])
    return call(
        "front", front_kernel, (tokens,), (one, one, one, one),
        dp=dp, after=after, far=(0,), scratch=[pltpu.SemaphoreType.DMA((4,))],
    )


def prep_kernel(place, *refs):
    far, (ids_o, lens_o, pg_o, par_o), near, sems = refs[:12], refs[12:16], refs[16:-1], refs[-1]
    copies = [pltpu.make_async_copy(p, q, sems.at[i]) for i, (p, q) in enumerate(zip(far, near))]
    for copy in copies:
        copy.start()
    for copy in copies:
        copy.wait()
    seg, text_len, pg, *biases = near
    own = 2 * place[-1] + place[0]
    block = ids_o.shape[1] // 4

    def chosen(index, items):
        value = items[0]
        for i in range(1, 4):
            value = jnp.where(index == i, items[i], value)
        return value

    row = chosen(own, [seg[i : i + 1] for i in range(4)])
    parts = [row[:, i * block : (i + 1) * block] for i in range(4)]
    for k in range(4):
        ids_o[:, k * block : (k + 1) * block] = chosen(own ^ k, parts)
    row = chosen(own, [text_len[i : i + 1] for i in range(4)]).astype(F32)
    at = lax.broadcasted_iota(jnp.int32, (8, SEGS), 0)
    column = jnp.where(at == lax.broadcasted_iota(jnp.int32, (8, SEGS), 1), row, 0.0)
    column = jnp.sum(column, axis=1, keepdims=True)
    lens_o[...] = jnp.where(lax.broadcasted_iota(jnp.int32, (8, 1), 0) < SEGS, column, 1.0)
    pg_o[:SEGS] = pg[own].astype(F32)
    pg_o[SEGS:] = jnp.zeros_like(pg_o[SEGS:])
    width = par_o.shape[1]
    for i, bias in enumerate(biases):
        for k in range(bias.shape[0] // width):
            par_o[i + k] = bias[k * width : (k + 1) * width].astype(F32)
    par_o[12:] = jnp.zeros_like(par_o[12:])


def prep(dp, seg, text_len, pg, biases, after):
    width = pg.shape[2]
    return call(
        "prep", prep_kernel, (seg, text_len, pg, *biases),
        (shape((1, seg.shape[1]), jnp.int32), shape((8, 1), F32), shape((8, width), F32), shape((16, width), F32)),
        dp=dp, after=after, far=tuple(range(12)),
        scratch=[pltpu.VMEM(v.shape, v.dtype) for v in (seg, text_len, pg, *biases)]
        + [pltpu.SemaphoreType.DMA((12,))],
    )


def load_kernel(*refs):
    sems, n = refs[-1], len(refs) // 2
    copies = [pltpu.make_async_copy(p, q, sems.at[i]) for i, (p, q) in enumerate(zip(refs[:n], refs[n:-1]))]
    for copy in copies:
        copy.start()
    for copy in copies:
        copy.wait()


def load(arrays, after):
    n = len(arrays)
    return call(
        "load", load_kernel, arrays, [shape(v.shape, v.dtype) for v in arrays],
        after=after, far=tuple(range(n)), scratch=[pltpu.SemaphoreType.DMA((n,))],
    )


def pack_kernel(at, one, two, out):
    out[0] = one[...] if at is None else one[at]
    out[1] = two[...] if at is None else two[at]


def pack(one, two, at=None, after=()):
    dims = one.shape if at is None else one.shape[1:]
    return call("pack", partial(pack_kernel, at), (one, two), (shape((2,) + dims),), after=after)


def rows_out_kernel(place, near, near_x, back, out):
    core, across = place[0], place[-1]
    out[2 * across + core] = near[0].astype(F32)
    out[2 * (1 - across) + core] = near_x[0].astype(F32)
    out[2 * across + 1 - core] = back[0].astype(F32)
    out[2 * (1 - across) + 1 - core] = back[1].astype(F32)


def finish_kernel(place, parts, own, got_x, got_c, *refs):
    outs, all_four = refs[:-1], refs[-1]
    core, across = place[0], place[-1]
    all_four[2 * core + across] = own[...]
    all_four[2 * core + 1 - across] = got_x[...]
    all_four[2 * (1 - core) + across] = got_c[0]
    all_four[2 * (1 - core) + 1 - across] = got_c[1]
    parts(all_four, *outs)


def finish_down_parts(four, down_o):
    down_o[...] = four[...].astype(F32)


def finish_up_parts(four, up_o):
    width = four.shape[2]
    for q in range(4):
        up_o[:, q * width : (q + 1) * width] = four[q].astype(F32)


def finish_attn_parts(four, q_o, k_o, v_o, o_o, vec_o, pool_o):
    part = q_o.shape[0]
    for q, out in enumerate((q_o, k_o, v_o, o_o)):
        out[...] = four[q, :part].astype(F32)
        pool_o[2 * (q % 2) + q // 2] = four[q, part + PAD : part + PAD + SEGS].astype(F32)
    vec_o[...] = four[0, part : part + PAD, :part].astype(F32) + four[2, part : part + PAD, :part].astype(F32)


def pick(array, index):
    return lax.dynamic_index_in_dim(array, index, 0, keepdims=False)


class Links:
    def __init__(self, dp):
        self.dp = dp
        self.bits = dp.bit_length() - 1
        dp_steps = [(0, 1 << i) for i in range(self.bits)]
        self.axes = [(2, 0)] + dp_steps

    def swap(self, array, first, second):
        perm = []
        for d in range(self.dp):
            for s in range(4):
                ds, dd = second if s % 2 else first
                perm.append((d * 4 + s, (d ^ dd) * 4 + (s ^ ds)))
        return lax.ppermute(array, AXES, perm)

    def flip_core(self, array):
        return self.swap(array, (1, 0), (1, 0))

    def flip_both(self, array):
        return self.swap(array, (3, 0), (3, 0))

    def flip_x(self, array):
        return self.swap(array, (2, 0), (2, 0))

    def send(self, order, at, array):
        return self.swap(array, *(self.axes[o[at]] for o in order))


def local(
    dp,
    tokens,
    seg_ids,
    text_len,
    out_grad,
    pooled_grad,
    w_query,
    b_query,
    w_key,
    w_value,
    b_value,
    w_out,
    b_out,
    attn_gain,
    attn_shift,
    w_up,
    b_up,
    w_down,
    b_down,
    ffn_gain,
    ffn_shift,
):
    rows_dev, local_len, width = tokens.shape
    links = Links(dp)
    wide = w_up.shape[1]
    part = width // dp

    t_own, *sent, mark = front(dp, tokens)
    x = (t_own, links.flip_x(sent[1]), links.flip_core(sent[0]), links.flip_both(sent[2]))
    biases = (b_query, b_value, b_out, attn_gain, attn_shift, b_down, ffn_gain, ffn_shift, b_up)
    ids, lens, pg, par, mark = prep(dp, seg_ids, text_len, pooled_grad, biases, (mark,))
    w_query, w_key, w_value, w_out, w_up, w_down, mark = load(
        (w_query, w_key, w_value, w_out, w_up, w_down), (mark,)
    )
    o_own, *o_sent, mark = front(dp, out_grad, (mark,))
    *o_sent, _ = lax.optimization_barrier((*o_sent, x[1]))
    og = (o_own, links.flip_x(o_sent[1]), links.flip_core(o_sent[0]), links.flip_both(o_sent[2]))
    a, qkv, probs, inv, mark = attn_fwd(dp, x, ids, par, w_query, w_key, w_value)
    a2 = links.flip_core(a)
    keep1, send1, dg, aug, na, sa, ghf, l_near, l_far, pool, cols_f, mark = ffn(
        dp, a, par, w_out, w_up, w_down, og, ids, pg, lens
    )
    got1 = links.flip_core(send1)
    l_x = links.flip_x(l_far)
    gu, send2, mark = grad_up(dp, keep1, w_down, dg, aug, (mark,))
    got2 = links.flip_core(send2)
    o_down, o_up, o_attn = orders_of(dp)
    groups = {}

    def begin(name, order, kept, sent):
        groups[name] = [order, 0, kept, links.send(order, 0, sent)]

    def advance(name, mark):
        order, at, kept, got = groups[name]
        kept, sent, mark = add_split(dp, order, at + 2, (kept,), (got,), (mark,))
        groups[name] = [order, at + 1, kept, links.send(order, at + 1, sent)]
        return mark

    def last(name, mark, extra=None):
        order, at, kept, got = groups[name]
        value, mark = last_add(kept, got, extra, after=(mark,))
        groups[name] = [value, links.flip_x(value)]
        return mark

    def spread(name, mark):
        own, across = groups[name]
        pair, mark = pack(own, across, after=(mark,))
        groups[name] = [own, across, links.flip_core(pair)]
        return mark

    def finish(name, parts, outs, mark):
        return call(
            "finish_" + name,
            lambda place, *refs: finish_kernel(place, parts, *refs),
            groups[name],
            outs,
            dp=dp,
            final=True,
            after=(mark,),
            scratch=[pltpu.VMEM((4,) + groups[name][0].shape, BF)],
        )

    dk, ds, row_d, mark = grad_down(dp, o_down, keep1, got1, width, (mark,))
    begin("down", o_down, dk, ds)
    uk, us, row_u, mark = grad_w_up(dp, o_up, aug, gu, got2, width, (mark,))
    begin("up", o_up, uk, us)
    gha, gb, gm, rows4, mark = middle(dp, gu, send2, w_up, w_out, na, sa, ghf, par, cols_f, (mark,))
    d, ak, send3, send4, mark = attn_bwd(dp, qkv, probs, inv, a, gm, gb, (mark,))
    got3 = links.flip_core(send3), links.flip_core(send4)
    g_near, g_far, mark = grad_tokens_rows(gha, d, w_query, w_key, w_value, (mark,))
    g_x = links.flip_x(g_far)
    products, mark = attn_w(dp, a, a2, ak, got3, (rows4, row_d, row_u), (mark,))
    mark = advance("down", mark)
    mark = advance("up", mark)
    tk, ts, mark = dealt(dp, o_attn, products, (mark,))
    begin("attn", o_attn, tk, ts)
    if links.bits == 3:
        turns = (
            "attn",
            "rows",
            "down",
            "up",
            "grad",
            "attn",
            "down",
            "up",
            "lay",
            "attn",
            "down.",
            "layer",
            "up.",
            "attn.",
            "down:",
            "up:",
            "attn:",
            "fin",
        )
    else:
        turns = ("down", "attn", "up") * links.bits
        turns += ("down.", "attn.", "up.", "down:", "attn:", "up:", "rows", "lay", "layer", "grad", "fin")
    def rows_out(*args):
        *arrays, mark = args
        return call(
            "rows_out", rows_out_kernel, arrays, (shape(tokens.shape, F32),), dp=dp, final=True, after=(mark,)
        )

    done = {"down": 1, "attn": 0, "up": 1}
    for turn in turns:
        name = turn.strip(".:")
        if turn == "rows":
            g_pair, mark = pack(g_near, g_x, 1, (mark,))
            g_back = links.flip_core(g_pair)
        elif turn == "lay":
            l_pair, mark = pack(l_near, l_x, 1, (mark,))
            l_back = links.flip_core(l_pair)
        elif turn == "layer":
            layer_back, mark = rows_out(l_near, l_x, l_back, mark)
        elif turn == "grad":
            grad_tokens, mark = rows_out(g_near, g_x, g_back, mark)
        elif turn == "fin":
            out_down, mark = finish("down", finish_down_parts, (shape((4, part, width), F32),), mark)
        elif turn.endswith("."):
            mark = last(name, mark, pool if name == "attn" else None)
        elif turn.endswith(":"):
            mark = spread(name, mark)
        elif done[name] < links.bits:
            done[name] += 1
            mark = advance(name, mark)
    out_down = out_down.reshape(4 * part, width)
    out_up, mark = finish("up", finish_up_parts, (shape((part, wide), F32),), mark)
    square = shape((part, width), F32)
    *square, vec, pooled_all, mark = finish(
        "attn",
        finish_attn_parts,
        (square, square, square, square, shape((PAD, part), F32), shape((4, SEGS, width), F32)),
        mark,
    )
    return (
        layer_back,
        pooled_all,
        grad_tokens,
        square[0],
        vec[0],
        square[1],
        square[2],
        vec[1],
        square[3],
        vec[2],
        vec[3],
        vec[4],
        out_up,
        vec[8:12].reshape(4 * part),
        out_down,
        vec[5],
        vec[6],
        vec[7],
    )


def solution(mesh):
    rows, cols = P("dp", None), P("dp")
    blocks = P("dp", "seq", None)
    return jax.shard_map(
        partial(local, mesh.shape["dp"]),
        mesh=mesh,
        in_specs=(blocks, rows, rows, blocks, P("dp", None, None)) + (P(),) * 15,
        out_specs=(
            blocks,
            P("dp", None, None),
            blocks,
            rows,
            cols,
            rows,
            rows,
            cols,
            rows,
            cols,
            cols,
            cols,
            rows,
            cols,
            rows,
            cols,
            cols,
            cols,
        ),
        check_vma=False,
    )
```

```python
from functools import partial

import jax
import jax.numpy as jnp
from jax import lax
from jax.experimental import pallas as pl
from jax.experimental.pallas import tpu as pltpu
from jax.sharding import PartitionSpec as P

HEAD = 64
SEGS = 4
EPS = 1e-12
PAD = 16
TILE = 384
VMEM_MIB = 10
BF = jnp.bfloat16
F32 = jnp.float32
AXES = ("dp", "seq")
VM = pl.BlockSpec(memory_space=pltpu.VMEM)
ANY = pl.BlockSpec(memory_space=pl.ANY)


def dot(a, b, da, db):
    return lax.dot_general(a, b, (((da,), (db,)), ((), ())), preferred_element_type=F32)


def nn(a, b):
    return dot(a, b, 1, 0)


def tn(a, b):
    return dot(a, b, 0, 0)


def nt(a, b):
    return dot(a, b, 1, 1)


def shape(dims, kind=BF):
    return jax.ShapeDtypeStruct(dims, kind)


def orders_of(dp):
    n = dp.bit_length()
    if n == 4:
        return (
            ((1, 0, 2, 3), (2, 0, 3, 1)),
            ((2, 0, 1, 3), (0, 3, 1, 2)),
            ((2, 1, 0, 3), (1, 0, 3, 2)),
        )
    plain = (tuple(range(n)), tuple(range(1, n)) + (0,))
    return (plain, plain, plain)


def my_place(dp, order):
    seq, place = lax.axis_index("seq"), lax.axis_index("dp")
    core, x = lax.rem(seq, 2), lax.div(seq, 2)
    bits = [x] + [lax.rem(lax.div(place, 1 << i), 2) for i in range(dp.bit_length() - 1)]
    steps = [jnp.where(core == 0, bits[p], bits[q]) for p, q in zip(*order)] if order else []
    return [core] + steps + [x]


def call(name, kernel, args, outs, dp=None, order=None, after=(), far=(), scratch=(), final=False, vmem=VMEM_MIB):
    n = len(args)
    if not final:
        outs = [pltpu.VMEM(o.shape, o.dtype) if pinned(o) else o for o in outs]
    outs = list(outs)
    args = [
        pltpu.with_memory_space_constraint(a, pltpu.HBM if i in far else pltpu.VMEM)
        if i in far or pinned(a)
        else a
        for i, a in enumerate(args)
    ]
    after = [pltpu.with_memory_space_constraint(a, pltpu.VMEM) if pinned(a) else a for a in after]

    def body(*refs):
        own = refs[:n] + refs[n + len(after) :]
        mark = own[n + len(outs)]
        mark[...] = jnp.zeros(mark.shape, mark.dtype)
        first = [my_place(dp, order)] if dp else []
        kernel(*first, *own[: n + len(outs)], *own[n + len(outs) + 1 :])

    return pl.pallas_call(
        body,
        out_shape=outs + [shape((8, 128), F32)],
        in_specs=[ANY if i in far else VM for i in range(n)] + [VM] * len(after),
        out_specs=[VM] * (len(outs) + 1),
        scratch_shapes=list(scratch),
        name=name,
        compiler_params=pltpu.CompilerParams(vmem_limit_bytes=vmem * 2**20),
    )(*args, *after)


def pinned(array):
    return array.size * array.dtype.itemsize > 2**18


def attn_fwd_kernel(
    place, x, x_x, x_c, x_d, ids, par, wq, wk, wv, a_o, qkv_o, e_o, inv_o
):
    width, rows = a_o.shape[1] - PAD, a_o.shape[2]
    heads = width // HEAD
    cols = par[...].T
    text = lax.broadcasted_iota(jnp.int32, (PAD, rows), 0)
    same = jnp.where(ids[...] == text, 1.0, 0.0)
    ones = jnp.ones((PAD, rows), BF)
    for i, pad in enumerate((((1.0 - same) * -1e30).astype(BF), same.astype(BF), ones)):
        for h in range(heads):
            qkv_o[i, h, HEAD:] = pad
    a_o[0, width:] = ones
    a_o[1, width:] = ones
    block = rows // 4
    for i, value in enumerate((x[0], x_c[0], x_x[0], x_d[0])):
        a_o[0, :width, i * block : (i + 1) * block] = value.T
    xt = a_o[0, :width]
    for i, w in enumerate((wq, wk, wv)):
        out = tn(w[...], xt)
        if i == 0:
            out = (out + cols[:, 0:1]).astype(BF) * BF(0.125)
        elif i == 2:
            out = out + cols[:, 1:2]
        qkv_o[i, :, :HEAD] = out.astype(BF).reshape(heads, HEAD, rows)
    for h in range(heads):
        s = tn(qkv_o[1, h], qkv_o[0, h])
        e = jnp.exp(s - jnp.max(s, axis=0, keepdims=True)).astype(BF)
        e_o[h] = e
        out = nn(qkv_o[2, h], e)
        inv = 1.0 / out[HEAD : HEAD + 1]
        inv_o[h : h + 1] = inv
        a_o[1, h * HEAD : (h + 1) * HEAD] = (out[:HEAD] * inv).astype(BF)


def attn_fwd(dp, x, ids, par, wq, wk, wv):
    width = wq.shape[0]
    rows = ids.shape[1]
    heads = width // HEAD
    return call(
        "attn_fwd",
        attn_fwd_kernel,
        (*x, ids, par, wq, wk, wv),
        (
            shape((2, width + PAD, rows)),
            shape((3, heads, HEAD + PAD, rows)),
            shape((heads, rows, rows)),
            shape((heads, rows), F32),
        ),
        dp=dp,
    )


def norm_cols(h):
    centre = h - jnp.mean(h, axis=0, keepdims=True)
    scale = lax.rsqrt(jnp.mean(centre * centre, axis=0, keepdims=True) + EPS)
    return centre * scale, scale


def norm_cols_back(grad, normed, scale):
    return scale * (
        grad
        - jnp.mean(grad, axis=0, keepdims=True)
        - normed * jnp.mean(grad * normed, axis=0, keepdims=True)
    )


def gelu_both(u):
    phi = 0.5 * lax.erf(u * 0.7071067811865476) + 0.5
    return u * phi, phi + u * (jnp.exp(u * u * -0.5) * 0.3989422804014327)


def split_two(value):
    high = value.astype(BF)
    return high, (value - high.astype(F32)).astype(BF)


def ffn_kernel(
    part, sc, a, par, w_out, w_up, w_down, og, og_x, og_c, og_d, ids, pg, lens,
    keep_o, send_o, dg_o, after_o, na_o, sa_o, ghf_o, near_o, far_o, pool_o, cols_o, acc,
):
    width, wide = w_up.shape
    rows = a.shape[2]
    first = sc[0] == 0
    cols = par[...].T
    normed_a, scale_a = norm_cols(
        a[0, :width].astype(F32) + (tn(w_out[...], a[1, :width]) + cols[:, 2:3])
    )
    na_o[...] = normed_a
    sa_o[...] = scale_a
    after = normed_a * cols[:, 3:4] + cols[:, 4:5]
    after_o[:width] = after.astype(BF)
    after_o[width:] = jnp.ones((PAD, rows), BF)
    acc[...] = after + cols[:, 5:6]
    pair = 2 * part
    tiles = wide // TILE
    for i in range(tiles):
        at = slice(i * TILE, (i + 1) * TILE)
        lane, row = divmod(i * TILE, width)
        up = tn(w_up[:, at], after_o[:width]) + cols[row : row + TILE, 8 + lane : 9 + lane]
        hid, slope = gelu_both(up)
        dg_o[at] = slope.astype(BF)
        acc[...] += tn(w_down[at], hid.astype(BF))
        hid = hid.reshape(TILE // (2 * pair), 2, pair, rows)
        zero, one = hid[:, 0].reshape(TILE // 2, rows), hid[:, 1].reshape(TILE // 2, rows)
        half = slice(width + i * TILE // 2, width + (i + 1) * TILE // 2)
        keep_o[half] = jnp.where(first, zero, one).astype(BF)
        send_o[half] = jnp.where(first, one, zero).astype(BF)
    normed_f, scale_f = norm_cols(acc[...])
    layer = normed_f * cols[:, 6:7] + cols[:, 7:8]
    high, low = split_two(layer)
    block = rows // 4
    for i in range(4):
        (near_o, far_o)[i // 2][i % 2] = high[:, i * block : (i + 1) * block].T
    text = lax.broadcasted_iota(jnp.int32, (8, rows), 0) + 1
    select = jnp.where(ids[...] == text, 1.0, 0.0).astype(BF)
    pool_o[...] = (nt(select, high) + nt(select, low)) / lens[...]
    high, low = split_two(pg[...] / lens[...])
    blocks = (og[0], og_c[0], og_x[0], og_d[0])
    grad_out = jnp.concatenate([v.T for v in blocks], axis=1).astype(F32) + (
        tn(high, select) + tn(low, select)
    )
    ghf = norm_cols_back(grad_out * cols[:, 6:7], normed_f, scale_f)
    ghf_b = ghf.astype(BF)
    keep_o[:width] = ghf_b
    send_o[:width] = ghf_b
    send_o[width + wide // 2 :] = jnp.zeros((PAD, rows), BF)
    ghf_o[...] = ghf
    cols_o[:, 0:1] = jnp.sum(grad_out * normed_f, axis=1, keepdims=True)
    cols_o[:, 1:2] = jnp.sum(grad_out, axis=1, keepdims=True)


def ffn(dp, a, par, w_out, w_up, w_down, og, ids, pg, lens):
    width, wide = w_up.shape
    part = width // dp
    rows = a.shape[2]
    tall = wide // 2 + width
    return call(
        "ffn",
        partial(ffn_kernel, part),
        (a, par, w_out, w_up, w_down, *og, ids, pg, lens),
        (
            shape((tall, rows)),
            shape((tall + PAD, rows)),
            shape((wide, rows)),
            shape((width + PAD, rows)),
            shape((width, rows), F32),
            shape((1, rows), F32),
            shape((width, rows), F32),
            shape((2, rows // 4, width)),
            shape((2, rows // 4, width)),
            shape((8, width), F32),
            shape((width, 8), F32),
        ),
        dp=dp,
        scratch=[pltpu.VMEM((width, rows), F32)],
    )


def grad_up_kernel(sc, grad, w_down, dg, after, gu_o, send_o):
    wide, width = w_down.shape
    half = wide // 2
    send_o[: width + PAD] = after[...]
    g = grad[:width]
    tiles = half // TILE
    for c in range(2):
        which = sc[0] if c else 1 - sc[0]
        for k in range(tiles):
            at = pl.ds(pl.multiple_of(which * half + k * TILE, TILE), TILE)
            value = (nn(w_down[at], g) * dg[at].astype(F32)).astype(BF)
            if c == 0:
                send_o[width + PAD + k * TILE : width + PAD + (k + 1) * TILE] = value
            else:
                gu_o[k * TILE : (k + 1) * TILE] = value


def grad_up(dp, keep, w_down, dg, aug, after):
    wide, width = w_down.shape
    rows = keep.shape[1]
    half = wide // 2
    return call(
        "grad_up",
        grad_up_kernel,
        (keep, w_down, dg, aug),
        (shape((half, rows)), shape((half + width + PAD, rows))),
        dp=dp,
        after=after,
    )


def deal(sc, order, res, keep_o, send_o):
    dp = keep_o.shape[0]
    n = dp.bit_length()
    weight = [dp] + [1 << i for i in range(n - 1)]
    for out, top in ((send_o, 1 - sc[1]), (keep_o, sc[1])):
        for low in range(dp):
            where = [
                top * weight[o[0]] + sum(((low >> (n - 1 - k)) & 1) * weight[o[k]] for k in range(1, n))
                for o in order
            ]
            out[low] = res[jnp.where(sc[0] == 0, *where)]


def deal_scratch(dp, tall, wide):
    return [pltpu.VMEM((2 * dp, tall, wide), BF)]


def down_kernel(part, order, sc, mine, other, keep_o, send_o, row_o, res):
    dp = res.shape[0] // 2
    width = dp * part
    half = 2 * width
    rows = mine.shape[1]
    grad, grad2 = mine[:width], other[:width]
    row_o[...] = nt(jnp.ones((8, rows), BF), grad)
    for k in range(half // TILE):
        at = slice(width + k * TILE, width + (k + 1) * TILE)
        value = nt(mine[at], grad) + nt(other[at], grad2)
        for i in range(TILE // part):
            j, x = divmod(k * TILE // part + i, 2)
            res[x * dp + j] = value[i * part : (i + 1) * part].astype(BF)
    deal(sc, order, res, keep_o, send_o)


def grad_down(dp, order, mine, other, width, after):
    part = width // dp
    rows = mine.shape[1]
    piece = shape((dp, part, width))
    return call(
        "grad_down",
        partial(down_kernel, part, order),
        (mine, other),
        (piece, piece, shape((8, width), F32)),
        dp=dp,
        order=order,
        after=after,
        scratch=deal_scratch(dp, part, width),
    )


def up_kernel(part, order, sc, after, gu, other, keep_o, send_o, row_o, res):
    dp = keep_o.shape[0]
    width = dp * part
    top = width + PAD
    for x in range(2):
        mine = gu[x * width : (x + 1) * width]
        theirs = other[top + x * width : top + (x + 1) * width]
        for k in range(width // TILE):
            at = slice(k * TILE, (k + 1) * TILE + (PAD if (k + 1) * TILE == width else 0))
            value = nt(after[at], mine) + nt(other[at], theirs)
            for i in range(TILE // part):
                res[x * dp + k * TILE // part + i] = value[i * part : (i + 1) * part].astype(BF)
        row_o[x] = value[TILE : TILE + 8]
    deal(sc, order, res, keep_o, send_o)


def grad_w_up(dp, order, aug, gu, other, width, after):
    part = width // dp
    piece = shape((dp, part, width))
    return call(
        "grad_w_up",
        partial(up_kernel, part, order),
        (aug, gu, other),
        (piece, piece, shape((2, 8, width), F32)),
        dp=dp,
        order=order,
        after=after,
        scratch=deal_scratch(dp, part, width),
    )


def middle_kernel(sc, gu, send, w_up, w_out, na, sa, ghf, par, cols_f, gha_o, gb_o, gm_o, rows_o):
    half = gu.shape[0]
    width = w_out.shape[0]
    core = sc[0]
    cols = par[...].T
    at = pl.ds(pl.multiple_of(core * half, half), half)
    to = pl.ds(pl.multiple_of((1 - core) * half, half), half)
    grad = nn(w_up[:, at], gu[...]) + nn(w_up[:, to], send[width + PAD :])
    grad = grad + ghf[...]
    normed = na[...]
    gha = norm_cols_back(grad * cols[:, 3:4], normed, sa[...])
    gb = gha.astype(BF)
    gb_o[...] = gb
    gha_o[...] = gha
    gm_o[...] = nn(w_out[...], gb).astype(BF)
    four = jnp.concatenate(
        [
            jnp.sum(grad * normed, axis=1, keepdims=True),
            jnp.sum(grad, axis=1, keepdims=True),
            cols_f[:, 0:2],
            jnp.zeros((width, 124), F32),
        ],
        axis=1,
    )
    rows_o[...] = four.T[:8]


def middle(dp, gu, send, w_up, w_out, na, sa, ghf, par, cols_f, after):
    width, rows = na.shape
    return call(
        "middle",
        middle_kernel,
        (gu, send, w_up, w_out, na, sa, ghf, par, cols_f),
        (shape((width, rows), F32), shape((width, rows)), shape((width, rows)), shape((8, width), F32)),
        dp=dp,
        after=after,
    )


def attn_bwd_kernel(sc, gm, gb, inv, a, qkv, e, d_o, keep_o, send_o, send2_o, g_all):
    first = sc[0] == 0
    heads = e.shape[0]
    rows = gm.shape[1]
    zero = jnp.zeros((PAD - 3, rows), BF)
    for h in range(heads):
        at = slice(h * HEAD, (h + 1) * HEAD)
        grad = (gm[at].astype(F32) * inv[h : h + 1]).astype(BF)
        inner = -jnp.sum(a[1, at].astype(F32) * grad.astype(F32), axis=0, keepdims=True)
        high, low = split_two(inner)
        mid, low = split_two(inner - high.astype(F32))
        g_all[h, :HEAD] = grad
        g_all[h, HEAD:] = jnp.concatenate([high, mid, low, zero], axis=0)
        probs = e[h]
        diff = tn(qkv[2, h], g_all[h])
        gs = (probs.astype(F32) * diff).astype(BF)
        gq = (nn(qkv[1, h, :HEAD], gs) * 0.125).astype(BF)
        gk = nt(qkv[0, h, :HEAD], gs).astype(BF)
        gv = nt(g_all[h, :HEAD], probs).astype(BF)
        d_o[0, at] = gq
        d_o[1, at] = gk
        d_o[2, at] = gv
        last = gb[at]
        keep_o[0, at] = jnp.where(first, gq, gv)
        keep_o[1, at] = jnp.where(first, gk, last)
        send_o[at] = jnp.where(first, gv, gq)
        send2_o[at] = jnp.where(first, last, gk)


def attn_bwd(dp, qkv, e, inv, a, gm, gb, after):
    heads, rows = inv.shape
    width = gm.shape[0]
    return call(
        "attn_bwd",
        attn_bwd_kernel,
        (gm, gb, inv, a, qkv, e),
        (shape((3, width, rows)), shape((2, width, rows)), shape((width, rows)), shape((width, rows))),
        dp=dp,
        after=after,
        scratch=[pltpu.VMEM((heads, HEAD + PAD, rows), BF)],
    )


def attn_w_kernel(part, sc, mine, other, other2, a, a2, rows, row_d, row_u, res):
    core = sc[0]
    dp = res.shape[0] // 2
    width = dp * part
    sums = []
    for m in range(2):
        pick_a = 0 if m == 0 else core
        left, right = mine[m], (other, other2)[m][...]
        for k in range(width // TILE):
            at = slice(k * TILE, (k + 1) * TILE + (PAD if (k + 1) * TILE == width else 0))
            value = nt(a[pick_a, at], left) + nt(a2[pick_a, at], right)
            for i in range(TILE // part):
                res[m * dp + k * TILE // part + i, :part] = value[i * part : (i + 1) * part].astype(BF)
        sums.append(value[TILE : TILE + 1])
    m0, m1 = sums
    zero = jnp.zeros_like(m0)
    first = core == 0
    vectors = jnp.concatenate(
        [
            jnp.where(first, m0, zero),
            jnp.where(first, zero, m0),
            jnp.where(first, zero, m1),
            rows[0:2],
            row_d[0:1],
            rows[2:4],
        ],
        axis=0,
    )
    for j in range(dp):
        ups = []
        for v in range(4):
            x, lane = divmod((j % (dp // 2)) * 4 * part + v * part, width)
            ups.append(row_u[x, 0:1, lane : lane + part])
        ups = jnp.concatenate(ups + [jnp.zeros((4, part), F32)], axis=0)
        ups = jnp.where(core == j // (dp // 2), ups, jnp.zeros_like(ups))
        block = jnp.concatenate([vectors[:, j * part : (j + 1) * part], ups], axis=0)
        block = jnp.concatenate([block, jnp.zeros((PAD, width - part), F32)], axis=1)
        res[j, part:] = block.astype(BF)
        res[dp + j, part:] = jnp.zeros((PAD, width), BF)


def attn_w(dp, a, a2, mine, other, vectors, after):
    width = mine.shape[1]
    part = width // dp
    rows = a.shape[2]
    return call(
        "attn_w",
        partial(attn_w_kernel, part),
        (mine, *other, a, a2) + tuple(vectors),
        (shape((2 * dp, part + PAD, width)),),
        dp=dp,
        after=after,
    )


def deal_kernel(order, sc, res, keep_o, send_o):
    deal(sc, order, res, keep_o, send_o)


def dealt(dp, order, res, after):
    piece = shape((dp,) + res.shape[1:])
    return call("dealt", partial(deal_kernel, order), (res,), (piece, piece), dp=dp, order=order, after=after)


def tokens_kernel(d, gha, wq, wk, wv, near_o, far_o):
    total = nn(wq[...], d[0]) + nn(wk[...], d[1]) + nn(wv[...], d[2])
    total = (total + gha[...]).astype(BF)
    block = total.shape[1] // 4
    for i in range(4):
        (near_o, far_o)[i // 2][i % 2] = total[:, i * block : (i + 1) * block].T


def grad_tokens_rows(gha, d, wq, wk, wv, after):
    width, rows = gha.shape
    return call(
        "grad_tokens",
        tokens_kernel,
        (d, gha, wq, wk, wv),
        (shape((2, rows // 4, width)), shape((2, rows // 4, width))),
        after=after,
    )


def add_kernel(at, n, sc, *refs):
    bit = sc[at]
    mine, got, (keep_o, send_o) = refs[:n], refs[n : 2 * n], refs[2 * n :]
    for out, b in ((send_o, 1 - bit), (keep_o, bit)):
        for i in range(out.shape[0]):
            for k in range(n):
                to = (i, k) if n > 1 else i
                out[to] = (mine[k][b, i].astype(F32) + got[k][b, i].astype(F32)).astype(BF)


def add_split(dp, order, at, mine, got, after=()):
    n = len(mine)
    half = mine[0].shape[0] // 2
    tail = mine[0].shape[1:]
    args = [v.reshape((2, half) + tail) for v in (*mine, *got)]
    piece = shape((half,) + ((n,) if n > 1 else ()) + tail)
    return call("add_split", partial(add_kernel, at, n), args, (piece, piece), dp=dp, order=order, after=after)


def last_add_kernel(mine, got, *refs):
    value = (mine[0].astype(F32) + got[0].astype(F32)).astype(BF)
    if len(refs) == 1:
        refs[0][...] = value
    else:
        pool, out = refs
        tall = value.shape[0]
        out[:tall] = value
        out[tall:] = jnp.concatenate([pool[...], jnp.zeros_like(pool[...])], axis=0).astype(BF)


def last_add(mine, got, pool=None, after=()):
    dims = mine.shape[1:]
    if pool is not None:
        dims = (dims[0] + 2 * pool.shape[0],) + dims[1:]
    args = (mine, got) + (() if pool is None else (pool,))
    return call("last_add", last_add_kernel, args, (shape(dims),), after=after)


def front_kernel(place, tokens, *refs):
    outs, sems = refs[:-1], refs[-1]
    own = 2 * place[-1] + place[0]
    copies = []
    for k, out in enumerate(outs):
        copies.append(pltpu.make_async_copy(tokens.at[pl.ds(own ^ k, 1)], out, sems.at[k]))
        copies[-1].start()
    for copy in copies:
        copy.wait()


def front(dp, tokens, after=()):
    one = shape((1,) + tokens.shape[1:])
    return call(
        "front", front_kernel, (tokens,), (one, one, one, one),
        dp=dp, after=after, far=(0,), scratch=[pltpu.SemaphoreType.DMA((4,))],
    )


def prep_kernel(place, *refs):
    far, (ids_o, lens_o, pg_o, par_o), near, sems = refs[:12], refs[12:16], refs[16:-1], refs[-1]
    copies = [pltpu.make_async_copy(p, q, sems.at[i]) for i, (p, q) in enumerate(zip(far, near))]
    for copy in copies:
        copy.start()
    for copy in copies:
        copy.wait()
    seg, text_len, pg, *biases = near
    own = 2 * place[-1] + place[0]
    block = ids_o.shape[1] // 4

    def chosen(index, items):
        value = items[0]
        for i in range(1, 4):
            value = jnp.where(index == i, items[i], value)
        return value

    row = chosen(own, [seg[i : i + 1] for i in range(4)])
    parts = [row[:, i * block : (i + 1) * block] for i in range(4)]
    for k in range(4):
        ids_o[:, k * block : (k + 1) * block] = chosen(own ^ k, parts)
    row = chosen(own, [text_len[i : i + 1] for i in range(4)]).astype(F32)
    at = lax.broadcasted_iota(jnp.int32, (8, SEGS), 0)
    column = jnp.where(at == lax.broadcasted_iota(jnp.int32, (8, SEGS), 1), row, 0.0)
    column = jnp.sum(column, axis=1, keepdims=True)
    lens_o[...] = jnp.where(lax.broadcasted_iota(jnp.int32, (8, 1), 0) < SEGS, column, 1.0)
    pg_o[:SEGS] = pg[own].astype(F32)
    pg_o[SEGS:] = jnp.zeros_like(pg_o[SEGS:])
    width = par_o.shape[1]
    for i, bias in enumerate(biases):
        for k in range(bias.shape[0] // width):
            par_o[i + k] = bias[k * width : (k + 1) * width].astype(F32)
    par_o[12:] = jnp.zeros_like(par_o[12:])


def prep(dp, seg, text_len, pg, biases, after):
    width = pg.shape[2]
    return call(
        "prep", prep_kernel, (seg, text_len, pg, *biases),
        (shape((1, seg.shape[1]), jnp.int32), shape((8, 1), F32), shape((8, width), F32), shape((16, width), F32)),
        dp=dp, after=after, far=tuple(range(12)),
        scratch=[pltpu.VMEM(v.shape, v.dtype) for v in (seg, text_len, pg, *biases)]
        + [pltpu.SemaphoreType.DMA((12,))],
    )


def load_kernel(*refs):
    sems, n = refs[-1], len(refs) // 2
    copies = [pltpu.make_async_copy(p, q, sems.at[i]) for i, (p, q) in enumerate(zip(refs[:n], refs[n:-1]))]
    for copy in copies:
        copy.start()
    for copy in copies:
        copy.wait()


def load(arrays, after):
    n = len(arrays)
    return call(
        "load", load_kernel, arrays, [shape(v.shape, v.dtype) for v in arrays],
        after=after, far=tuple(range(n)), scratch=[pltpu.SemaphoreType.DMA((n,))],
    )


def pack_kernel(at, one, two, out):
    out[0] = one[...] if at is None else one[at]
    out[1] = two[...] if at is None else two[at]


def pack(one, two, at=None, after=()):
    dims = one.shape if at is None else one.shape[1:]
    return call("pack", partial(pack_kernel, at), (one, two), (shape((2,) + dims),), after=after)


def rows_out_kernel(place, near, near_x, back, out):
    core, across = place[0], place[-1]
    out[2 * across + core] = near[0].astype(F32)
    out[2 * (1 - across) + core] = near_x[0].astype(F32)
    out[2 * across + 1 - core] = back[0].astype(F32)
    out[2 * (1 - across) + 1 - core] = back[1].astype(F32)


def finish_kernel(place, parts, own, got_x, got_c, *refs):
    outs, all_four = refs[:-1], refs[-1]
    core, across = place[0], place[-1]
    all_four[2 * core + across] = own[...]
    all_four[2 * core + 1 - across] = got_x[...]
    all_four[2 * (1 - core) + across] = got_c[0]
    all_four[2 * (1 - core) + 1 - across] = got_c[1]
    parts(all_four, *outs)


def finish_down_parts(four, down_o):
    down_o[...] = four[...].astype(F32)


def finish_up_parts(four, up_o):
    width = four.shape[2]
    for q in range(4):
        up_o[:, q * width : (q + 1) * width] = four[q].astype(F32)


def finish_attn_parts(four, q_o, k_o, v_o, o_o, vec_o, pool_o):
    part = q_o.shape[0]
    for q, out in enumerate((q_o, k_o, v_o, o_o)):
        out[...] = four[q, :part].astype(F32)
        pool_o[2 * (q % 2) + q // 2] = four[q, part + PAD : part + PAD + SEGS].astype(F32)
    vec_o[...] = four[0, part : part + PAD, :part].astype(F32) + four[2, part : part + PAD, :part].astype(F32)


def pick(array, index):
    return lax.dynamic_index_in_dim(array, index, 0, keepdims=False)


class Links:
    def __init__(self, dp):
        self.dp = dp
        self.bits = dp.bit_length() - 1
        dp_steps = [(0, 1 << i) for i in range(self.bits)]
        self.axes = [(2, 0)] + dp_steps

    def swap(self, array, first, second):
        perm = []
        for d in range(self.dp):
            for s in range(4):
                ds, dd = second if s % 2 else first
                perm.append((d * 4 + s, (d ^ dd) * 4 + (s ^ ds)))
        return lax.ppermute(array, AXES, perm)

    def flip_core(self, array):
        return self.swap(array, (1, 0), (1, 0))

    def flip_both(self, array):
        return self.swap(array, (3, 0), (3, 0))

    def flip_x(self, array):
        return self.swap(array, (2, 0), (2, 0))

    def send(self, order, at, array):
        return self.swap(array, *(self.axes[o[at]] for o in order))


def local(
    dp,
    tokens,
    seg_ids,
    text_len,
    out_grad,
    pooled_grad,
    w_query,
    b_query,
    w_key,
    w_value,
    b_value,
    w_out,
    b_out,
    attn_gain,
    attn_shift,
    w_up,
    b_up,
    w_down,
    b_down,
    ffn_gain,
    ffn_shift,
):
    rows_dev, local_len, width = tokens.shape
    links = Links(dp)
    wide = w_up.shape[1]
    part = width // dp

    t_own, *sent, mark = front(dp, tokens)
    x = (t_own, links.flip_x(sent[1]), links.flip_core(sent[0]), links.flip_both(sent[2]))
    biases = (b_query, b_value, b_out, attn_gain, attn_shift, b_down, ffn_gain, ffn_shift, b_up)
    ids, lens, pg, par, mark = prep(dp, seg_ids, text_len, pooled_grad, biases, (mark,))
    w_query, w_key, w_value, w_out, w_up, w_down, mark = load(
        (w_query, w_key, w_value, w_out, w_up, w_down), (mark,)
    )
    o_own, *o_sent, mark = front(dp, out_grad, (mark,))
    *o_sent, _ = lax.optimization_barrier((*o_sent, x[1]))
    og = (o_own, links.flip_x(o_sent[1]), links.flip_core(o_sent[0]), links.flip_both(o_sent[2]))
    a, qkv, probs, inv, mark = attn_fwd(dp, x, ids, par, w_query, w_key, w_value)
    a2 = links.flip_core(a)
    keep1, send1, dg, aug, na, sa, ghf, l_near, l_far, pool, cols_f, mark = ffn(
        dp, a, par, w_out, w_up, w_down, og, ids, pg, lens
    )
    got1 = links.flip_core(send1)
    l_x = links.flip_x(l_far)
    gu, send2, mark = grad_up(dp, keep1, w_down, dg, aug, (mark,))
    got2 = links.flip_core(send2)
    o_down, o_up, o_attn = orders_of(dp)
    groups = {}

    def begin(name, order, kept, sent):
        groups[name] = [order, 0, kept, links.send(order, 0, sent)]

    def advance(name, mark):
        order, at, kept, got = groups[name]
        kept, sent, mark = add_split(dp, order, at + 2, (kept,), (got,), (mark,))
        groups[name] = [order, at + 1, kept, links.send(order, at + 1, sent)]
        return mark

    def last(name, mark, extra=None):
        order, at, kept, got = groups[name]
        value, mark = last_add(kept, got, extra, after=(mark,))
        groups[name] = [value, links.flip_x(value)]
        return mark

    def spread(name, mark):
        own, across = groups[name]
        pair, mark = pack(own, across, after=(mark,))
        groups[name] = [own, across, links.flip_core(pair)]
        return mark

    def finish(name, parts, outs, mark):
        return call(
            "finish_" + name,
            lambda place, *refs: finish_kernel(place, parts, *refs),
            groups[name],
            outs,
            dp=dp,
            final=True,
            after=(mark,),
            scratch=[pltpu.VMEM((4,) + groups[name][0].shape, BF)],
        )

    dk, ds, row_d, mark = grad_down(dp, o_down, keep1, got1, width, (mark,))
    begin("down", o_down, dk, ds)
    uk, us, row_u, mark = grad_w_up(dp, o_up, aug, gu, got2, width, (mark,))
    begin("up", o_up, uk, us)
    gha, gb, gm, rows4, mark = middle(dp, gu, send2, w_up, w_out, na, sa, ghf, par, cols_f, (mark,))
    d, ak, send3, send4, mark = attn_bwd(dp, qkv, probs, inv, a, gm, gb, (mark,))
    got3 = links.flip_core(send3), links.flip_core(send4)
    g_near, g_far, mark = grad_tokens_rows(gha, d, w_query, w_key, w_value, (mark,))
    g_x = links.flip_x(g_far)
    products, mark = attn_w(dp, a, a2, ak, got3, (rows4, row_d, row_u), (mark,))
    mark = advance("down", mark)
    mark = advance("up", mark)
    tk, ts, mark = dealt(dp, o_attn, products, (mark,))
    begin("attn", o_attn, tk, ts)
    if links.bits == 3:
        turns = (
            "attn",
            "rows",
            "down",
            "up",
            "grad",
            "attn",
            "down",
            "up",
            "lay",
            "attn",
            "down.",
            "layer",
            "up.",
            "attn.",
            "down:",
            "up:",
            "attn:",
            "fin",
        )
    else:
        turns = ("down", "attn", "up") * links.bits
        turns += ("down.", "attn.", "up.", "down:", "attn:", "up:", "rows", "lay", "layer", "grad", "fin")
    def rows_out(*args):
        *arrays, mark = args
        return call(
            "rows_out", rows_out_kernel, arrays, (shape(tokens.shape, F32),), dp=dp, final=True, after=(mark,)
        )

    done = {"down": 1, "attn": 0, "up": 1}
    for turn in turns:
        name = turn.strip(".:")
        if turn == "rows":
            g_pair, mark = pack(g_near, g_x, 1, (mark,))
            g_back = links.flip_core(g_pair)
        elif turn == "lay":
            l_pair, mark = pack(l_near, l_x, 1, (mark,))
            l_back = links.flip_core(l_pair)
        elif turn == "layer":
            layer_back, mark = rows_out(l_near, l_x, l_back, mark)
        elif turn == "grad":
            grad_tokens, mark = rows_out(g_near, g_x, g_back, mark)
        elif turn == "fin":
            out_down, mark = finish("down", finish_down_parts, (shape((4, part, width), F32),), mark)
        elif turn.endswith("."):
            mark = last(name, mark, pool if name == "attn" else None)
        elif turn.endswith(":"):
            mark = spread(name, mark)
        elif done[name] < links.bits:
            done[name] += 1
            mark = advance(name, mark)
    out_down = out_down.reshape(4 * part, width)
    out_up, mark = finish("up", finish_up_parts, (shape((part, wide), F32),), mark)
    square = shape((part, width), F32)
    *square, vec, pooled_all, mark = finish(
        "attn",
        finish_attn_parts,
        (square, square, square, square, shape((PAD, part), F32), shape((4, SEGS, width), F32)),
        mark,
    )
    return (
        layer_back,
        pooled_all,
        grad_tokens,
        square[0],
        vec[0],
        square[1],
        square[2],
        vec[1],
        square[3],
        vec[2],
        vec[3],
        vec[4],
        out_up,
        vec[8:12].reshape(4 * part),
        out_down,
        vec[5],
        vec[6],
        vec[7],
    )


def solution(mesh):
    rows, cols = P("dp", None), P("dp")
    blocks = P("dp", "seq", None)
    return jax.shard_map(
        partial(local, mesh.shape["dp"]),
        mesh=mesh,
        in_specs=(blocks, rows, rows, blocks, P("dp", None, None)) + (P(),) * 15,
        out_specs=(
            blocks,
            P("dp", None, None),
            blocks,
            rows,
            cols,
            rows,
            rows,
            cols,
            rows,
            cols,
            cols,
            cols,
            rows,
            cols,
            rows,
            cols,
            cols,
            cols,
        ),
        check_vma=False,
    )
```
